32 devices in a mesh: dp: 8 (over y, x, core), mp: 4 (over z).
Axes of the slice: x: 2, y: 2, z: 4, core: 2. Of those that a mesh axis runs over, the one named last changes fastest.
Arguments:
- patches: bfloat16 [3, 12288, 441], P(None, ('dp', 'mp')), may hold values from -6 to 6
- clip_len: int32 [8, 5], P('dp'), may hold values from 768 to 1536, as said below
- box_count: int32 [8, 3], P('dp'), may hold values from 1 to 8, as said below
- box_bounds: int32 [8, 3, 8, 2], P('dp'), may hold values from 0 to 64, as said below
- box_labels: int32 [8, 3, 8, 80], P('dp'), may hold values 0 or 1
- memory: bfloat16 [2, 2, 3072, 768], P(None, None, 'dp', 'mp'), may hold values from -6 to 6
- up_weight: float32 [768, 5376], P('dp', 'mp'), may hold values from -0.21875 to 0.21875
- down_weight: float32 [768, 3840], P('dp', 'mp'), may hold values from -0.21875 to 0.21875
- embed_weight: float32 [441, 768], P(None, ('dp', 'mp')), may hold values from -0.25 to 0.25
- head_weight: float32 [80, 768], P(None, ('dp', 'mp')), may hold values from -0.21875 to 0.21875
- vector_weight: float32 [7, 768], P(None, ('dp', 'mp'))
- conv_weight: float32 [2, 6, 768], P(None, None, 'mp'), may hold values from 0.15 to 0.6
- position_bias: float32 [12, 3], P('mp'), may hold values from -3 to 3
- up_moment: float32 [768, 5376], P('dp', 'mp'), may hold values from -0.00010681152 to 0.00010681152
- down_moment: float32 [768, 3840], P('dp', 'mp'), may hold values from -0.00010681152 to 0.00010681152
- embed_moment: float32 [441, 768], P(None, ('dp', 'mp')), may hold values from -0.00010681152 to 0.00010681152
- head_moment: float32 [80, 768], P(None, ('dp', 'mp')), may hold values from -0.00010681152 to 0.00010681152
- vector_moment: float32 [7, 768], P(None, ('dp', 'mp')), may hold values from -0.0004272461 to 0.0004272461
- conv_moment: float32 [2, 6, 768], P(None, None, 'mp'), may hold values from -0.0004272461 to 0.0004272461
- position_moment: float32 [12, 3], P('mp'), may hold values from -0.0004272461 to 0.0004272461
- up_average: float32 [768, 5376], P('dp', 'mp'), may hold values from -0.21875 to 0.21875
- down_average: float32 [768, 3840], P('dp', 'mp'), may hold values from -0.21875 to 0.21875
- embed_average: float32 [441, 768], P(None, ('dp', 'mp')), may hold values from -0.25 to 0.25
- head_average: float32 [80, 768], P(None, ('dp', 'mp')), may hold values from -0.21875 to 0.21875
- vector_average: float32 [7, 768], P(None, ('dp', 'mp')), may hold values from 0.3 to 1.2
- conv_average: float32 [2, 6, 768], P(None, None, 'mp'), may hold values from 0.15 to 0.6
- position_average: float32 [12, 3], P('mp'), may hold values from -3 to 3
Outputs:
- loss_sum: float32 [], replicated
- box_total: float32 [], replicated
- grad_norm: float32 [], replicated
- new_memory: bfloat16 [2, 2, 3072, 768], P(None, None, 'dp', 'mp')
- up_new: float32 [768, 5376], P('dp', 'mp')
- down_new: float32 [768, 3840], P('dp', 'mp')
- embed_new: float32 [441, 768], P(None, ('dp', 'mp'))
- head_new: float32 [80, 768], P(None, ('dp', 'mp'))
- vector_new: float32 [7, 768], P(None, ('dp', 'mp'))
- conv_new: float32 [2, 6, 768], P(None, None, 'mp')
- position_new: float32 [12, 3], P('mp')
- up_moment_new: float32 [768, 5376], P('dp', 'mp')
- down_moment_new: float32 [768, 3840], P('dp', 'mp')
- embed_moment_new: float32 [441, 768], P(None, ('dp', 'mp'))
- head_moment_new: float32 [80, 768], P(None, ('dp', 'mp'))
- vector_moment_new: float32 [7, 768], P(None, ('dp', 'mp'))
- conv_moment_new: float32 [2, 6, 768], P(None, None, 'mp')
- position_moment_new: float32 [12, 3], P('mp')
- up_average_new: float32 [768, 5376], P('dp', 'mp')
- down_average_new: float32 [768, 3840], P('dp', 'mp')
- embed_average_new: float32 [441, 768], P(None, ('dp', 'mp'))
- head_average_new: float32 [80, 768], P(None, ('dp', 'mp'))
- vector_average_new: float32 [7, 768], P(None, ('dp', 'mp'))
- conv_average_new: float32 [2, 6, 768], P(None, None, 'mp')
- position_average_new: float32 [12, 3], P('mp')
- up_copy: bfloat16 [768, 5376], P('dp', 'mp')
- down_copy: bfloat16 [768, 3840], P('dp', 'mp')
The draws below stay inside these ranges and needn't reach their ends.
Inputs may be any that keep to these rules, and one draw needn't show every extreme that they name: `clip_len`: each entry is 1536 or 768; columns 0 and 1 are the older and the newer memory clip, column 2 + m the clip of micro-step m. `box_count`: boxes that count in each clip of each micro-step. `box_bounds`: each box is a pair start < end of positions within a frame.
All inputs are finite; a program needn't handle non-finite values. No bound on the sum of `box_labels` on one device may be relied on, other than what follows from the above.
Results may differ from the reference program's by a relative error of at most 0.0075.
Values may be sent and summed in bfloat16 or wider, within the bound.
No kernel may reach another device: no remote copies, remote signals or barrier semaphores. Data moves between devices by JAX's collectives and lax.ppermute only.
A program may use at most 256 MiB of HBM per device.

```python
import math
from functools import partial
import jax
import jax.numpy as jnp
from jax import lax

D = 768
HEADS = 12
HD = 64
FF = 3072
PATCH = 441
CLASSES = 80
CLIP = 1536
MICRO = 3
MEMS = 2
NBOX = 8
FRAME = 64
BATCH = 8
PARAMS = 7483392
N_DP = 8
N_MP = 4


def draw_clip_len(key, part):
    key = jax.random.fold_in(key, 11)
    long_flags = jax.random.randint(key, (BATCH, MEMS + MICRO), 0, 2)
    lengths = CLIP // 2 + long_flags * (CLIP // 2)
    lengths = lengths.at[0, 0].set(CLIP).at[0, 1].set(CLIP // 2)
    return lengths.astype(jnp.int32)


def draw_box_count(key, part):
    key = jax.random.fold_in(key, 12)
    row_index = jnp.arange(BATCH)[:, None]
    spread_rows = max(BATCH - 1, 1)
    base_count = (NBOX * spread_rows + 2 * NBOX * row_index) // (3 * spread_rows)
    noise_term = jax.random.randint(key, (BATCH, MICRO), -1, 2)
    counts_drawn = jnp.clip(base_count + noise_term, 1, NBOX)
    counts_drawn = counts_drawn.at[BATCH - 1, 0].set(NBOX).at[0, 0].set(1)
    return counts_drawn.astype(jnp.int32)


def draw_box_bounds(key, part):
    key = jax.random.fold_in(key, 13)
    first_key, second_key = jax.random.split(key)
    starting = jax.random.randint(first_key, (BATCH, MICRO, NBOX), 0, FRAME)
    extent = 1 + jax.random.randint(second_key, (BATCH, MICRO, NBOX), 0, FRAME) % (FRAME - starting)
    ending = starting + extent
    starting = starting.at[0, 0, 0].set(0)
    ending = ending.at[0, 0, 0].set(FRAME)
    return jnp.stack([starting, ending], axis=-1).astype(jnp.int32)


def draw_vector_weight(key, part):
    key = jax.random.fold_in(key, 14)
    first_key, second_key = jax.random.split(key)
    ramp = 0.5 + jnp.arange(D, dtype=jnp.float32) / D
    gains = ramp * jax.random.uniform(first_key, (7, D), minval=0.8, maxval=1.25)
    shifts = 0.3 * jax.random.normal(second_key, (7, D))
    row_index = jnp.arange(7)[:, None]
    return jnp.where(row_index % 2 == 1, gains, shifts).astype(jnp.float32)


def with_ends(array, rng, least, top_value):
    shape = array.shape
    spot = [jax.random.randint(jax.random.fold_in(rng, axis), (), 0, shape[axis]) for axis in range(len(shape))]
    array = array.at[tuple(spot)].set(least)
    longest = shape.index(max(shape))
    spot[longest] = (spot[longest] + 1) % shape[longest]
    return array.at[tuple(spot)].set(top_value)


def steps_of(key, shape, cuts, low, largest):
    def one(dim, parts):
        heights = jax.random.uniform(jax.random.fold_in(jax.random.fold_in(key, 6), dim), (parts,), jnp.float32, low / len(cuts), largest / len(cuts))
        return jnp.repeat(jnp.exp(heights), shape[dim] // parts).reshape((-1,) + (1,) * (len(shape) - dim - 1))

    loudness = one(*cuts[0])
    for cut in cuts[1:]:
        loudness = loudness * one(*cut)
    return loudness


def noise(rng, shape, deviation, most, shards=(), kind=jnp.bfloat16):
    array = jax.random.normal(rng, shape, jnp.float32) * deviation
    if len(shards) > 0:
        array = steps_of(rng, shape, shards, -0.22, 0.18) * array
    return jnp.clip(array, min=-most, max=most).astype(kind)


def setup_inputs(seed: int = 0) -> dict:
    key_of = jax.random.split(jax.random.key(seed), 28)
    return {
        "patches": noise(key_of[0], (MICRO, BATCH * CLIP, PATCH), 1.0, 6.0, ((1, 32),)),
        "clip_len": draw_clip_len(jax.random.fold_in(key_of[27], 71), 0),
        "box_count": draw_box_count(jax.random.fold_in(key_of[27], 71), 0),
        "box_bounds": draw_box_bounds(jax.random.fold_in(key_of[27], 71), 0),
        "box_labels": with_ends((jax.random.randint(key_of[4], (BATCH, MICRO, NBOX, CLASSES), 0, 4) < 1).astype(jnp.int32), jax.random.fold_in(key_of[4], 1), 0, 1),
        "memory": noise(key_of[5], (MEMS, 2, BATCH * CLIP // 4, D), 1.0, 6.0, ((2, 8), (3, 4))),
        "up_weight": noise(key_of[6], (D, 3 * HEADS * HD + FF), D ** -0.5, 0.21875, ((0, 8), (1, 4)), jnp.float32),
        "down_weight": noise(key_of[7], (D, HEADS * HD + FF), D ** -0.5, 0.21875, ((0, 8), (1, 4)), jnp.float32),
        "embed_weight": noise(key_of[8], (PATCH, D), PATCH ** -0.5, 0.25, ((1, 32),), jnp.float32),
        "head_weight": noise(key_of[9], (CLASSES, D), D ** -0.5, 0.21875, ((1, 32),), jnp.float32),
        "vector_weight": draw_vector_weight(jax.random.fold_in(key_of[27], 71), 0),
        "conv_weight": jnp.clip(jnp.exp(math.log(0.6) - 1.3862944 * jax.random.uniform(key_of[11], (2, 6, HEADS * HD), jnp.float32) ** steps_of(key_of[11], (2, 6, HEADS * HD), ((2, 4),), -0.2, 0.2)), 0.15, 0.6),
        "position_bias": noise(key_of[12], (HEADS, 3), 1.0, 3.0, ((0, 4),), jnp.float32),
        "up_moment": noise(key_of[13], (D, 3 * HEADS * HD + FF), (0.05 / PARAMS ** 0.5), 0.00010681152, ((0, 8), (1, 4)), jnp.float32),
        "down_moment": noise(key_of[14], (D, HEADS * HD + FF), (0.05 / PARAMS ** 0.5), 0.00010681152, ((0, 8), (1, 4)), jnp.float32),
        "embed_moment": noise(key_of[15], (PATCH, D), (0.05 / PARAMS ** 0.5), 0.00010681152, ((1, 32),), jnp.float32),
        "head_moment": noise(key_of[16], (CLASSES, D), (0.05 / PARAMS ** 0.5), 0.00010681152, ((1, 32),), jnp.float32),
        "vector_moment": noise(key_of[17], (7, D), (0.2 / PARAMS ** 0.5), 0.0004272461, ((1, 32),), jnp.float32),
        "conv_moment": noise(key_of[18], (2, 6, HEADS * HD), (0.2 / PARAMS ** 0.5), 0.0004272461, ((2, 4),), jnp.float32),
        "position_moment": noise(key_of[19], (HEADS, 3), (0.2 / PARAMS ** 0.5), 0.0004272461, ((0, 4),), jnp.float32),
        "up_average": noise(key_of[20], (D, 3 * HEADS * HD + FF), D ** -0.5, 0.21875, ((0, 8), (1, 4)), jnp.float32),
        "down_average": noise(key_of[21], (D, HEADS * HD + FF), D ** -0.5, 0.21875, ((0, 8), (1, 4)), jnp.float32),
        "embed_average": noise(key_of[22], (PATCH, D), PATCH ** -0.5, 0.25, ((1, 32),), jnp.float32),
        "head_average": noise(key_of[23], (CLASSES, D), D ** -0.5, 0.21875, ((1, 32),), jnp.float32),
        "vector_average": jnp.clip(0.3 + 0.90000004 * jax.random.uniform(key_of[24], (7, D), jnp.float32) ** steps_of(key_of[24], (7, D), ((1, 32),), -0.2, 0.2), 0.3, 1.2),
        "conv_average": jnp.clip(jnp.exp(math.log(0.6) - 1.3862944 * jax.random.uniform(key_of[25], (2, 6, HEADS * HD), jnp.float32) ** steps_of(key_of[25], (2, 6, HEADS * HD), ((2, 4),), -0.2, 0.2)), 0.15, 0.6),
        "position_average": noise(key_of[26], (HEADS, 3), 1.0, 3.0, ((0, 4),), jnp.float32),
    }


EPSILON = 1e-06
LEARNING = 300.0
VECTOR_LEARNING = 6000.0
MOMENTUM = 0.5
AVERAGING = 0.5
THRESHOLD = 0.05
PRECISE = lax.Precision.HIGHEST

@jax.custom_vjp
def low(v):
    return lax.optimization_barrier(v.astype(jnp.bfloat16)).astype(jnp.float32)

@jax.custom_vjp
def low_back(v):
    return v

def low_keep(v):
    return (low(v), None)

def low_pass(kept, grad):
    return (grad,)

def back_keep(v):
    return (v, None)

def back_low(kept, grad):
    return (low(grad),)
low.defvjp(low_keep, low_pass)
low_back.defvjp(back_keep, back_low)

def norm_rows(inputs, gain_row, shift_row):
    row_mean = lax.optimization_barrier(jnp.mean(inputs, axis=-1, keepdims=True))
    centered = inputs - row_mean
    variance = lax.optimization_barrier(jnp.mean(centered * centered, axis=-1, keepdims=True))
    return centered * lax.rsqrt(variance + EPSILON) * gain_row + shift_row

def matmul(first_operand, second_operand):
    return jnp.matmul(first_operand, second_operand, precision=PRECISE)

def pool_taps(inputs, conv_taps):
    channels = inputs.shape[-1]
    return lax.optimization_barrier(jnp.sum(inputs.reshape(-1, conv_taps.shape[0], channels) * conv_taps, axis=1))

def apply_update(weight, gradient, moment, average, rate):
    moment = MOMENTUM * moment + gradient
    updated = weight - rate * (gradient + MOMENTUM * moment)
    return (updated, moment, AVERAGING * average + (1.0 - AVERAGING) * updated)

def unpack_weights(weights):
    up_weight, down_weight, embed_weight, head_weight, vectors, conv_all, rel_bias = weights
    head_cols = HEADS * HD // N_MP
    up_parts = low(up_weight).reshape(D, N_MP, -1)
    down_parts = low(down_weight).reshape(D, N_MP, -1)
    w_query = up_parts[:, :, :head_cols].reshape(D, HEADS * HD)
    w_key = up_parts[:, :, head_cols:2 * head_cols].reshape(D, HEADS * HD)
    w_value = up_parts[:, :, 2 * head_cols:3 * head_cols].reshape(D, HEADS * HD)
    w_hidden = up_parts[:, :, 3 * head_cols:].reshape(D, FF)
    w_out = down_parts[:, :, :head_cols].reshape(D, HEADS * HD)
    w_back = down_parts[:, :, head_cols:].reshape(D, FF)
    return (low(embed_weight), vectors, low(head_weight), w_query, w_key, w_value, w_hidden, w_out, w_back, conv_all, rel_bias)

def embed_norm(unpacked, patch_rows):
    embedded = low_back(matmul(patch_rows, unpacked[0]) + unpacked[1][0])
    return (embedded, low(norm_rows(embedded, unpacked[1][1], unpacked[1][2])))

def pooled_pair(unpacked, patch_rows):
    embedded, normed = embed_norm(unpacked, patch_rows)
    conv_all = unpacked[9]
    key_rows = low(pool_taps(matmul(normed, unpacked[4]), conv_all[0, :4]))
    value_rows = low(pool_taps(matmul(normed, unpacked[5]), conv_all[1, :4]))
    return (key_rows, value_rows)

def clip_loss(unpacked, patch_rows, lengths, mem_newer, mem_older, bounds, labels_row, box_number):
    embed_low, vectors, head_low, w_query, w_key, w_value, w_hidden, w_out, w_back, conv_all, rel_bias = unpacked
    embedded, normed = embed_norm(unpacked, patch_rows)
    query_rows = low(low_back(matmul(normed, w_query)))
    key_raw = low_back(matmul(normed, w_key))
    value_raw = low_back(matmul(normed, w_value))
    key_rows = jnp.concatenate([low(pool_taps(key_raw, conv_all[0, :4])), low(pool_taps(mem_newer[0], conv_all[0, 4:])), low(pool_taps(mem_older[0], conv_all[0, 4:]))], axis=0)
    value_rows = jnp.concatenate([low(pool_taps(value_raw, conv_all[1, :4])), low(pool_taps(mem_newer[1], conv_all[1, 4:])), low(pool_taps(mem_older[1], conv_all[1, 4:]))], axis=0)
    pooled = CLIP // 4
    position = jnp.arange(2 * pooled)
    offset = (position >= pooled).astype(jnp.int32) + (position >= pooled + pooled // 2).astype(jnp.int32)
    key_limit = jnp.where(offset == 0, lengths[0] // 4, jnp.where(offset == 1, lengths[1] // 8, lengths[2] // 8))
    key_local = position - jnp.where(offset == 0, 0, jnp.where(offset == 1, pooled, pooled + pooled // 2))
    key_valid = key_local < key_limit
    scores = jnp.einsum('qhd,khd->hqk', query_rows.reshape(CLIP, HEADS, HD), key_rows.reshape(-1, HEADS, HD), precision=PRECISE) * HD ** (-0.5)
    scores = low_back(scores + rel_bias[:, offset][:, None, :])
    scores = jnp.where(key_valid[None, None, :], scores, -1e+30)
    prob_rows = low(jax.nn.softmax(scores, axis=-1))
    attended = jnp.einsum('hqk,khd->qhd', prob_rows, value_rows.reshape(-1, HEADS, HD), precision=PRECISE).reshape(CLIP, HEADS * HD)
    attended = low_back(low(attended + query_rows))
    first_res = embedded + low_back(matmul(attended, w_out.T))
    normed_mlp = low(norm_rows(first_res, vectors[3], vectors[4]))
    hidden = low_back(matmul(normed_mlp, w_hidden))
    active = low(jax.nn.gelu(hidden, approximate=False))
    second_res = first_res + low_back(matmul(active, w_back.T))
    final_rows = norm_rows(second_res, vectors[5], vectors[6])
    position_tok = jnp.arange(CLIP)
    within = position_tok % FRAME
    inside = (within[None, :] >= bounds[:, 0:1]) & (within[None, :] < bounds[:, 1:2]) & (position_tok[None, :] < lengths[0])
    denominator = ((bounds[:, 1] - bounds[:, 0]) * (lengths[0] // FRAME)).astype(jnp.float32)
    select = inside.astype(jnp.float32) / denominator[:, None]
    feature = matmul(select, final_rows)
    logits = low_back(matmul(low(feature), head_low.T))
    target = labels_row.astype(jnp.float32)
    box_keep = (jnp.arange(NBOX) < box_number).astype(jnp.float32)
    return jnp.sum((jax.nn.softplus(logits) - target * logits) * box_keep[:, None])

def reference(patches, clip_len, box_count, box_bounds, box_labels, memory, up_weight, down_weight, embed_weight, head_weight, vector_weight, conv_weight, position_bias, up_moment, down_moment, embed_moment, head_moment, vector_moment, conv_moment, position_moment, up_average, down_average, embed_average, head_average, vector_average, conv_average, position_average):
    masters = (up_weight, down_weight, embed_weight, head_weight, vector_weight, conv_weight, position_bias)
    moments = (up_moment, down_moment, embed_moment, head_moment, vector_moment, conv_moment, position_moment)
    averages = (up_average, down_average, embed_average, head_average, vector_average, conv_average, position_average)
    rates = (LEARNING, LEARNING, LEARNING, LEARNING, VECTOR_LEARNING, VECTOR_LEARNING, VECTOR_LEARNING)
    patch_all = patches.astype(jnp.float32).reshape(MICRO, N_DP, CLIP, PATCH)
    stored = jnp.transpose(memory.astype(jnp.float32).reshape(MEMS, 2, N_DP, CLIP // 4, D), (2, 0, 1, 3, 4))
    unpacked = unpack_weights(masters)
    memories = [stored[:, 0], stored[:, 1]]
    for micro_step in range(MICRO):
        key_rows, value_rows = lax.map(partial(pooled_pair, unpacked), patch_all[micro_step])
        memories.append(jnp.stack([key_rows, value_rows], axis=1))

    def total_loss(weights):
        inner_weights = unpack_weights(weights)

        def one_clip(inputs):
            return clip_loss(inner_weights, *inputs)
        loss_total = jnp.zeros((), jnp.float32)
        for micro_step in range(MICRO):
            lengths = jnp.stack([clip_len[:, 2 + micro_step], clip_len[:, 1 + micro_step], clip_len[:, micro_step]], axis=1)
            losses = lax.map(jax.checkpoint(one_clip), (patch_all[micro_step], lengths, memories[micro_step + 1], memories[micro_step], box_bounds[:, micro_step], box_labels[:, micro_step], box_count[:, micro_step]))
            loss_total = loss_total + jnp.sum(losses)
        return loss_total
    loss_sum, pullback = jax.vjp(total_loss, masters)
    raw_grads = pullback(jnp.ones((), jnp.float32))[0]
    box_total = jnp.sum(box_count).astype(jnp.float32)
    gradients = [gradient / box_total for gradient in raw_grads]
    grad_norm = jnp.sqrt(sum((jnp.sum(gradient * gradient) for gradient in gradients)))
    factor = jnp.minimum(1.0, THRESHOLD / grad_norm)
    results = [apply_update(weight, gradient * factor, moment, average, rate) for weight, gradient, moment, average, rate in zip(masters, gradients, moments, averages, rates)]
    new_memory = jnp.stack([memories[MICRO], memories[MICRO + 1]], axis=1)
    new_memory = jnp.transpose(new_memory, (1, 2, 0, 3, 4)).reshape(MEMS, 2, N_DP * (CLIP // 4), D).astype(jnp.bfloat16)
    return (loss_sum, box_total, grad_norm, new_memory, results[0][0], results[1][0], results[2][0], results[3][0], results[4][0], results[5][0], results[6][0], results[0][1], results[1][1], results[2][1], results[3][1], results[4][1], results[5][1], results[6][1], results[0][2], results[1][2], results[2][2], results[3][2], results[4][2], results[5][2], results[6][2], results[0][0].astype(jnp.bfloat16), results[1][0].astype(jnp.bfloat16))
```

```python
import functools

import jax
import jax.numpy as jnp
from jax import lax
from jax.experimental import pallas as pl
from jax.experimental.pallas import tpu as pltpu
from jax.sharding import PartitionSpec as P

MICRO = 3
FRAME = 64
EPSILON = 1e-06
LEARNING = 300.0
VECTOR_LEARNING = 6000.0
MOMENTUM = 0.5
AVERAGING = 0.5
THRESHOLD = 0.05
PRECISE = lax.Precision.HIGHEST
QUAD = 4
bf16 = jnp.bfloat16
f32 = jnp.float32


def norm_rows(inputs, gain_row, shift_row):
    row_mean = jnp.mean(inputs, axis=-1, keepdims=True)
    centered = inputs - row_mean
    variance = jnp.mean(centered * centered, axis=-1, keepdims=True)
    return centered * lax.rsqrt(variance + EPSILON) * gain_row + shift_row


def gelu_exact(inputs):
    return jax.nn.gelu(inputs, approximate=False)


def product(first_operand, second_operand):
    return jnp.dot(first_operand, second_operand, preferred_element_type=f32)


def contract_last(first_operand, second_operand):
    return lax.dot_general(
        first_operand, second_operand, (((1,), (1,)), ((), ())), preferred_element_type=f32
    )


def contract_rows(first_operand, second_operand):
    return lax.dot_general(
        first_operand, second_operand, (((0,), (0,)), ((), ())), preferred_element_type=f32
    )


def apply_update(weight, gradient, moment, average, rate):
    moment = MOMENTUM * moment + gradient
    updated = weight - rate * (gradient + MOMENTUM * moment)
    return (updated, moment, AVERAGING * average + (1.0 - AVERAGING) * updated)


def swap_dp(inputs, mask):
    size = lax.axis_size("dp")
    return lax.ppermute(inputs, "dp", [(i, i ^ mask) for i in range(size)])


def swap_mp(inputs, mask):
    size = lax.axis_size("mp")
    return lax.ppermute(inputs, "mp", [(i, i ^ mask) for i in range(size)])


def dp_bits():
    return lax.axis_size("dp").bit_length() - 1


def regroup(inputs):
    count = lax.axis_size("dp")
    pairs = []
    for d in range(count):
        for z in range(4):
            hi, x, k = d // 4, (d // 2) % 2, d % 2
            pairs.append((d * 4 + z, (hi * 4 + (z % 2) * 2 + z // 2) * 4 + 2 * k + x))
    return lax.ppermute(inputs, ("dp", "mp"), pairs)


def gather_mp(inputs):
    place = lax.axis_index("mp")
    pieces = jnp.stack([inputs] + [swap_mp(inputs, s) for s in (1, 2, 3)])
    return [lax.dynamic_index_in_dim(pieces, j ^ place, 0, keepdims=False) for j in range(4)]


def gather_dp(inputs, order):
    pieces = {0: inputs}
    rows = inputs.shape[0]
    for bit in order:
        keys = sorted(pieces)
        sent = jnp.concatenate([pieces[k] for k in keys]) if len(keys) > 1 else pieces[0]
        got = swap_dp(sent, 1 << bit)
        for i, k in enumerate(keys):
            pieces[k ^ (1 << bit)] = got[i * rows : (i + 1) * rows]
    return jnp.concatenate([pieces[k] for k in sorted(pieces)])


def scatter_dp(inputs, order):
    count = lax.axis_size("dp")
    rows = inputs.shape[0] // count
    pieces = {k: inputs[k * rows : (k + 1) * rows] for k in range(count)}
    for bit in order:
        mine = [k for k in sorted(pieces) if not (k >> bit) & 1]
        away = [k for k in sorted(pieces) if (k >> bit) & 1]
        sent = jnp.concatenate([pieces[k] for k in away]) if len(away) > 1 else pieces[away[0]]
        got = swap_dp(sent, 1 << bit)
        pieces = {
            k: (
                pieces[k].astype(f32) + got[i * rows : (i + 1) * rows].astype(f32)
            ).astype(inputs.dtype)
            for i, k in enumerate(mine)
        }
    return pieces[0]


def gather_split(inputs):
    half = inputs.shape[1] // 2
    up = list(range(1, dp_bits()))
    return jnp.concatenate(
        [
            gather_dp(inputs[:, :half], up + [0]),
            gather_dp(inputs[:, half:], up[::-1] + [0]),
        ],
        axis=1,
    )


def scatter_split(inputs):
    half = inputs.shape[1] // 2
    up = list(range(1, dp_bits()))
    return jnp.concatenate(
        [
            scatter_dp(inputs[:, :half], [0] + up),
            scatter_dp(inputs[:, half:], [0] + up[::-1]),
        ],
        axis=1,
    )


def scatter_mp(pieces):
    place = lax.axis_index("mp")
    stacked = jnp.stack(pieces)
    total = lax.dynamic_index_in_dim(stacked, place, 0, keepdims=False).astype(f32)
    for s in (1, 2, 3):
        total = total + swap_mp(
            lax.dynamic_index_in_dim(stacked, place ^ s, 0, keepdims=False), s
        ).astype(f32)
    return total


def sum_all(inputs):
    for bit in range(dp_bits()):
        inputs = inputs + swap_dp(inputs, 1 << bit)
    for mask in (1, 2):
        inputs = inputs + swap_mp(inputs, mask)
    return inputs


def group_gather(inputs):
    one = swap_dp(inputs, 1)
    two = swap_dp(inputs, 2)
    three = swap_dp(two, 1)
    return [inputs, one, two, three]


def group_scatter(parts):
    got = swap_dp(jnp.stack([parts[1], parts[3]]), 1)
    mine = parts[0].astype(f32) + got[0].astype(f32)
    far = (parts[2].astype(f32) + got[1].astype(f32)).astype(bf16)
    return mine + swap_dp(far, 2).astype(f32)


def group_sum_features(inputs):
    count = lax.axis_size("dp")
    width = inputs.shape[1] // count
    for mask in (1, 2):
        got = swap_dp(inputs, mask)
        blocks = [got[:, (b ^ mask) * width : ((b ^ mask) + 1) * width] for b in range(count)]
        inputs = inputs + jnp.concatenate(blocks, axis=1)
    return inputs


def attend_kernel(q_ref, k_ref, v_ref, bias_ref, out_ref, prob_ref):
    query = q_ref[...]
    rows, width = query.shape
    size = width // QUAD
    keys_t = k_ref[...].T
    values = v_ref[...]
    lane = lax.broadcasted_iota(jnp.int32, (rows, width), 1) // size
    scaled = query * (size**-0.5)
    total = query.astype(f32)
    for h in range(QUAD):
        own = jnp.where(lane == h, scaled, jnp.zeros_like(scaled))
        scores = jnp.dot(own, keys_t, preferred_element_type=f32) + bias_ref[0, h : h + 1, :]
        top = jnp.max(scores, axis=-1, keepdims=True)
        exponent = jnp.exp(scores - top)
        denominator = jnp.sum(exponent, axis=-1, keepdims=True)
        probs = (exponent * (1.0 / denominator)).astype(bf16)
        prob_ref[h] = probs
        mixed = jnp.dot(probs, values, preferred_element_type=f32)
        total = total + jnp.where(lane == h, mixed, 0.0)
    out_ref[...] = total.astype(bf16)


def attend(query, keys, values, bias):
    rows, width = query.shape
    count = keys.shape[0]
    heads = bias.shape[0] * QUAD
    block = width // bias.shape[0]
    return pl.pallas_call(
        attend_kernel,
        grid=(bias.shape[0],),
        in_specs=[
            pl.BlockSpec((rows, block), lambda i: (0, i)),
            pl.BlockSpec((count, block), lambda i: (0, i)),
            pl.BlockSpec((count, block), lambda i: (0, i)),
            pl.BlockSpec((1, QUAD, count), lambda i: (i, 0, 0)),
        ],
        out_specs=[
            pl.BlockSpec((rows, block), lambda i: (0, i)),
            pl.BlockSpec((QUAD, rows, count), lambda i: (i, 0, 0)),
        ],
        out_shape=[
            jax.ShapeDtypeStruct((rows, width), bf16),
            jax.ShapeDtypeStruct((heads, rows, count), bf16),
        ],
        compiler_params=pltpu.CompilerParams(vmem_limit_bytes=40 * 1024 * 1024),
        cost_estimate=pl.CostEstimate(
            flops=4 * rows * count * width * 4,
            bytes_accessed=heads * rows * count * 2,
            transcendentals=heads * rows * count,
        ),
    )(query, keys, values, bias)


def attend_back_kernel(q_ref, k_ref, v_ref, prob_ref, grad_ref, dq_ref, dk_ref, dv_ref, db_ref):
    query = q_ref[...]
    grad = grad_ref[...]
    rows, width = query.shape
    size = width // QUAD
    keys = k_ref[...]
    values_t = v_ref[...].T
    query_t = query.T
    grad_t = grad.T
    scaling = size**-0.5
    lane = lax.broadcasted_iota(jnp.int32, (rows, width), 1) // size
    total = jnp.zeros((rows, width), f32)
    ones = jnp.ones((16, rows), bf16)
    key_parts, value_parts = [], []
    for h in range(QUAD):
        own = jnp.where(lane == h, grad, jnp.zeros_like(grad))
        probs_low = prob_ref[h]
        probs = probs_low.astype(f32)
        pulled = probs * jnp.dot(own, values_t, preferred_element_type=f32)
        shift = jnp.sum(pulled, axis=-1, keepdims=True)
        score_grad = (pulled - probs * shift).astype(bf16)
        mixed = jnp.dot(score_grad, keys, preferred_element_type=f32)
        total = total + jnp.where(lane == h, mixed, 0.0)
        left = jnp.concatenate([query_t[h * size : (h + 1) * size], ones])
        found = jnp.dot(left, score_grad, preferred_element_type=f32)
        key_parts.append(found[:size])
        db_ref[0, h : h + 1, :] = found[size : size + 1]
        value_parts.append(
            jnp.dot(
                grad_t[h * size : (h + 1) * size], probs_low, preferred_element_type=f32
            )
        )
    dq_ref[...] = (total * scaling + grad.astype(f32)).astype(bf16)
    dk_ref[...] = jnp.concatenate(key_parts).T * scaling
    dv_ref[...] = jnp.concatenate(value_parts).T


def attend_back(query, keys, values, probs, grad):
    rows, width = query.shape
    count = keys.shape[0]
    heads = probs.shape[0]
    quads = heads // QUAD
    block = width // quads
    return pl.pallas_call(
        attend_back_kernel,
        grid=(quads,),
        in_specs=[
            pl.BlockSpec((rows, block), lambda i: (0, i)),
            pl.BlockSpec((count, block), lambda i: (0, i)),
            pl.BlockSpec((count, block), lambda i: (0, i)),
            pl.BlockSpec((QUAD, rows, count), lambda i: (i, 0, 0)),
            pl.BlockSpec((rows, block), lambda i: (0, i)),
        ],
        out_specs=[
            pl.BlockSpec((rows, block), lambda i: (0, i)),
            pl.BlockSpec((count, block), lambda i: (0, i)),
            pl.BlockSpec((count, block), lambda i: (0, i)),
            pl.BlockSpec((1, QUAD, count), lambda i: (i, 0, 0)),
        ],
        out_shape=[
            jax.ShapeDtypeStruct((rows, width), bf16),
            jax.ShapeDtypeStruct((count, width), f32),
            jax.ShapeDtypeStruct((count, width), f32),
            jax.ShapeDtypeStruct((quads, QUAD, count), f32),
        ],
        compiler_params=pltpu.CompilerParams(vmem_limit_bytes=40 * 1024 * 1024),
        cost_estimate=pl.CostEstimate(
            flops=8 * rows * count * width * 4,
            bytes_accessed=heads * rows * count * 2,
            transcendentals=0,
        ),
    )(query, keys, values, probs, grad)


def one_hot_rows(index, count):
    return (index[:, None] == jnp.arange(count)[None, :]).astype(bf16)


def shards(
    patches,
    clip_len,
    box_count,
    box_bounds,
    box_labels,
    memory,
    up_weight,
    down_weight,
    embed_weight,
    head_weight,
    vector_weight,
    conv_weight,
    position_bias,
    up_moment,
    down_moment,
    embed_moment,
    head_moment,
    vector_moment,
    conv_moment,
    position_moment,
    up_average,
    down_average,
    embed_average,
    head_average,
    vector_average,
    conv_average,
    position_average,
):
    dp_index = lax.axis_index("dp")
    mp_index = lax.axis_index("mp")
    dp_count = lax.axis_size("dp")
    across, core = (dp_index // 2) % 2, dp_index % 2
    quarter = 2 * core + across
    rows = patches.shape[1]
    eighth = rows // 8
    pooled = rows // 4
    head_cols = conv_weight.shape[2]
    width = 4 * head_cols
    sub = embed_weight.shape[1]
    patch = embed_weight.shape[0]
    classes = head_weight.shape[0]
    boxes = box_bounds.shape[2]
    heads = position_bias.shape[0] * 4

    ints = jnp.concatenate(
        [clip_len.reshape(-1), box_count.reshape(-1), box_bounds.reshape(-1), box_labels.reshape(-1)]
    )
    total_ints = ints.shape[0]
    ints = jnp.pad(ints, (0, -total_ints % 1024)).reshape(-1, 128)
    ints = regroup(ints).reshape(-1)
    patches = regroup(patches)
    memory_part = regroup(memory)
    lengths_all = ints[:5]
    counts = ints[5:8]
    bounds = ints[8 : 8 + MICRO * boxes * 2].reshape(MICRO, boxes, 2)
    labels = ints[8 + MICRO * boxes * 2 : total_ints].reshape(MICRO * boxes, classes)

    vec_hi = lax.reduce_precision(vector_weight, 8, 7)
    vec_mid = lax.reduce_precision(vector_weight - vec_hi, 8, 7)
    vec_lo = vector_weight - vec_hi - vec_mid
    small = jnp.concatenate(
        [embed_weight, head_weight, vec_hi, vec_mid, vec_lo], axis=0
    ).astype(bf16).T
    small = jnp.concatenate(gather_mp(small), axis=0)
    small = gather_dp(small, [1, 2] + list(range(3, dp_bits())) + [0])
    embed_t = small[:, :patch]
    head_t = small[:, patch : patch + classes]
    vec3 = small[:, patch + classes :].astype(f32)
    vectors = (vec3[:, :7] + vec3[:, 7:14] + vec3[:, 14:]).T

    taps_pos = jnp.concatenate(
        [
            conv_weight.reshape(12, head_cols),
            jnp.pad(position_bias.reshape(1, -1), ((0, 0), (0, head_cols - position_bias.size))),
        ]
    )
    taps_pos = gather_mp(taps_pos)
    conv_all = jnp.concatenate([t[:12] for t in taps_pos], axis=1).reshape(2, 6, width)
    rel_bias = jnp.concatenate(
        [t[12, : position_bias.size].reshape(position_bias.shape) for t in taps_pos], axis=0
    )

    up_low = up_weight.astype(bf16)
    down_low = down_weight.astype(bf16)
    qkv_pieces = gather_mp(up_low[:, : 3 * head_cols])
    qkv = jnp.concatenate(
        [p[:, j * head_cols : (j + 1) * head_cols] for j in range(3) for p in qkv_pieces], axis=1
    )
    qkv = gather_split(qkv)
    rest_pieces = gather_mp(jnp.concatenate([down_low, up_low[:, 3 * head_cols :]], axis=1))
    hidden_cols = up_weight.shape[1] - 3 * head_cols
    rest = jnp.concatenate(
        [p[:, :head_cols] for p in rest_pieces]
        + [p[:, head_cols : head_cols + hidden_cols] for p in rest_pieces]
        + [p[:, head_cols + hidden_cols :] for p in rest_pieces],
        axis=1,
    )
    rest = gather_split(rest)
    w_out = rest[:, :width]
    w_back = rest[:, width : width + 4 * hidden_cols]
    w_hidden = rest[:, width + 4 * hidden_cols :]

    place = jnp.arange(rows)
    token = 8 * (place % eighth) + 4 * ((place // eighth) % 2) + place // (2 * eighth)
    order = one_hot_rows(token, rows)
    patches = jnp.einsum("rt,mtc->mrc", order, patches, preferred_element_type=f32).astype(bf16)
    patches = patches.reshape(MICRO * rows, patch)
    mem_rows = memory_part.shape[2]
    mem_place = jnp.arange(mem_rows)
    mem_order = one_hot_rows(
        2 * (mem_place % (mem_rows // 2)) + mem_place // (mem_rows // 2), mem_rows
    )
    memory_part = jnp.einsum(
        "rt,abtc->abrc", mem_order, memory_part, preferred_element_type=f32
    ).astype(bf16)
    mem_parts = jnp.stack(group_gather(memory_part))
    part_of = [((q // 2) ^ core) + 2 * ((q % 2) ^ across) for q in range(4)]
    mem_full = jnp.concatenate(
        [lax.dynamic_index_in_dim(mem_parts, s, 0, keepdims=False) for s in part_of], axis=3
    )

    def compress(first, second, channel):
        return (
            first.astype(f32) * conv_all[channel, 4] + second.astype(f32) * conv_all[channel, 5]
        ).astype(bf16)

    half_mem = mem_rows // 2
    stored = []
    for m in range(2):
        stored.append(
            [
                (
                    mem_full[m, ch, :half_mem],
                    mem_full[m, ch, half_mem:],
                    compress(mem_full[m, ch, :half_mem], mem_full[m, ch, half_mem:], ch),
                )
                for ch in range(2)
            ]
        )

    embedded = contract_last(patches, embed_t) + vectors[0]
    normed = norm_rows(embedded, vectors[1], vectors[2]).astype(bf16)
    projected = product(normed, qkv)
    query = projected[:, :width].astype(bf16).reshape(MICRO, rows, width)
    raw = [
        projected[:, width * (1 + ch) : width * (2 + ch)].reshape(MICRO, 4, pooled, width)
        for ch in range(2)
    ]
    pools = [
        jnp.sum(raw[ch] * conv_all[ch, :4][None, :, None, :], axis=1).astype(bf16)
        for ch in range(2)
    ]
    gathered = [
        group_gather(jnp.stack([pools[0][m], pools[1][m]])) for m in range(MICRO)
    ]
    half_pool = pooled // 2
    for m in range(2):
        entry = []
        for ch in range(2):
            first = jnp.concatenate([g[ch, :half_pool] for g in gathered[m]])
            second = jnp.concatenate([g[ch, half_pool:] for g in gathered[m]])
            entry.append((first, second, compress(first, second, ch)))
        stored.append(entry)
    key_rows, value_rows = [], []
    for m in range(MICRO):
        for ch, out in ((0, key_rows), (1, value_rows)):
            out.append(
                jnp.concatenate(
                    [g[ch] for g in gathered[m]] + [stored[m + 1][ch][2], stored[m][ch][2]]
                )
            )

    part_quarter = [2 * (core ^ (s % 2)) + (across ^ (s // 2)) for s in range(4)]
    pool_place = jnp.arange(pooled)
    pool_token = 2 * (pool_place % half_pool) + pool_place // half_pool
    now_index = jnp.concatenate([pq * pooled + pool_token for pq in part_quarter])
    pool_index = jnp.concatenate([pq * half_pool + jnp.arange(half_pool) for pq in part_quarter])
    mem_index = jnp.arange(half_mem)

    def key_bias(m):
        newer_index = mem_index if m == 0 else pool_index
        older_index = mem_index if m < 2 else pool_index
        pieces = [
            (now_index, lengths_all[2 + m] // 4),
            (newer_index, lengths_all[1 + m] // 8),
            (older_index, lengths_all[m] // 8),
        ]
        return jnp.concatenate(
            [
                jnp.where((index < limit)[None, :], rel_bias[:, g : g + 1], -1e30)
                for g, (index, limit) in enumerate(pieces)
            ],
            axis=1,
        ).reshape(heads // QUAD, QUAD, -1)

    attended, probs = [], []
    for m in range(MICRO):
        out, prob = attend(query[m], key_rows[m], value_rows[m], key_bias(m))
        attended.append(out)
        probs.append(prob)
    attended_all = jnp.concatenate(attended)

    first_res = embedded + contract_last(attended_all, w_out)
    normed_mlp = norm_rows(first_res, vectors[3], vectors[4]).astype(bf16)
    hidden = product(normed_mlp, w_hidden)
    active = gelu_exact(hidden).astype(bf16)
    second_res = first_res + contract_last(active, w_back)
    final_rows = norm_rows(second_res, vectors[5], vectors[6])

    position = quarter * rows + token
    within = position % FRAME
    live = position[None, :] < lengths_all[2:, None]
    inside = (
        (within[None, None, :] >= bounds[:, :, 0:1])
        & (within[None, None, :] < bounds[:, :, 1:2])
        & live[:, None, :]
    )
    denominator = ((bounds[:, :, 1] - bounds[:, :, 0]) * (lengths_all[2:, None] // FRAME)).astype(
        f32
    )
    select = inside.astype(f32) / denominator[:, :, None]
    feature = jnp.einsum(
        "mbt,mtd->mbd", select, final_rows.reshape(MICRO, rows, width), precision=PRECISE
    ).reshape(MICRO * boxes, width)
    feature = group_sum_features(feature).astype(bf16)
    logits = product(feature, head_t)
    target = labels.astype(f32)
    keep = (jnp.arange(boxes)[None, :] < counts[:, None]).astype(f32).reshape(-1, 1)
    lead = (quarter == 0).astype(f32)
    loss_part = jnp.sum((jax.nn.softplus(logits) - target * logits) * keep) * lead
    grad_logits = ((jax.nn.sigmoid(logits) - target) * keep).astype(bf16)

    grad_head = contract_rows(feature, grad_logits) * lead
    grad_feature = contract_last(grad_logits, head_t).reshape(MICRO, boxes, width)
    grad_final = jnp.einsum("mbt,mbd->mtd", select, grad_feature, precision=PRECISE).reshape(
        MICRO * rows, width
    )
    grad_second, grad_gain3, grad_shift3 = jax.vjp(norm_rows, second_res, vectors[5], vectors[6])[
        1
    ](grad_final)
    grad_branch = grad_second.astype(bf16)
    grad_back = contract_rows(grad_branch, active)
    grad_active = product(grad_branch, w_back)
    grad_hidden = jax.vjp(gelu_exact, hidden)[1](grad_active)[0].astype(bf16)
    grad_w_hidden = contract_rows(normed_mlp, grad_hidden)
    rest_grad = scatter_split(
        jnp.concatenate([grad_back.astype(bf16), grad_w_hidden.astype(bf16)], axis=1)
    )
    grad_normed = contract_last(grad_hidden, w_hidden)
    grad_first, grad_gain2, grad_shift2 = jax.vjp(norm_rows, first_res, vectors[3], vectors[4])[1](
        grad_normed
    )
    grad_first = grad_first + grad_second
    grad_attn = grad_first.astype(bf16)
    grad_out = contract_rows(grad_attn, attended_all)
    grad_attended = product(grad_attn, w_out).astype(bf16).reshape(MICRO, rows, width)

    grad_query, pool_grads, bias_grads = [], [], []
    mem_taps = [jnp.zeros((2, width), f32), jnp.zeros((2, width), f32)]
    now = 4 * pooled
    for m in range(MICRO):
        dq, dk, dv, db = attend_back(
            query[m], key_rows[m], value_rows[m], probs[m], grad_attended[m]
        )
        grad_query.append(dq)
        bias_grads.append(db.reshape(heads, -1))
        low = jnp.stack([dk[:now].astype(bf16), dv[:now].astype(bf16)])
        pool_grads.append(
            group_scatter([low[:, s * pooled : (s + 1) * pooled] for s in range(4)])
        )
        for ch, grad in ((0, dk), (1, dv)):
            for which, start in ((m + 1, now), (m, now + half_mem)):
                part = grad[start : start + half_mem]
                mem_taps[ch] = mem_taps[ch] + jnp.stack(
                    [
                        jnp.sum(part * stored[which][ch][0].astype(f32), axis=0),
                        jnp.sum(part * stored[which][ch][1].astype(f32), axis=0),
                    ]
                )
    bias_total = bias_grads[0] + bias_grads[1] + bias_grads[2]
    grad_rel = jnp.stack(
        [
            jnp.sum(bias_total[:, :now], axis=1),
            jnp.sum(bias_total[:, now : now + half_mem], axis=1),
            jnp.sum(bias_total[:, now + half_mem :], axis=1),
        ],
        axis=1,
    )
    pool_grad = jnp.stack(pool_grads)
    raw_grads, taps_grads = [], []
    for ch in range(2):
        spread = pool_grad[:, ch][:, None] * conv_all[ch, :4][None, :, None, :]
        raw_grads.append(spread.astype(bf16).reshape(MICRO * rows, width))
        taps_grads.append(jnp.sum(pool_grad[:, ch][:, None] * raw[ch], axis=(0, 2)))
    grad_conv = jnp.stack(
        [jnp.concatenate([taps_grads[ch], mem_taps[ch]], axis=0) for ch in range(2)]
    )
    grad_projected = jnp.concatenate([jnp.concatenate(grad_query)] + raw_grads, axis=1)
    grad_qkv = contract_rows(normed, grad_projected)
    grad_normed_in = contract_last(grad_projected, qkv)
    grad_embedded, grad_gain1, grad_shift1 = jax.vjp(norm_rows, embedded, vectors[1], vectors[2])[
        1
    ](grad_normed_in)
    grad_embedded = (grad_embedded + grad_first).astype(bf16)
    grad_embed = contract_rows(grad_embedded, patches)
    grad_vectors = jnp.stack(
        [
            jnp.sum(grad_embedded.astype(f32), axis=0),
            grad_gain1,
            grad_shift1,
            grad_gain2,
            grad_shift2,
            grad_gain3,
            grad_shift3,
        ]
    )

    attn_grad = scatter_split(
        jnp.concatenate([grad_out.astype(bf16), grad_qkv.astype(bf16)], axis=1)
    )
    small_grad = scatter_dp(
        jnp.concatenate([grad_embed, grad_head, grad_vectors.T], axis=1),
        list(range(dp_bits())),
    )
    small_grad = scatter_mp([small_grad[j * sub : (j + 1) * sub] for j in range(4)]).T
    embed_grad = small_grad[:patch]
    head_grad = small_grad[patch : patch + classes]
    vector_grad = small_grad[patch + classes :]

    rest_mine = scatter_mp(
        [
            jnp.concatenate(
                [
                    rest_grad[:, j * hidden_cols : (j + 1) * hidden_cols],
                    rest_grad[:, (4 + j) * hidden_cols : (5 + j) * hidden_cols],
                ],
                axis=1,
            )
            for j in range(4)
        ]
    )
    attn_mine = scatter_mp(
        [
            jnp.concatenate(
                [
                    attn_grad[:, i * width + j * head_cols : i * width + (j + 1) * head_cols]
                    for i in range(4)
                ],
                axis=1,
            )
            for j in range(4)
        ]
    )
    down_grad = jnp.concatenate([attn_mine[:, :head_cols], rest_mine[:, :hidden_cols]], axis=1)
    up_grad = jnp.concatenate([attn_mine[:, head_cols:], rest_mine[:, hidden_cols:]], axis=1)

    count_local = jnp.sum(box_count).astype(f32) * (mp_index == 0).astype(f32)
    flat = jnp.concatenate(
        [grad_conv.reshape(-1), grad_rel.reshape(-1), loss_part[None], count_local[None]]
    )
    size = flat.shape[0]
    flat = sum_all(jnp.pad(flat, (0, -size % 1024)).reshape(-1, 128)).reshape(-1)
    conv_full = flat[: 12 * width].reshape(2, 6, 4, head_cols)
    conv_grad = lax.dynamic_index_in_dim(conv_full, mp_index, 2, keepdims=False)
    rel_full = flat[12 * width : 12 * width + heads * 3].reshape(4, heads // 4, 3)
    position_grad = lax.dynamic_index_in_dim(rel_full, mp_index, 0, keepdims=False)
    loss_global = flat[size - 2]
    box_total = flat[size - 1]

    reduced = (up_grad, down_grad, embed_grad, head_grad, vector_grad, conv_grad, position_grad)
    squares = sum((jnp.sum(gradient * gradient) for gradient in reduced[:5]))
    squares = squares + (
        jnp.sum(conv_grad * conv_grad) + jnp.sum(position_grad * position_grad)
    ) / dp_count
    square_total = sum_all(jnp.full((8, 128), squares, f32))[0, 0]
    grad_norm = jnp.sqrt(square_total) / box_total
    scaling = jnp.minimum(1.0, THRESHOLD / grad_norm) / box_total
    masters = (
        up_weight,
        down_weight,
        embed_weight,
        head_weight,
        vector_weight,
        conv_weight,
        position_bias,
    )
    moments = (
        up_moment,
        down_moment,
        embed_moment,
        head_moment,
        vector_moment,
        conv_moment,
        position_moment,
    )
    averages = (
        up_average,
        down_average,
        embed_average,
        head_average,
        vector_average,
        conv_average,
        position_average,
    )
    rates = (LEARNING,) * 4 + (VECTOR_LEARNING,) * 3
    results = [
        apply_update(weight, gradient * scaling, moment, average, rate)
        for weight, gradient, moment, average, rate in zip(
            masters, reduced, moments, averages, rates
        )
    ]

    kept = []
    for m in (1, 2):
        parts = jnp.stack(gathered[m]).reshape(4, 2, 2, half_pool, 4, head_cols)
        parts = lax.dynamic_index_in_dim(parts, quarter, 4, keepdims=False)
        ordered = jnp.stack(
            [lax.dynamic_index_in_dim(parts, s, 0, keepdims=False) for s in part_of], axis=1
        )
        kept.append(ordered.transpose(0, 1, 3, 2, 4).reshape(2, 4 * pooled, head_cols))
    new_memory = regroup(jnp.stack(kept))
    return (
        (loss_global, box_total, grad_norm, new_memory)
        + tuple(r[0] for r in results)
        + tuple(r[1] for r in results)
        + tuple(r[2] for r in results)
        + (results[0][0].astype(bf16), results[1][0].astype(bf16))
    )


def solution(mesh):
    both = ("dp", "mp")
    weight_specs = (
        P("dp", "mp"),
        P("dp", "mp"),
        P(None, both),
        P(None, both),
        P(None, both),
        P(None, None, "mp"),
        P("mp", None),
    )
    memory_spec = P(None, None, "dp", "mp")
    return jax.shard_map(
        shards,
        mesh=mesh,
        in_specs=(
            P(None, both, None),
            P("dp", None),
            P("dp", None),
            P("dp", None, None, None),
            P("dp", None, None, None),
            memory_spec,
        )
        + weight_specs * 3,
        out_specs=(P(), P(), P(), memory_spec)
        + weight_specs * 3
        + (P("dp", "mp"), P("dp", "mp")),
        check_vma=False,
    )
```

```python
import functools

import jax
import jax.numpy as jnp
from jax import lax
from jax.experimental import pallas as pl
from jax.experimental.pallas import tpu as pltpu
from jax.sharding import PartitionSpec as P

MICRO = 3
FRAME = 64
EPSILON = 1e-06
LEARNING = 300.0
VECTOR_LEARNING = 6000.0
MOMENTUM = 0.5
AVERAGING = 0.5
THRESHOLD = 0.05
PRECISE = lax.Precision.HIGHEST
QUAD = 4
bf16 = jnp.bfloat16
f32 = jnp.float32


NEAR = 48 * 1024 * 1024


def product(first_operand, second_operand):
    return jnp.dot(first_operand, second_operand, preferred_element_type=f32)


def contract_last(first_operand, second_operand):
    return lax.dot_general(
        first_operand, second_operand, (((1,), (1,)), ((), ())), preferred_element_type=f32
    )


def contract_rows(first_operand, second_operand):
    return lax.dot_general(
        first_operand, second_operand, (((0,), (0,)), ((), ())), preferred_element_type=f32
    )


def apply_update(weight, gradient, moment, average, rate):
    moment = MOMENTUM * moment + gradient
    updated = weight - rate * (gradient + MOMENTUM * moment)
    return (updated, moment, AVERAGING * average + (1.0 - AVERAGING) * updated)


def swap_dp(inputs, mask):
    size = lax.axis_size("dp")
    return lax.ppermute(inputs, "dp", [(i, i ^ mask) for i in range(size)])


def swap_mp(inputs, mask):
    size = lax.axis_size("mp")
    return lax.ppermute(inputs, "mp", [(i, i ^ mask) for i in range(size)])


def dp_bits():
    return lax.axis_size("dp").bit_length() - 1


def regroup(inputs):
    count = lax.axis_size("dp")
    pairs = []
    for d in range(count):
        for z in range(4):
            hi, x, k = d // 4, (d // 2) % 2, d % 2
            pairs.append((d * 4 + z, (hi * 4 + (z % 2) * 2 + z // 2) * 4 + 2 * k + x))
    return lax.ppermute(inputs, ("dp", "mp"), pairs)


def gather_mp(inputs):
    return [inputs] + [swap_mp(inputs, s) for s in (1, 2, 3)]


def scatter_mp(pieces):
    total = pieces[0].astype(f32)
    for s in (1, 2, 3):
        total = total + swap_mp(pieces[s], s).astype(f32)
    return total


def gather_dp(inputs, order):
    pieces = {0: inputs}
    rows = inputs.shape[0]
    for bit in order:
        keys = sorted(pieces)
        sent = jnp.concatenate([pieces[k] for k in keys]) if len(keys) > 1 else inputs
        got = swap_dp(sent, 1 << bit)
        for i, k in enumerate(keys):
            pieces[k ^ (1 << bit)] = got[i * rows : (i + 1) * rows]
    near = jnp.concatenate([pieces[k] for k in sorted(pieces)])
    return near, swap_dp(near, 1)


def scatter_dp(near, far, order):
    got = swap_dp(far, 1)
    left = list(range(1, dp_bits()))
    rows = near.shape[0] >> len(left)
    columns = near.shape[1]
    kind = far.dtype
    for bit in order:
        at = left.index(bit)
        shape = (-1, 2, rows << at, columns)
        mine, other = near.reshape(shape), got.reshape(shape)
        away = (mine[:, 1].astype(f32) + other[:, 1].astype(f32)).astype(kind)
        near = (mine[:, 0].astype(f32) + other[:, 0].astype(f32)).astype(kind)
        near = near.reshape(-1, columns)
        got = swap_dp(away.reshape(-1, columns), 1 << bit)
        left.remove(bit)
    return (near.astype(f32) + got.astype(f32)).astype(kind)


def sum_dp(inputs):
    for bit in range(dp_bits()):
        inputs = inputs + swap_dp(inputs, 1 << bit)
    return inputs


def sum_all(inputs):
    inputs = sum_dp(inputs)
    for mask in (1, 2):
        inputs = inputs + swap_mp(inputs, mask)
    return inputs


def group_sum_features(inputs):
    count = lax.axis_size("dp")
    width = inputs.shape[1] // count
    order = [b for b in range(count) if b % 2 == 0] + [b for b in range(count) if b % 2]
    for mask in (1, 2):
        got = swap_dp(inputs, mask)
        at = [order.index(b ^ mask) for b in order]
        inputs = inputs + jnp.concatenate(
            [got[:, p * width : (p + 1) * width] for p in at], axis=1
        )
    return inputs


def call(body, grid, in_specs, out_specs, out_shape, operands, flops, scratch=(), alias=None):
    moved = sum(o.size * o.dtype.itemsize for o in operands)
    return pl.pallas_call(
        body,
        grid=grid,
        in_specs=in_specs,
        out_specs=out_specs,
        out_shape=out_shape,
        scratch_shapes=list(scratch),
        input_output_aliases=alias or {},
        compiler_params=pltpu.CompilerParams(vmem_limit_bytes=NEAR),
        cost_estimate=pl.CostEstimate(flops=flops, bytes_accessed=moved, transcendentals=0),
    )(*operands)


def whole(array):
    return pl.BlockSpec(array.shape, lambda *i, n=array.ndim: (0,) * n)


def fetch(pairs, sems):
    copies = [
        pltpu.make_async_copy(source, target, sems.at[i])
        for i, (source, target) in enumerate(pairs)
    ]
    for copy in copies:
        copy.start()
    for copy in copies:
        copy.wait()


def standard(inputs):
    centered = inputs - jnp.mean(inputs, axis=-1, keepdims=True)
    scale = lax.rsqrt(jnp.mean(centered * centered, axis=-1, keepdims=True) + EPSILON)
    return centered * scale, scale


def standard_back(grad, unit, scale):
    return scale * (
        grad
        - jnp.mean(grad, axis=-1, keepdims=True)
        - unit * jnp.mean(grad * unit, axis=-1, keepdims=True)
    )


def memory_in_kernel(index_ref, order_ref, one_ref, two_ref, three_ref, four_ref, out_ref):
    parts = [r[0, 0] for r in (one_ref, two_ref, three_ref, four_ref)]
    blocks = []
    for c in range(4):
        s = index_ref[c]
        chosen = parts[3]
        for p in (2, 1, 0):
            chosen = jnp.where(s == p, parts[p], chosen)
        blocks.append(chosen)
    out_ref[0, 0] = contract_last(order_ref[...], jnp.concatenate(blocks)).astype(bf16)


def memory_in(index, order, parts):
    _, _, columns, rows = parts[0].shape
    return call(
        memory_in_kernel,
        (2, 2),
        [pl.BlockSpec(memory_space=pltpu.SMEM), pl.BlockSpec((rows, rows), lambda i, j: (0, 0))]
        + [pl.BlockSpec((1, 1, columns, rows), lambda i, j: (i, j, 0, 0))] * 4,
        pl.BlockSpec((1, 1, rows, 4 * columns), lambda i, j: (i, j, 0, 0)),
        jax.ShapeDtypeStruct((2, 2, rows, 4 * columns), bf16),
        (index, order) + tuple(parts),
        8 * rows * rows * 4 * columns,
    )


def memory_out_kernel(index_ref, order_ref, *refs):
    out_ref = refs[-1]
    chosen = index_ref[0]
    for m in range(2):
        rows = jnp.concatenate([r[0, 0] for r in refs[4 * m : 4 * m + 4]])
        turned = contract_rows(rows, order_ref[...]).astype(bf16)
        columns = turned.shape[0] // 4
        blocks = [turned[c * columns : (c + 1) * columns] for c in range(4)]
        block = blocks[3]
        for c in (2, 1, 0):
            block = jnp.where(chosen == c, blocks[c], block)
        out_ref[m, 0] = block


def memory_out(index, order, parts):
    _, _, rows, width = parts[0][0].shape
    return call(
        memory_out_kernel,
        (2,),
        [
            pl.BlockSpec(memory_space=pltpu.SMEM),
            pl.BlockSpec((4 * rows, 4 * rows), lambda i: (0, 0)),
        ]
        + [pl.BlockSpec((1, 1, rows, width), lambda i, m=m: (m, i, 0, 0)) for _, m in parts],
        pl.BlockSpec((2, 1, width // 4, 4 * rows), lambda i: (0, i, 0, 0)),
        jax.ShapeDtypeStruct((2, 2, width // 4, 4 * rows), bf16),
        (index, order) + tuple(a for a, _ in parts),
        8 * (4 * rows) ** 2 * width,
    )


def embed_kernel(
    patch_ref, order_ref, embed_ref, vec_ref, taps_ref, qk0, qk1, vo0, vo1,
    sorted_ref, embedded_ref, normed_ref, query_ref, key_ref, value_ref, pool_ref,
    qk_s, v_s, sems,
):
    width = embedded_ref.shape[1]
    half = width // 2

    @pl.when(pl.program_id(0) == 0)
    def _():
        fetch(
            [
                (qk0, qk_s.at[:half]),
                (qk1, qk_s.at[half:]),
                (vo0.at[:, :width], v_s.at[:half]),
                (vo1.at[:, :width], v_s.at[half:]),
            ],
            sems,
        )

    patch = contract_last(order_ref[...], patch_ref[0]).astype(bf16)
    sorted_ref[...] = patch
    embedded = contract_last(patch, embed_ref[...]) + vec_ref[0:1]
    embedded_ref[...] = embedded
    unit, _ = standard(embedded)
    normed = (unit * vec_ref[1:2] + vec_ref[2:3]).astype(bf16)
    normed_ref[...] = normed
    query_ref[...] = product(normed, qk_s[:, :width]).astype(bf16)
    for ch, weight, raw_ref in ((0, qk_s[:, width:], key_ref), (1, v_s[...], value_ref)):
        raw = product(normed, weight)
        raw_ref[...] = raw.astype(bf16)
        rows = raw.shape[0] // 4
        pooled = raw[:rows] * taps_ref[ch, 0:1]
        for t in range(1, 4):
            pooled = pooled + raw[t * rows : (t + 1) * rows] * taps_ref[ch, t : t + 1]
        pool_ref[0, ch] = pooled.astype(bf16)


def embed(patches_t, order, embed_t, vec, taps, qk, vo):
    _, patch, rows = patches_t.shape
    width = vec.shape[1]
    total = MICRO * rows

    def tile(columns):
        return pl.BlockSpec((rows, columns), lambda i: (i, 0))

    anywhere = pl.BlockSpec(memory_space=pl.ANY)
    return call(
        embed_kernel,
        (MICRO,),
        [pl.BlockSpec((1, patch, rows), lambda i: (i, 0, 0))]
        + [whole(a) for a in (order, embed_t, vec, taps)]
        + [anywhere] * 4,
        [tile(patch), tile(width), tile(width), tile(width), tile(width), tile(width)]
        + [pl.BlockSpec((1, 2, rows // 4, width), lambda i: (i, 0, 0, 0))],
        [
            jax.ShapeDtypeStruct((total, patch), bf16),
            jax.ShapeDtypeStruct((total, width), f32),
        ]
        + [jax.ShapeDtypeStruct((total, width), bf16)] * 4
        + [jax.ShapeDtypeStruct((MICRO, 2, rows // 4, width), bf16)],
        (patches_t, order, embed_t, vec, taps) + qk + vo,
        2 * total * width * (patch + 3 * width),
        scratch=[
            pltpu.VMEM((width, 2 * width), bf16),
            pltpu.VMEM((width, width), bf16),
            pltpu.SemaphoreType.DMA((4,)),
        ],
    )


def attend_kernel(sources, q_ref, taps_ref, bias_ref, *refs):
    count = sum(sources)
    now, newer = refs[: sources[0]], refs[sources[0] : sources[0] + sources[1]]
    older = refs[sources[0] + sources[1] : count]
    out_ref, prob_ref, key_ref, value_ref = refs[-4:]
    query = q_ref[...]
    rows, width = query.shape
    size = width // QUAD
    for ch, target in ((0, key_ref), (1, value_ref)):
        at = 0
        for r in now:
            n = r.shape[2]
            target[at : at + n] = r[0, ch]
            at += n
        first, second = taps_ref[ch, 4:5], taps_ref[ch, 5:6]
        for r in newer + older:
            n = r.shape[2] // 2
            target[at : at + n] = (
                r[0, ch, :n].astype(f32) * first + r[0, ch, n:].astype(f32) * second
            ).astype(bf16)
            at += n
    keys_t = key_ref[...].T
    values = value_ref[...]
    lane = lax.broadcasted_iota(jnp.int32, (rows, width), 1) // size
    scaled = query * (size**-0.5)
    total = query.astype(f32)
    for h in range(QUAD):
        own = jnp.where(lane == h, scaled, jnp.zeros_like(scaled))
        scores = product(own, keys_t) + bias_ref[0, h : h + 1, :]
        top = jnp.max(scores, axis=-1, keepdims=True)
        exponent = jnp.exp(scores - top)
        denominator = jnp.sum(exponent, axis=-1, keepdims=True)
        probs = (exponent * (1.0 / denominator)).astype(bf16)
        prob_ref[h] = probs
        total = total + jnp.where(lane == h, product(probs, values), 0.0)
    out_ref[...] = total.astype(bf16)


def source_specs(entries, block):
    return [
        pl.BlockSpec((1, 2, a.shape[2], block), lambda i, m=m: (m, 0, 0, i)) for a, m in entries
    ]


def attend(micro, query, taps, bias, now, newer, older, before):
    rows = query.shape[0] // MICRO
    width = query.shape[1]
    count = bias.shape[2]
    quads = bias.shape[0]
    block = width // quads
    entries = now + newer + older
    operands = (query, taps, bias) + tuple(a for a, _ in entries)
    specs = [
        pl.BlockSpec((rows, block), lambda i: (micro, i)),
        pl.BlockSpec((2, 6, block), lambda i: (0, 0, i)),
        pl.BlockSpec((1, QUAD, count), lambda i: (i, 0, 0)),
    ] + source_specs(entries, block)
    alias = {}
    if before is not None:
        alias = {len(operands): 0}
        operands = operands + (before,)
        specs.append(pl.BlockSpec(memory_space=pl.ANY))
    return call(
        functools.partial(attend_kernel, (len(now), len(newer), len(older))),
        (quads,),
        specs,
        [
            pl.BlockSpec((rows, block), lambda i: (micro, i)),
            pl.BlockSpec((QUAD, rows, count), lambda i: (i, 0, 0)),
            pl.BlockSpec((count, block), lambda i: (0, i)),
            pl.BlockSpec((count, block), lambda i: (0, i)),
        ],
        [
            jax.ShapeDtypeStruct(query.shape, bf16),
            jax.ShapeDtypeStruct((quads * QUAD, rows, count), bf16),
            jax.ShapeDtypeStruct((count, width), bf16),
            jax.ShapeDtypeStruct((count, width), bf16),
        ],
        operands,
        4 * rows * count * width * 4,
        alias=alias,
    )


def attend_back_kernel(sources, q_ref, k_ref, v_ref, prob_ref, grad_ref, *refs):
    entries = refs[: sum(sources)]
    dq_ref, keep_ref, send_ref, taps_ref, bias_ref = refs[-5:]
    query = q_ref[...]
    grad = grad_ref[...]
    rows, width = query.shape
    size = width // QUAD
    keys = k_ref[...]
    count = keys.shape[0]
    values_t = v_ref[...].T
    query_t = query.T
    grad_t = grad.T
    scaling = size**-0.5
    lane = lax.broadcasted_iota(jnp.int32, (rows, width), 1) // size
    total = jnp.zeros((rows, width), f32)
    ones = jnp.ones((16, rows), bf16)
    half = count // 2
    spot = lax.broadcasted_iota(jnp.int32, (1, 128), 1)
    key_parts, value_parts = [], []
    for h in range(QUAD):
        own = jnp.where(lane == h, grad, jnp.zeros_like(grad))
        probs_low = prob_ref[h]
        probs = probs_low.astype(f32)
        pulled = probs * product(own, values_t)
        shift = jnp.sum(pulled, axis=-1, keepdims=True)
        score_grad = (pulled - probs * shift).astype(bf16)
        total = total + jnp.where(lane == h, product(score_grad, keys), 0.0)
        left = jnp.concatenate([query_t[h * size : (h + 1) * size], ones])
        found = product(left, score_grad)
        key_parts.append(found[:size])
        sums = found[size : size + 1]
        row = jnp.zeros((1, 128), f32)
        for g, (a, b) in enumerate(((0, half), (half, half + half // 2), (half + half // 2, count))):
            row = row + jnp.where(spot == g, jnp.sum(sums[:, a:b], axis=1, keepdims=True), 0.0)
        bias_ref[0, h : h + 1, :] = row
        value_parts.append(product(grad_t[h * size : (h + 1) * size], probs_low))
    dq_ref[...] = (total * scaling + grad.astype(f32)).astype(bf16)
    part = keep_ref.shape[2]
    for ch, parts, factor in ((0, key_parts, scaling), (1, value_parts, 1.0)):
        found = jnp.concatenate(parts).T * factor
        for s in range(4):
            target = send_ref if s % 2 else keep_ref
            target[ch, s // 2] = found[s * part : (s + 1) * part].astype(bf16)
        at = half
        first = jnp.zeros((1, width), f32)
        second = jnp.zeros((1, width), f32)
        for r in entries:
            n = r.shape[2] // 2
            piece = found[at : at + n]
            first = first + jnp.sum(piece * r[0, ch, :n].astype(f32), axis=0, keepdims=True)
            second = second + jnp.sum(piece * r[0, ch, n:].astype(f32), axis=0, keepdims=True)
            at += n
        taps_ref[ch, 0:1] = first
        taps_ref[ch, 1:2] = second


def attend_back(micro, query, keys, values, probs, grad, newer, older, before):
    heads, rows, count = probs.shape
    width = query.shape[1]
    quads = heads // QUAD
    block = width // quads
    entries = newer + older
    operands = (query, keys, values, probs, grad) + tuple(a for a, _ in entries)
    specs = [
        pl.BlockSpec((rows, block), lambda i: (micro, i)),
        pl.BlockSpec((count, block), lambda i: (0, i)),
        pl.BlockSpec((count, block), lambda i: (0, i)),
        pl.BlockSpec((QUAD, rows, count), lambda i: (i, 0, 0)),
        pl.BlockSpec((rows, block), lambda i: (micro, i)),
    ] + source_specs(entries, block)
    alias = {}
    if before is not None:
        alias = {len(operands): 0}
        operands = operands + (before,)
        specs.append(pl.BlockSpec(memory_space=pl.ANY))
    part = count // 8
    return call(
        functools.partial(attend_back_kernel, (len(newer), len(older))),
        (quads,),
        specs,
        [
            pl.BlockSpec((rows, block), lambda i: (micro, i)),
            pl.BlockSpec((2, 2, part, block), lambda i: (0, 0, 0, i)),
            pl.BlockSpec((2, 2, part, block), lambda i: (0, 0, 0, i)),
            pl.BlockSpec((2, 2, block), lambda i: (0, 0, i)),
            pl.BlockSpec((1, QUAD, 128), lambda i: (i, 0, 0)),
        ],
        [
            jax.ShapeDtypeStruct(query.shape, bf16),
            jax.ShapeDtypeStruct((2, 2, part, width), bf16),
            jax.ShapeDtypeStruct((2, 2, part, width), bf16),
            jax.ShapeDtypeStruct((2, 2, width), f32),
            jax.ShapeDtypeStruct((quads, QUAD, 128), f32),
        ],
        operands,
        8 * rows * count * width * 4,
        alias=alias,
    )


def gelu_pair(inputs):
    size = jnp.abs(inputs)
    t = 1.0 / (1.0 + (0.3275911 * 0.5**0.5) * size)
    bell = jnp.exp(-0.5 * inputs * inputs)
    tail = (
        t
        * (
            0.5 * 0.254829592
            + t
            * (
                0.5 * -0.284496736
                + t * (0.5 * 1.421413741 + t * (0.5 * -1.453152027 + t * (0.5 * 1.061405429)))
            )
        )
        * bell
    )
    share = jnp.where(inputs > 0.0, 1.0 - tail, tail)
    return inputs * share, share + inputs * bell * 0.3989422804014327


def mlp_kernel(
    attended_ref, embedded_ref, vec_ref, select_ref, vo0, vo1, wb0, wb1, wh0, wh1,
    first_ref, normed_ref, active_ref, slope_ref, second_ref, feature_ref,
    wo_s, wb_s, wh_s, sems,
):
    width = embedded_ref.shape[1]
    half = width // 2

    @pl.when(pl.program_id(0) == 0)
    def _():
        fetch(
            [
                (vo0.at[:, width:], wo_s.at[:half]),
                (vo1.at[:, width:], wo_s.at[half:]),
                (wh0, wh_s.at[:half]),
                (wh1, wh_s.at[half:]),
                (wb0, wb_s.at[:half]),
                (wb1, wb_s.at[half:]),
            ],
            sems,
        )

    first = embedded_ref[...] + contract_last(attended_ref[...], wo_s[...])
    first_ref[...] = first
    unit, _ = standard(first)
    normed = (unit * vec_ref[3:4] + vec_ref[4:5]).astype(bf16)
    normed_ref[...] = normed
    total = first
    chunk = 512
    for at in range(0, wh_s.shape[1], chunk):
        hidden = product(normed, wh_s[:, at : at + chunk])
        value, slope = gelu_pair(hidden)
        value = value.astype(bf16)
        active_ref[:, at : at + chunk] = value
        slope_ref[:, at : at + chunk] = slope.astype(bf16)
        total = total + contract_last(value, wb_s[:, at : at + chunk])
    second_ref[...] = total
    unit, _ = standard(total)
    final = unit * vec_ref[5:6] + vec_ref[6:7]
    feature_ref[0] = jnp.dot(
        select_ref[0], final, precision=PRECISE, preferred_element_type=f32
    )


def mlp(attended, embedded, vec, select, vo, wb, wh):
    total, width = embedded.shape
    rows = total // MICRO
    units = wb[0].shape[1]
    boxes = select.shape[1]

    def tile(columns):
        return pl.BlockSpec((rows, columns), lambda i: (i, 0))

    return call(
        mlp_kernel,
        (MICRO,),
        [
            tile(width),
            tile(width),
            whole(vec),
            pl.BlockSpec((1, boxes, rows), lambda i: (i, 0, 0)),
        ]
        + [pl.BlockSpec(memory_space=pl.ANY)] * 6,
        [tile(width), tile(width), tile(units), tile(units), tile(width)]
        + [pl.BlockSpec((1, boxes, width), lambda i: (i, 0, 0))],
        [
            jax.ShapeDtypeStruct((total, width), f32),
            jax.ShapeDtypeStruct((total, width), bf16),
            jax.ShapeDtypeStruct((total, units), bf16),
            jax.ShapeDtypeStruct((total, units), bf16),
            jax.ShapeDtypeStruct((total, width), f32),
            jax.ShapeDtypeStruct((MICRO, boxes, width), f32),
        ],
        (attended, embedded, vec, select) + vo + wb + wh,
        2 * total * width * (width + 2 * units),
        scratch=[
            pltpu.VMEM((width, width), bf16),
            pltpu.VMEM((width, units), bf16),
            pltpu.VMEM((width, units), bf16),
            pltpu.SemaphoreType.DMA((6,)),
        ],
    )


def mlp_back_kernel(
    pull_ref, select_ref, second_ref, first_ref, slope_ref, vec_ref, vo0, vo1, wb0, wb1, wh0, wh1,
    branch_ref, hidden_ref, attn_ref, first_grad_ref, attended_ref, sums_ref,
    wo_s, wb_s, wh_s, sems,
):
    width = second_ref.shape[1]
    half = width // 2

    @pl.when(pl.program_id(0) == 0)
    def _():
        sums_ref[...] = jnp.zeros_like(sums_ref)
        fetch(
            [
                (vo0.at[:, width:], wo_s.at[:half]),
                (vo1.at[:, width:], wo_s.at[half:]),
                (wh0, wh_s.at[:half]),
                (wh1, wh_s.at[half:]),
                (wb0, wb_s.at[:half]),
                (wb1, wb_s.at[half:]),
            ],
            sems,
        )

    pull = lax.dot_general(
        select_ref[0],
        pull_ref[0],
        (((0,), (0,)), ((), ())),
        precision=PRECISE,
        preferred_element_type=f32,
    )
    unit, scale = standard(second_ref[...])
    sums_ref[2:3] += jnp.sum(pull * unit, axis=0, keepdims=True)
    sums_ref[3:4] += jnp.sum(pull, axis=0, keepdims=True)
    second_grad = standard_back(pull * vec_ref[5:6], unit, scale)
    branch = second_grad.astype(bf16)
    branch_ref[...] = branch
    chunk = 512
    normed_grad = jnp.zeros(second_grad.shape, f32)
    for at in range(0, wh_s.shape[1], chunk):
        active_grad = product(branch, wb_s[:, at : at + chunk])
        hidden_grad = (active_grad * slope_ref[:, at : at + chunk].astype(f32)).astype(bf16)
        hidden_ref[:, at : at + chunk] = hidden_grad
        normed_grad = normed_grad + contract_last(hidden_grad, wh_s[:, at : at + chunk])
    unit, scale = standard(first_ref[...])
    sums_ref[0:1] += jnp.sum(normed_grad * unit, axis=0, keepdims=True)
    sums_ref[1:2] += jnp.sum(normed_grad, axis=0, keepdims=True)
    first_grad = standard_back(normed_grad * vec_ref[3:4], unit, scale) + second_grad
    first_grad_ref[...] = first_grad
    attn = first_grad.astype(bf16)
    attn_ref[...] = attn
    attended_ref[...] = product(attn, wo_s[...]).astype(bf16)


def mlp_back(pull, select, second, first, slope, vec, vo, wb, wh):
    total, width = second.shape
    rows = total // MICRO
    units = wb[0].shape[1]
    boxes = select.shape[1]

    def tile(columns):
        return pl.BlockSpec((rows, columns), lambda i: (i, 0))

    return call(
        mlp_back_kernel,
        (MICRO,),
        [
            pl.BlockSpec((1, boxes, width), lambda i: (i, 0, 0)),
            pl.BlockSpec((1, boxes, rows), lambda i: (i, 0, 0)),
            tile(width),
            tile(width),
            tile(units),
            whole(vec),
        ]
        + [pl.BlockSpec(memory_space=pl.ANY)] * 6,
        [tile(width), tile(units), tile(width), tile(width), tile(width)]
        + [pl.BlockSpec((8, width), lambda i: (0, 0))],
        [
            jax.ShapeDtypeStruct((total, width), bf16),
            jax.ShapeDtypeStruct((total, units), bf16),
            jax.ShapeDtypeStruct((total, width), bf16),
            jax.ShapeDtypeStruct((total, width), f32),
            jax.ShapeDtypeStruct((total, width), bf16),
            jax.ShapeDtypeStruct((8, width), f32),
        ],
        (pull, select, second, first, slope, vec) + vo + wb + wh,
        2 * total * width * (width + 2 * units),
        scratch=[
            pltpu.VMEM((width, width), bf16),
            pltpu.VMEM((width, units), bf16),
            pltpu.VMEM((width, units), bf16),
            pltpu.SemaphoreType.DMA((6,)),
        ],
    )


def embed_back_kernel(
    dq_ref, pool_ref, key_ref, value_ref, taps_ref, embedded_ref, first_ref, vec_ref,
    qk0, qk1, vo0, vo1,
    projected_ref, grad_ref, sums_ref, taps_out,
    qk_s, v_s, sems,
):
    width = embedded_ref.shape[1]
    half = width // 2

    @pl.when(pl.program_id(0) == 0)
    def _():
        sums_ref[...] = jnp.zeros_like(sums_ref)
        taps_out[...] = jnp.zeros_like(taps_out)
        fetch(
            [
                (qk0, qk_s.at[:half]),
                (qk1, qk_s.at[half:]),
                (vo0.at[:, :width], v_s.at[:half]),
                (vo1.at[:, :width], v_s.at[half:]),
            ],
            sems,
        )

    projected_ref[:, :width] = dq_ref[...]
    rows = pool_ref.shape[2]
    for ch, raw_ref in ((0, key_ref), (1, value_ref)):
        pool = pool_ref[0, ch]
        for t in range(4):
            projected_ref[t * rows : (t + 1) * rows, (1 + ch) * width : (2 + ch) * width] = (
                pool * taps_ref[ch, t : t + 1]
            ).astype(bf16)
            raw = raw_ref[t * rows : (t + 1) * rows].astype(f32)
            taps_out[4 * ch + t : 4 * ch + t + 1] += jnp.sum(pool * raw, axis=0, keepdims=True)
    normed_grad = contract_last(projected_ref[:, : 2 * width], qk_s[...])
    normed_grad = normed_grad + contract_last(projected_ref[:, 2 * width :], v_s[...])
    unit, scale = standard(embedded_ref[...])
    sums_ref[1:2] += jnp.sum(normed_grad * unit, axis=0, keepdims=True)
    sums_ref[2:3] += jnp.sum(normed_grad, axis=0, keepdims=True)
    grad = standard_back(normed_grad * vec_ref[1:2], unit, scale) + first_ref[...]
    grad = grad.astype(bf16)
    grad_ref[...] = grad
    sums_ref[0:1] += jnp.sum(grad.astype(f32), axis=0, keepdims=True)


def embed_back(dq, pool, keys, values, taps, embedded, first_grad, vec, qk, vo):
    total, width = embedded.shape
    rows = total // MICRO

    def tile(columns):
        return pl.BlockSpec((rows, columns), lambda i: (i, 0))

    return call(
        embed_back_kernel,
        (MICRO,),
        [
            tile(width),
            pl.BlockSpec((1, 2, rows // 4, width), lambda i: (i, 0, 0, 0)),
            tile(width),
            tile(width),
            whole(taps),
            tile(width),
            tile(width),
            whole(vec),
        ]
        + [pl.BlockSpec(memory_space=pl.ANY)] * 4,
        [
            tile(3 * width),
            tile(width),
            pl.BlockSpec((8, width), lambda i: (0, 0)),
            pl.BlockSpec((8, width), lambda i: (0, 0)),
        ],
        [
            jax.ShapeDtypeStruct((total, 3 * width), bf16),
            jax.ShapeDtypeStruct((total, width), bf16),
            jax.ShapeDtypeStruct((8, width), f32),
            jax.ShapeDtypeStruct((8, width), f32),
        ],
        (dq, pool, keys, values, taps, embedded, first_grad, vec) + qk + vo,
        2 * total * width * 3 * width,
        scratch=[
            pltpu.VMEM((width, 2 * width), bf16),
            pltpu.VMEM((width, width), bf16),
            pltpu.SemaphoreType.DMA((4,)),
        ],
    )


def one_hot_rows(index, count):
    return (index[:, None] == jnp.arange(count)[None, :]).astype(bf16)


def shards(
    patches,
    clip_len,
    box_count,
    box_bounds,
    box_labels,
    memory,
    up_weight,
    down_weight,
    embed_weight,
    head_weight,
    vector_weight,
    conv_weight,
    position_bias,
    up_moment,
    down_moment,
    embed_moment,
    head_moment,
    vector_moment,
    conv_moment,
    position_moment,
    up_average,
    down_average,
    embed_average,
    head_average,
    vector_average,
    conv_average,
    position_average,
):
    dp_index = lax.axis_index("dp")
    mp_index = lax.axis_index("mp")
    dp_count = lax.axis_size("dp")
    across, core = (dp_index // 2) % 2, dp_index % 2
    quarter = 2 * core + across
    rows = patches.shape[1]
    eighth = rows // 8
    pooled = rows // 4
    half_pool = pooled // 2
    head_cols = conv_weight.shape[2]
    width = 4 * head_cols
    sub = embed_weight.shape[1]
    patch = embed_weight.shape[0]
    classes = head_weight.shape[0]
    boxes = box_bounds.shape[2]
    own_heads = position_bias.shape[0]
    heads = own_heads * 4
    hidden_cols = up_weight.shape[1] - 3 * head_cols
    up_bits = list(range(1, dp_bits()))
    down_bits = up_bits[::-1]

    ints = jnp.concatenate(
        [clip_len.reshape(-1), box_count.reshape(-1), box_bounds.reshape(-1), box_labels.reshape(-1)]
    )
    total_ints = ints.shape[0]
    ints = jnp.pad(ints, (0, -total_ints % 1024)).reshape(-1, 128)
    ints = regroup(ints).reshape(-1)
    patches_t = regroup(patches.transpose(0, 2, 1))
    memory_t = regroup(memory.transpose(0, 1, 3, 2))
    lengths_all = ints[:5]
    counts = ints[5:8]
    bounds = ints[8 : 8 + MICRO * boxes * 2].reshape(MICRO, boxes, 2)
    labels = ints[8 + MICRO * boxes * 2 : total_ints].reshape(MICRO * boxes, classes)

    vec_hi = lax.reduce_precision(vector_weight, 8, 7)
    vec_mid = lax.reduce_precision(vector_weight - vec_hi, 8, 7)
    vec_lo = vector_weight - vec_hi - vec_mid
    small = jnp.concatenate(
        [embed_weight, head_weight, vec_hi, vec_mid, vec_lo], axis=0
    ).astype(bf16).T
    small = jnp.concatenate(gather_mp(small), axis=0)
    place = jnp.arange(4 * sub)
    small = product(
        one_hot_rows(((place // sub) ^ mp_index) * sub + place % sub, 4 * sub), small
    ).astype(bf16)
    small = jnp.concatenate(gather_dp(small, up_bits))
    embed_t = small[:, :patch]
    head_t = small[:, patch : patch + classes]
    vec3 = small[:, patch + classes :].astype(f32)
    vectors = (vec3[:, :7] + vec3[:, 7:14] + vec3[:, 14:]).T
    vectors = jnp.pad(vectors, ((0, 1), (0, 0)))

    taps_pos = jnp.concatenate(
        [
            conv_weight.reshape(12, head_cols),
            jnp.pad(position_bias.reshape(1, -1), ((0, 0), (0, head_cols - position_bias.size))),
        ]
    )
    taps_pos = gather_mp(taps_pos)
    conv_all = jnp.concatenate([t[:12] for t in taps_pos], axis=1).reshape(2, 6, width)
    rel_bias = jnp.concatenate(
        [t[12, : position_bias.size].reshape(position_bias.shape) for t in taps_pos], axis=0
    )

    up_low = up_weight.astype(bf16)
    down_low = down_weight.astype(bf16)
    pieces = gather_mp(
        jnp.concatenate([up_low[:, : 3 * head_cols], down_low[:, :head_cols]], axis=1)
    )

    def columns(first, last):
        return jnp.concatenate(
            [p[:, j * head_cols : (j + 1) * head_cols] for j in range(first, last) for p in pieces],
            axis=1,
        )

    w_qk = gather_dp(columns(0, 2), up_bits)
    w_vo = gather_dp(columns(2, 4), down_bits)
    w_back = gather_dp(jnp.concatenate(gather_mp(down_low[:, head_cols:]), axis=1), up_bits)
    w_hidden = gather_dp(jnp.concatenate(gather_mp(up_low[:, 3 * head_cols :]), axis=1), down_bits)

    place = jnp.arange(rows)
    token = 8 * (place % eighth) + 4 * ((place // eighth) % 2) + place // (2 * eighth)
    token_order = one_hot_rows(token, rows)
    mem_rows = memory.shape[2]
    half_mem = mem_rows // 2
    mem_place = jnp.arange(mem_rows)
    mem_order = one_hot_rows(2 * (mem_place % half_mem) + mem_place // half_mem, mem_rows)
    mem_two = swap_dp(memory_t, 2)
    mem_parts = (memory_t, swap_dp(memory_t, 1), mem_two, swap_dp(mem_two, 1))
    mem_full = memory_in(
        jnp.stack(
            [
                (((c ^ mp_index) // 2) ^ core) + 2 * (((c ^ mp_index) % 2) ^ across)
                for c in range(4)
            ]
        ),
        mem_order,
        mem_parts,
    )

    patches_in, embedded, normed, query, raw_keys, raw_values, pools = embed(
        patches_t, token_order, embed_t, vectors, conv_all, w_qk, w_vo
    )
    stored = [[(mem_full, 0)], [(mem_full, 1)]]
    for m in range(MICRO):
        one = swap_dp(pools[m : m + 1], 1)
        two = swap_dp(pools[m : m + 1], 2)
        three = swap_dp(two, 1)
        stored.append([(pools, m), (one, 0), (two, 0), (three, 0)])

    part_quarter = [2 * (core ^ (s % 2)) + (across ^ (s // 2)) for s in range(4)]
    pool_place = jnp.arange(pooled)
    pool_token = 2 * (pool_place % half_pool) + pool_place // half_pool
    now_index = jnp.concatenate([pq * pooled + pool_token for pq in part_quarter])
    pool_index = jnp.concatenate([pq * half_pool + jnp.arange(half_pool) for pq in part_quarter])
    mem_index = jnp.arange(half_mem)

    def key_bias(m):
        sides = [
            (now_index, lengths_all[2 + m] // 4),
            (mem_index if m == 0 else pool_index, lengths_all[1 + m] // 8),
            (mem_index if m < 2 else pool_index, lengths_all[m] // 8),
        ]
        return jnp.concatenate(
            [
                jnp.where((index < limit)[None, :], rel_bias[:, g : g + 1], -1e30)
                for g, (index, limit) in enumerate(sides)
            ],
            axis=1,
        ).reshape(heads // QUAD, QUAD, -1)

    attended, saved = None, []
    for m in range(MICRO):
        attended, probs, keys, values = attend(
            m, query, conv_all, key_bias(m), stored[m + 2], stored[m + 1], stored[m], attended
        )
        saved.append((keys, values, probs))

    position = quarter * rows + token
    within = position % FRAME
    live = position[None, :] < lengths_all[2:, None]
    inside = (
        (within[None, None, :] >= bounds[:, :, 0:1])
        & (within[None, None, :] < bounds[:, :, 1:2])
        & live[:, None, :]
    )
    denominator = ((bounds[:, :, 1] - bounds[:, :, 0]) * (lengths_all[2:, None] // FRAME)).astype(
        f32
    )
    select = inside.astype(f32) / denominator[:, :, None]
    first_res, normed_mlp, active, slope, second_res, feature = mlp(
        attended, embedded, vectors, select, w_vo, w_back, w_hidden
    )
    feature = group_sum_features(feature.reshape(MICRO * boxes, width)).astype(bf16)
    logits = product(feature, head_t)
    target = labels.astype(f32)
    keep = (jnp.arange(boxes)[None, :] < counts[:, None]).astype(f32).reshape(-1, 1)
    lead = (quarter == 0).astype(f32)
    loss_part = jnp.sum((jax.nn.softplus(logits) - target * logits) * keep) * lead
    grad_logits = ((jax.nn.sigmoid(logits) - target) * keep).astype(bf16)

    grad_head = contract_rows(feature, grad_logits) * lead
    grad_feature = contract_last(grad_logits, head_t).reshape(MICRO, boxes, width)
    grad_branch, grad_hidden, grad_attn, grad_first, grad_attended, sums = mlp_back(
        grad_feature, select, second_res, first_res, slope, vectors, w_vo, w_back, w_hidden
    )
    half = width // 2

    def weight_grad(left, right):
        return tuple(
            contract_rows(left[:, at : at + half], right).astype(bf16) for at in (0, half)
        )

    back_grad = scatter_dp(*weight_grad(grad_branch, active), down_bits)
    hidden_grad = scatter_dp(*weight_grad(normed_mlp, grad_hidden), up_bits)
    out_grad = weight_grad(grad_attn, attended)

    dq, pool_grads, bias_grad, mem_taps = None, [], 0.0, 0.0
    for m in range(MICRO):
        keys, values, probs = saved[m]
        dq, kept, sent, taps_part, bias_part = attend_back(
            m, query, keys, values, probs, grad_attended, stored[m + 1], stored[m], dq
        )
        got = swap_dp(sent, 1)
        away = (kept[:, 1].astype(f32) + got[:, 1].astype(f32)).astype(bf16)
        mine = kept[:, 0].astype(f32) + got[:, 0].astype(f32)
        pool_grads.append(mine + swap_dp(away, 2).astype(f32))
        bias_grad = bias_grad + bias_part
        mem_taps = mem_taps + taps_part
    projected_grad, embedded_grad, embed_sums, taps_grad = embed_back(
        dq,
        jnp.stack(pool_grads),
        raw_keys,
        raw_values,
        conv_all,
        embedded,
        grad_first,
        vectors,
        w_qk,
        w_vo,
    )
    qk_grad = scatter_dp(*weight_grad(normed, projected_grad[:, : 2 * width]), up_bits)
    v_grad = weight_grad(normed, projected_grad[:, 2 * width :])
    vo_grad = scatter_dp(
        *(jnp.concatenate([a, b], axis=1) for a, b in zip(v_grad, out_grad)), down_bits
    )
    grad_embed = contract_rows(embedded_grad, patches_in)
    grad_vectors = jnp.concatenate([embed_sums[:3], sums[:4]])

    small_grad = jnp.concatenate([grad_embed, grad_head, grad_vectors.T], axis=1)
    small_grad = scatter_dp(small_grad[:half], small_grad[half:], up_bits)
    small_grad = scatter_mp(
        [
            lax.dynamic_slice_in_dim(small_grad, (mp_index ^ s) * sub, sub, axis=0)
            for s in range(4)
        ]
    ).T
    embed_grad = small_grad[:patch]
    head_grad = small_grad[patch : patch + classes]
    vector_grad = small_grad[patch + classes :]

    def pieces_of(array, count):
        return [array[:, s * count : (s + 1) * count] for s in range(4)]

    back_mine = scatter_mp(pieces_of(back_grad, hidden_cols))
    hidden_mine = scatter_mp(pieces_of(hidden_grad, hidden_cols))
    attn_mine = scatter_mp(
        [
            jnp.concatenate(
                [
                    part[:, (4 * i + s) * head_cols : (4 * i + s + 1) * head_cols]
                    for part in (qk_grad, vo_grad)
                    for i in range(2)
                ],
                axis=1,
            )
            for s in range(4)
        ]
    )
    down_grad = jnp.concatenate([attn_mine[:, 3 * head_cols :], back_mine], axis=1)
    up_grad = jnp.concatenate([attn_mine[:, : 3 * head_cols], hidden_mine], axis=1)

    count_local = jnp.sum(box_count).astype(f32) * (mp_index == 0).astype(f32)
    taps_rows = jnp.stack(
        [
            jnp.concatenate([taps_grad[4 * ch : 4 * ch + 4], mem_taps[ch]], axis=0)
            for ch in range(2)
        ]
    ).reshape(12, 4, head_cols)
    scalars = jnp.stack([loss_part, count_local])
    last = jnp.concatenate(
        [
            bias_grad.reshape(heads, 128)[:, :3].reshape(4, -1),
            jnp.broadcast_to(scalars[None], (4, 2)),
        ],
        axis=1,
    )
    last = jnp.pad(last, ((0, 0), (0, head_cols - last.shape[1])))
    flat = jnp.concatenate([taps_rows, last[None]]).transpose(1, 0, 2)
    flat = sum_dp(flat)
    flat = scatter_mp([flat[s] for s in range(4)])
    conv_grad = flat[:12].reshape(2, 6, head_cols)
    position_grad = flat[12, : own_heads * 3].reshape(own_heads, 3)
    loss_global = flat[12, own_heads * 3]
    box_total = flat[12, own_heads * 3 + 1]

    reduced = (up_grad, down_grad, embed_grad, head_grad, vector_grad, conv_grad, position_grad)
    squares = sum((jnp.sum(gradient * gradient) for gradient in reduced[:5]))
    squares = squares + (
        jnp.sum(conv_grad * conv_grad) + jnp.sum(position_grad * position_grad)
    ) / dp_count
    square_total = sum_all(jnp.full((8, 128), squares, f32))[0, 0]
    grad_norm = jnp.sqrt(square_total) / box_total
    scaling = jnp.minimum(1.0, THRESHOLD / grad_norm) / box_total
    masters = (
        up_weight,
        down_weight,
        embed_weight,
        head_weight,
        vector_weight,
        conv_weight,
        position_bias,
    )
    moments = (
        up_moment,
        down_moment,
        embed_moment,
        head_moment,
        vector_moment,
        conv_moment,
        position_moment,
    )
    averages = (
        up_average,
        down_average,
        embed_average,
        head_average,
        vector_average,
        conv_average,
        position_average,
    )
    rates = (LEARNING,) * 4 + (VECTOR_LEARNING,) * 3
    results = [
        apply_update(weight, gradient * scaling, moment, average, rate)
        for weight, gradient, moment, average, rate in zip(
            masters, reduced, moments, averages, rates
        )
    ]

    target_row = jnp.arange(4 * pooled)
    target_quarter, target_rest = target_row // pooled, target_row % pooled
    source_row = (
        (((target_quarter // 2) ^ core) + 2 * ((target_quarter % 2) ^ across)) * pooled
        + (target_rest % 2) * half_pool
        + target_rest // 2
    )
    new_memory = memory_out(
        (quarter ^ mp_index)[None],
        one_hot_rows(source_row, 4 * pooled).T,
        stored[3] + stored[4],
    )
    new_memory = regroup(new_memory).transpose(0, 1, 3, 2)
    return (
        (loss_global, box_total, grad_norm, new_memory)
        + tuple(r[0] for r in results)
        + tuple(r[1] for r in results)
        + tuple(r[2] for r in results)
        + (results[0][0].astype(bf16), results[1][0].astype(bf16))
    )


def solution(mesh):
    both = ("dp", "mp")
    weight_specs = (
        P("dp", "mp"),
        P("dp", "mp"),
        P(None, both),
        P(None, both),
        P(None, both),
        P(None, None, "mp"),
        P("mp", None),
    )
    memory_spec = P(None, None, "dp", "mp")
    return jax.shard_map(
        shards,
        mesh=mesh,
        in_specs=(
            P(None, both, None),
            P("dp", None),
            P("dp", None),
            P("dp", None, None, None),
            P("dp", None, None, None),
            memory_spec,
        )
        + weight_specs * 3,
        out_specs=(P(), P(), P(), memory_spec)
        + weight_specs * 3
        + (P("dp", "mp"), P("dp", "mp")),
        check_vma=False,
    )
```

```python
import functools

import jax
import jax.numpy as jnp
from jax import lax
from jax.experimental import pallas as pl
from jax.experimental.pallas import tpu as pltpu
from jax.sharding import PartitionSpec as P

MICRO = 3
FRAME = 64
EPSILON = 1e-06
LEARNING = 300.0
VECTOR_LEARNING = 6000.0
MOMENTUM = 0.5
AVERAGING = 0.5
THRESHOLD = 0.05
PRECISE = lax.Precision.HIGHEST
QUAD = 4
bf16 = jnp.bfloat16
f32 = jnp.float32


NEAR = 60 * 1024 * 1024


def product(first_operand, second_operand):
    return jnp.dot(first_operand, second_operand, preferred_element_type=f32)


def contract_last(first_operand, second_operand):
    return lax.dot_general(
        first_operand, second_operand, (((1,), (1,)), ((), ())), preferred_element_type=f32
    )


def contract_rows(first_operand, second_operand):
    return lax.dot_general(
        first_operand, second_operand, (((0,), (0,)), ((), ())), preferred_element_type=f32
    )


def swap_dp(inputs, mask):
    size = lax.axis_size("dp")
    return lax.ppermute(inputs, "dp", [(i, i ^ mask) for i in range(size)])


def swap_mp(inputs, mask):
    size = lax.axis_size("mp")
    return lax.ppermute(inputs, "mp", [(i, i ^ mask) for i in range(size)])


def dp_bits():
    return lax.axis_size("dp").bit_length() - 1


def regroup(inputs):
    count = lax.axis_size("dp")
    pairs = []
    for d in range(count):
        for z in range(4):
            moved = (d % 2) ^ (z // 2)
            pairs.append((d * 4 + z, (d ^ moved) * 4 + (z ^ (2 * moved))))
    return lax.ppermute(inputs, ("dp", "mp"), pairs)


def pick(pieces):
    odd = lax.axis_index("mp") % 2 == 1
    return [jnp.where(odd, pieces[c ^ 1], pieces[c]) for c in range(4)]


def gather_mp(inputs):
    return [inputs] + [swap_mp(inputs, s) for s in (1, 2, 3)]


def trade_mp(pieces):
    return (pieces[0],) + tuple(swap_mp(pieces[s], s) for s in (1, 2, 3))


def scatter_mp(pieces):
    return sum(p.astype(f32) for p in trade_mp(pieces))


def spread_dp(inputs):
    return [inputs] + [swap_dp(inputs, b) for b in range(2, lax.axis_size("dp"), 2)]


def spread_core(pieces):
    pieces = pieces + [swap_dp(p, 1) for p in pieces]
    if pieces[0].shape[0] % 16:
        pieces = [jnp.concatenate(pieces)]
    return tuple(pieces)


def halve_dp(near, far):
    got = [swap_dp(f, 1) for f in far]
    count = lax.axis_size("dp") // 2
    rows = near[0].shape[0] // count
    return [
        jnp.concatenate(
            [
                n[i * rows : (i + 1) * rows].astype(f32) + g[i * rows : (i + 1) * rows].astype(f32)
                for n, g in zip(near, got)
            ],
            axis=1,
        ).astype(bf16)
        for i in range(count)
    ]


def collect_dp(pieces):
    total = pieces[0].astype(f32)
    for i, piece in enumerate(pieces[1:]):
        total = total + swap_dp(piece, 2 * i + 2).astype(f32)
    return total


def after(value, *events):
    return lax.optimization_barrier((value,) + events)[0]


def sum_dp(inputs):
    for bit in range(dp_bits()):
        inputs = inputs + swap_dp(inputs, 1 << bit)
    return inputs


def group_sum_features(inputs):
    count = lax.axis_size("dp")
    width = inputs.shape[1] // count
    order = [b for b in range(count) if b % 2 == 0] + [b for b in range(count) if b % 2]
    at = [order.index(b ^ 1) for b in order]
    got = swap_dp(inputs, 1)
    inputs = inputs + jnp.concatenate([got[:, p * width : (p + 1) * width] for p in at], axis=1)
    return inputs + swap_mp(inputs, 1)


def call(
    body, grid, in_specs, out_specs, out_shape, operands, flops, scratch=(), alias=None, events=()
):
    moved = sum(o.size * o.dtype.itemsize for o in operands)
    known, late = len(operands), len(operands) + len(events)

    def run(*refs):
        body(*refs[:known], *refs[late:])

    return pl.pallas_call(
        run,
        grid=grid,
        in_specs=list(in_specs) + [pl.BlockSpec(memory_space=pl.ANY)] * len(events),
        out_specs=out_specs,
        out_shape=out_shape,
        scratch_shapes=list(scratch),
        input_output_aliases=alias or {},
        compiler_params=pltpu.CompilerParams(vmem_limit_bytes=NEAR),
        cost_estimate=pl.CostEstimate(flops=1000, bytes_accessed=1000, transcendentals=0),
    )(*operands, *events)


def whole(array):
    return pl.BlockSpec(array.shape, lambda *i, n=array.ndim: (0,) * n)


def fetch(pieces, targets, sems):
    copies, at = [], 0
    for piece in pieces:
        rows = piece.shape[0]
        for column, target in targets:
            copies.append(
                pltpu.make_async_copy(
                    piece.at[:, column : column + target.shape[1]],
                    target.at[at : at + rows],
                    sems.at[len(copies)],
                )
            )
        at += rows
    for copy in copies:
        copy.start()
    for copy in copies:
        copy.wait()


def standard(inputs):
    centered = inputs - jnp.mean(inputs, axis=-1, keepdims=True)
    scale = lax.rsqrt(jnp.mean(centered * centered, axis=-1, keepdims=True) + EPSILON)
    return centered * scale, scale


def standard_back(grad, unit, scale):
    return scale * (
        grad
        - jnp.mean(grad, axis=-1, keepdims=True)
        - unit * jnp.mean(grad * unit, axis=-1, keepdims=True)
    )


def memory_in_kernel(index_ref, order_ref, one_ref, two_ref, three_ref, four_ref, out_ref):
    parts = [r[0, 0] for r in (one_ref, two_ref, three_ref, four_ref)]
    blocks = []
    for c in range(4):
        s = index_ref[c]
        chosen = parts[3]
        for p in (2, 1, 0):
            chosen = jnp.where(s == p, parts[p], chosen)
        blocks.append(chosen)
    out_ref[0, 0] = contract_last(order_ref[...], jnp.concatenate(blocks)).astype(bf16)


def memory_in(index, order, parts):
    _, _, columns, rows = parts[0].shape
    return call(
        memory_in_kernel,
        (2, 2),
        [pl.BlockSpec(memory_space=pltpu.SMEM), pl.BlockSpec((rows, rows), lambda i, j: (0, 0))]
        + [pl.BlockSpec((1, 1, columns, rows), lambda i, j: (i, j, 0, 0))] * 4,
        pl.BlockSpec((1, 1, rows, 4 * columns), lambda i, j: (i, j, 0, 0)),
        jax.ShapeDtypeStruct((2, 2, rows, 4 * columns), bf16),
        (index, order) + tuple(parts),
        8 * rows * rows * 4 * columns,
    )


def memory_out_kernel(index_ref, order_ref, *refs):
    out_ref = refs[-1]
    chosen = index_ref[0]
    for m in range(2):
        rows = jnp.concatenate([r[0, 0] for r in refs[4 * m : 4 * m + 4]])
        turned = contract_rows(rows, order_ref[...]).astype(bf16)
        columns = turned.shape[0] // 4
        blocks = [turned[c * columns : (c + 1) * columns] for c in range(4)]
        block = blocks[3]
        for c in (2, 1, 0):
            block = jnp.where(chosen == c, blocks[c], block)
        out_ref[m, 0] = block


def memory_out(index, order, parts):
    _, _, rows, width = parts[0][0].shape
    return call(
        memory_out_kernel,
        (2,),
        [
            pl.BlockSpec(memory_space=pltpu.SMEM),
            pl.BlockSpec((4 * rows, 4 * rows), lambda i: (0, 0)),
        ]
        + [pl.BlockSpec((1, 1, rows, width), lambda i, m=m: (m, i, 0, 0)) for _, m in parts],
        pl.BlockSpec((2, 1, width // 4, 4 * rows), lambda i: (0, i, 0, 0)),
        jax.ShapeDtypeStruct((2, 2, width // 4, 4 * rows), bf16),
        (index, order) + tuple(a for a, _ in parts),
        8 * (4 * rows) ** 2 * width,
    )


def embed_kernel(count, patch_ref, order_ref, taps_ref, *refs):
    pieces = refs[:count]
    (
        sorted_ref, embedded_ref, normed_ref, query_ref, key_ref, value_ref, pool_ref,
        vec_ref, head_ref, qk_s, v_s, small_s, sems,
    ) = refs[count:]
    width = embedded_ref.shape[1]
    edge = small_s.shape[1] - 128

    @pl.when(pl.program_id(0) == 0)
    def _():
        fetch(pieces, ((0, qk_s), (2 * width, v_s), (3 * width, small_s)), sems)
        turned = small_s[:, edge:].astype(f32).T
        vec_ref[...] = turned[0:8] + turned[8:16] + turned[16:24]
        head_ref[...] = turned[24 : 24 + head_ref.shape[0]].astype(bf16)

    patch = contract_last(order_ref[...], patch_ref[0]).astype(bf16)
    sorted_ref[...] = patch
    embedded = contract_last(patch, small_s[:, : patch.shape[1]]) + vec_ref[0:1]
    embedded_ref[...] = embedded
    unit, _ = standard(embedded)
    normed = (unit * vec_ref[1:2] + vec_ref[2:3]).astype(bf16)
    normed_ref[...] = normed
    query_ref[...] = product(normed, qk_s[:, :width]).astype(bf16)
    for ch, weight, raw_ref in ((0, qk_s[:, width:], key_ref), (1, v_s[...], value_ref)):
        raw = product(normed, weight)
        raw_ref[...] = raw.astype(bf16)
        rows = raw.shape[0] // 4
        pooled = raw[:rows] * taps_ref[ch, 0:1]
        for t in range(1, 4):
            pooled = pooled + raw[t * rows : (t + 1) * rows] * taps_ref[ch, t : t + 1]
        pool_ref[0, ch] = pooled.astype(bf16)


def embed(patches_t, order, taps, weights, classes, events=()):
    _, patch, rows = patches_t.shape
    width = taps.shape[2]
    total = MICRO * rows
    edge = weights[0].shape[1] - 3 * width

    def tile(columns):
        return pl.BlockSpec((rows, columns), lambda i: (i, 0))

    return call(
        functools.partial(embed_kernel, len(weights)),
        (MICRO,),
        [pl.BlockSpec((1, patch, rows), lambda i: (i, 0, 0)), whole(order), whole(taps)]
        + [pl.BlockSpec(memory_space=pl.ANY)] * len(weights),
        [tile(patch), tile(width), tile(width), tile(width), tile(width), tile(width)]
        + [
            pl.BlockSpec((1, 2, rows // 4, width), lambda i: (i, 0, 0, 0)),
            pl.BlockSpec((8, width), lambda i: (0, 0)),
            pl.BlockSpec((classes, width), lambda i: (0, 0)),
        ],
        [
            jax.ShapeDtypeStruct((total, patch), bf16),
            jax.ShapeDtypeStruct((total, width), f32),
        ]
        + [jax.ShapeDtypeStruct((total, width), bf16)] * 4
        + [
            jax.ShapeDtypeStruct((MICRO, 2, rows // 4, width), bf16),
            jax.ShapeDtypeStruct((8, width), f32),
            jax.ShapeDtypeStruct((classes, width), bf16),
        ],
        (patches_t, order, taps) + weights,
        2 * total * width * (patch + 3 * width),
        scratch=[
            pltpu.VMEM((width, 2 * width), bf16),
            pltpu.VMEM((width, width), bf16),
            pltpu.VMEM((width, edge), bf16),
            pltpu.SemaphoreType.DMA((3 * len(weights),)),
        ],
        events=events,
    )


def attend_kernel(sources, q_ref, taps_ref, bias_ref, *refs):
    count = sum(sources)
    now, newer = refs[: sources[0]], refs[sources[0] : sources[0] + sources[1]]
    older = refs[sources[0] + sources[1] : count]
    out_ref, prob_ref, key_ref, value_ref = refs[-4:]
    query = q_ref[...]
    rows, width = query.shape
    size = width // QUAD
    for ch, target in ((0, key_ref), (1, value_ref)):
        at = 0
        for r in now:
            n = r.shape[2]
            target[at : at + n] = r[0, ch]
            at += n
        first, second = taps_ref[ch, 4:5], taps_ref[ch, 5:6]
        for r in newer + older:
            n = r.shape[2] // 2
            target[at : at + n] = (
                r[0, ch, :n].astype(f32) * first + r[0, ch, n:].astype(f32) * second
            ).astype(bf16)
            at += n
    keys_t = key_ref[...].T
    values = value_ref[...]
    lane = lax.broadcasted_iota(jnp.int32, (rows, width), 1) // size
    scaled = query * (size**-0.5)
    total = query.astype(f32)
    for h in range(QUAD):
        own = jnp.where(lane == h, scaled, jnp.zeros_like(scaled))
        scores = product(own, keys_t) + bias_ref[0, h : h + 1, :]
        top = jnp.max(scores, axis=-1, keepdims=True)
        exponent = jnp.exp(scores - top)
        denominator = jnp.sum(exponent, axis=-1, keepdims=True)
        probs = (exponent * (1.0 / denominator)).astype(bf16)
        prob_ref[h] = probs
        total = total + jnp.where(lane == h, product(probs, values), 0.0)
    out_ref[...] = total.astype(bf16)


def source_specs(entries, block):
    return [
        pl.BlockSpec((1, 2, a.shape[2], block), lambda i, m=m: (m, 0, 0, i)) for a, m in entries
    ]


def attend(micro, query, taps, bias, now, newer, older, before, events=()):
    rows = query.shape[0] // MICRO
    width = query.shape[1]
    count = bias.shape[2]
    quads = bias.shape[0]
    block = width // quads
    entries = now + newer + older
    operands = (query, taps, bias) + tuple(a for a, _ in entries)
    specs = [
        pl.BlockSpec((rows, block), lambda i: (micro, i)),
        pl.BlockSpec((2, 6, block), lambda i: (0, 0, i)),
        pl.BlockSpec((1, QUAD, count), lambda i: (i, 0, 0)),
    ] + source_specs(entries, block)
    alias = {}
    if before is not None:
        alias = {len(operands): 0}
        operands = operands + (before,)
        specs.append(pl.BlockSpec(memory_space=pl.ANY))
    return call(
        functools.partial(attend_kernel, (len(now), len(newer), len(older))),
        (quads,),
        specs,
        [
            pl.BlockSpec((rows, block), lambda i: (micro, i)),
            pl.BlockSpec((QUAD, rows, count), lambda i: (i, 0, 0)),
            pl.BlockSpec((count, block), lambda i: (0, i)),
            pl.BlockSpec((count, block), lambda i: (0, i)),
        ],
        [
            jax.ShapeDtypeStruct(query.shape, bf16),
            jax.ShapeDtypeStruct((quads * QUAD, rows, count), bf16),
            jax.ShapeDtypeStruct((count, width), bf16),
            jax.ShapeDtypeStruct((count, width), bf16),
        ],
        operands,
        4 * rows * count * width * 4,
        alias=alias,
        events=events,
    )


def attend_back_kernel(sources, q_ref, k_ref, v_ref, prob_ref, grad_ref, *refs):
    entries = refs[: sum(sources)]
    dq_ref, keep_ref, send_ref, taps_ref, bias_ref = refs[-5:]
    query = q_ref[...]
    grad = grad_ref[...]
    rows, width = query.shape
    size = width // QUAD
    keys = k_ref[...]
    count = keys.shape[0]
    values_t = v_ref[...].T
    query_t = query.T
    grad_t = grad.T
    scaling = size**-0.5
    lane = lax.broadcasted_iota(jnp.int32, (rows, width), 1) // size
    total = jnp.zeros((rows, width), f32)
    ones = jnp.ones((16, rows), bf16)
    half = count // 2
    spot = lax.broadcasted_iota(jnp.int32, (1, 128), 1)
    key_parts, value_parts = [], []
    for h in range(QUAD):
        own = jnp.where(lane == h, grad, jnp.zeros_like(grad))
        probs_low = prob_ref[h]
        probs = probs_low.astype(f32)
        pulled = probs * product(own, values_t)
        shift = jnp.sum(pulled, axis=-1, keepdims=True)
        score_grad = (pulled - probs * shift).astype(bf16)
        total = total + jnp.where(lane == h, product(score_grad, keys), 0.0)
        left = jnp.concatenate([query_t[h * size : (h + 1) * size], ones])
        found = product(left, score_grad)
        key_parts.append(found[:size])
        sums = found[size : size + 1]
        row = jnp.zeros((1, 128), f32)
        for g, (a, b) in enumerate(((0, half), (half, half + half // 2), (half + half // 2, count))):
            row = row + jnp.where(spot == g, jnp.sum(sums[:, a:b], axis=1, keepdims=True), 0.0)
        bias_ref[0, h : h + 1, :] = row
        value_parts.append(product(grad_t[h * size : (h + 1) * size], probs_low))
    dq_ref[...] = (total * scaling + grad.astype(f32)).astype(bf16)
    part = keep_ref.shape[2]
    for ch, parts, factor in ((0, key_parts, scaling), (1, value_parts, 1.0)):
        found = jnp.concatenate(parts).T * factor
        for s in range(4):
            target = send_ref if s % 2 else keep_ref
            target[ch, s // 2] = found[s * part : (s + 1) * part].astype(bf16)
        at = half
        first = jnp.zeros((1, width), f32)
        second = jnp.zeros((1, width), f32)
        for r in entries:
            n = r.shape[2] // 2
            piece = found[at : at + n]
            first = first + jnp.sum(piece * r[0, ch, :n].astype(f32), axis=0, keepdims=True)
            second = second + jnp.sum(piece * r[0, ch, n:].astype(f32), axis=0, keepdims=True)
            at += n
        taps_ref[ch, 0:1] = first
        taps_ref[ch, 1:2] = second


def attend_back(micro, query, keys, values, probs, grad, newer, older, before, events=()):
    heads, rows, count = probs.shape
    width = query.shape[1]
    quads = heads // QUAD
    block = width // quads
    entries = newer + older
    operands = (query, keys, values, probs, grad) + tuple(a for a, _ in entries)
    specs = [
        pl.BlockSpec((rows, block), lambda i: (micro, i)),
        pl.BlockSpec((count, block), lambda i: (0, i)),
        pl.BlockSpec((count, block), lambda i: (0, i)),
        pl.BlockSpec((QUAD, rows, count), lambda i: (i, 0, 0)),
        pl.BlockSpec((rows, block), lambda i: (micro, i)),
    ] + source_specs(entries, block)
    alias = {}
    if before is not None:
        alias = {len(operands): 0}
        operands = operands + (before,)
        specs.append(pl.BlockSpec(memory_space=pl.ANY))
    part = count // 8
    return call(
        functools.partial(attend_back_kernel, (len(newer), len(older))),
        (quads,),
        specs,
        [
            pl.BlockSpec((rows, block), lambda i: (micro, i)),
            pl.BlockSpec((2, 2, part, block), lambda i: (0, 0, 0, i)),
            pl.BlockSpec((2, 2, part, block), lambda i: (0, 0, 0, i)),
            pl.BlockSpec((2, 2, block), lambda i: (0, 0, i)),
            pl.BlockSpec((1, QUAD, 128), lambda i: (i, 0, 0)),
        ],
        [
            jax.ShapeDtypeStruct(query.shape, bf16),
            jax.ShapeDtypeStruct((2, 2, part, width), bf16),
            jax.ShapeDtypeStruct((2, 2, part, width), bf16),
            jax.ShapeDtypeStruct((2, 2, width), f32),
            jax.ShapeDtypeStruct((quads, QUAD, 128), f32),
        ],
        operands,
        8 * rows * count * width * 4,
        alias=alias,
        events=events,
    )


def gelu_pair(inputs):
    size = jnp.abs(inputs)
    t = 1.0 / (1.0 + (0.3275911 * 0.5**0.5) * size)
    bell = jnp.exp(-0.5 * inputs * inputs)
    tail = (
        t
        * (
            0.5 * 0.254829592
            + t
            * (
                0.5 * -0.284496736
                + t * (0.5 * 1.421413741 + t * (0.5 * -1.453152027 + t * (0.5 * 1.061405429)))
            )
        )
        * bell
    )
    share = jnp.where(inputs > 0.0, 1.0 - tail, tail)
    return inputs * share, share + inputs * bell * 0.3989422804014327


def mlp_weights(width, units, count):
    return [
        pltpu.VMEM((width, width), bf16),
        pltpu.VMEM((width, units), bf16),
        pltpu.VMEM((width, units), bf16),
        pltpu.SemaphoreType.DMA((3 * count,)),
    ]


def mlp_kernel(count, attended_ref, embedded_ref, vec_ref, select_ref, *refs):
    (
        first_ref, normed_ref, active_ref, slope_ref, second_ref, feature_ref,
        wo_s, wb_s, wh_s, sems,
    ) = refs[count:]
    width = embedded_ref.shape[1]

    @pl.when(pl.program_id(0) == 0)
    def _():
        units = wb_s.shape[1]
        fetch(refs[:count], ((0, wb_s), (units, wh_s), (2 * units, wo_s)), sems)

    first = embedded_ref[...] + contract_last(attended_ref[...], wo_s[...])
    first_ref[...] = first
    unit, _ = standard(first)
    normed = (unit * vec_ref[3:4] + vec_ref[4:5]).astype(bf16)
    normed_ref[...] = normed
    total = first
    chunk = 512
    for at in range(0, wh_s.shape[1], chunk):
        hidden = product(normed, wh_s[:, at : at + chunk])
        value, slope = gelu_pair(hidden)
        value = value.astype(bf16)
        active_ref[:, at : at + chunk] = value
        slope_ref[:, at : at + chunk] = slope.astype(bf16)
        total = total + contract_last(value, wb_s[:, at : at + chunk])
    second_ref[...] = total
    unit, _ = standard(total)
    final = unit * vec_ref[5:6] + vec_ref[6:7]
    feature_ref[0] = jnp.dot(
        select_ref[0], final, precision=PRECISE, preferred_element_type=f32
    )


def mlp(attended, embedded, vec, select, weights, events=()):
    total, width = embedded.shape
    rows = total // MICRO
    units = (weights[0].shape[1] - width) // 2
    boxes = select.shape[1]

    def tile(columns):
        return pl.BlockSpec((rows, columns), lambda i: (i, 0))

    return call(
        functools.partial(mlp_kernel, len(weights)),
        (MICRO,),
        [
            tile(width),
            tile(width),
            whole(vec),
            pl.BlockSpec((1, boxes, rows), lambda i: (i, 0, 0)),
        ]
        + [pl.BlockSpec(memory_space=pl.ANY)] * len(weights),
        [tile(width), tile(width), tile(units), tile(units), tile(width)]
        + [pl.BlockSpec((1, boxes, width), lambda i: (i, 0, 0))],
        [
            jax.ShapeDtypeStruct((total, width), f32),
            jax.ShapeDtypeStruct((total, width), bf16),
            jax.ShapeDtypeStruct((total, units), bf16),
            jax.ShapeDtypeStruct((total, units), bf16),
            jax.ShapeDtypeStruct((total, width), f32),
            jax.ShapeDtypeStruct((MICRO, boxes, width), f32),
        ],
        (attended, embedded, vec, select) + weights,
        2 * total * width * (width + 2 * units),
        scratch=mlp_weights(width, units, len(weights)),
        events=events,
    )


def mlp_back_kernel(
    count, pull_ref, select_ref, second_ref, first_ref, slope_ref, vec_ref, *refs
):
    (
        branch_ref, hidden_ref, attn_ref, first_grad_ref, attended_ref, sums_ref,
        wo_s, wb_s, wh_s, sems,
    ) = refs[count:]
    width = second_ref.shape[1]

    @pl.when(pl.program_id(0) == 0)
    def _():
        sums_ref[...] = jnp.zeros_like(sums_ref)
        units = wb_s.shape[1]
        fetch(refs[:count], ((0, wb_s), (units, wh_s), (2 * units, wo_s)), sems)

    pull = lax.dot_general(
        select_ref[0],
        pull_ref[0],
        (((0,), (0,)), ((), ())),
        precision=PRECISE,
        preferred_element_type=f32,
    )
    unit, scale = standard(second_ref[...])
    sums_ref[2:3] += jnp.sum(pull * unit, axis=0, keepdims=True)
    sums_ref[3:4] += jnp.sum(pull, axis=0, keepdims=True)
    second_grad = standard_back(pull * vec_ref[5:6], unit, scale)
    branch = second_grad.astype(bf16)
    branch_ref[...] = branch
    chunk = 512
    normed_grad = jnp.zeros(second_grad.shape, f32)
    for at in range(0, wh_s.shape[1], chunk):
        active_grad = product(branch, wb_s[:, at : at + chunk])
        hidden_grad = (active_grad * slope_ref[:, at : at + chunk].astype(f32)).astype(bf16)
        hidden_ref[:, at : at + chunk] = hidden_grad
        normed_grad = normed_grad + contract_last(hidden_grad, wh_s[:, at : at + chunk])
    unit, scale = standard(first_ref[...])
    sums_ref[0:1] += jnp.sum(normed_grad * unit, axis=0, keepdims=True)
    sums_ref[1:2] += jnp.sum(normed_grad, axis=0, keepdims=True)
    first_grad = standard_back(normed_grad * vec_ref[3:4], unit, scale) + second_grad
    first_grad_ref[...] = first_grad
    attn = first_grad.astype(bf16)
    attn_ref[...] = attn
    attended_ref[...] = product(attn, wo_s[...]).astype(bf16)


def mlp_back(pull, select, second, first, slope, vec, weights, events=()):
    total, width = second.shape
    rows = total // MICRO
    units = (weights[0].shape[1] - width) // 2
    boxes = select.shape[1]

    def tile(columns):
        return pl.BlockSpec((rows, columns), lambda i: (i, 0))

    return call(
        functools.partial(mlp_back_kernel, len(weights)),
        (MICRO,),
        [
            pl.BlockSpec((1, boxes, width), lambda i: (i, 0, 0)),
            pl.BlockSpec((1, boxes, rows), lambda i: (i, 0, 0)),
            tile(width),
            tile(width),
            tile(units),
            whole(vec),
        ]
        + [pl.BlockSpec(memory_space=pl.ANY)] * len(weights),
        [tile(width), tile(units), tile(width), tile(width), tile(width)]
        + [pl.BlockSpec((8, width), lambda i: (0, 0))],
        [
            jax.ShapeDtypeStruct((total, width), bf16),
            jax.ShapeDtypeStruct((total, units), bf16),
            jax.ShapeDtypeStruct((total, width), bf16),
            jax.ShapeDtypeStruct((total, width), f32),
            jax.ShapeDtypeStruct((total, width), bf16),
            jax.ShapeDtypeStruct((8, width), f32),
        ],
        (pull, select, second, first, slope, vec) + weights,
        2 * total * width * (width + 2 * units),
        scratch=mlp_weights(width, units, len(weights)),
        events=events,
    )


def embed_back_kernel(
    count, dq_ref, pool_ref, key_ref, value_ref, taps_ref, embedded_ref, first_ref, vec_ref, *refs
):
    projected_ref, grad_ref, sums_ref, taps_out, qk_s, v_s, sems = refs[count:]
    width = embedded_ref.shape[1]

    @pl.when(pl.program_id(0) == 0)
    def _():
        sums_ref[...] = jnp.zeros_like(sums_ref)
        taps_out[...] = jnp.zeros_like(taps_out)
        fetch(refs[:count], ((0, qk_s), (2 * width, v_s)), sems)

    projected_ref[:, :width] = dq_ref[...]
    rows = pool_ref.shape[2]
    for ch, raw_ref in ((0, key_ref), (1, value_ref)):
        pool = pool_ref[0, ch]
        for t in range(4):
            projected_ref[t * rows : (t + 1) * rows, (1 + ch) * width : (2 + ch) * width] = (
                pool * taps_ref[ch, t : t + 1]
            ).astype(bf16)
            raw = raw_ref[t * rows : (t + 1) * rows].astype(f32)
            taps_out[4 * ch + t : 4 * ch + t + 1] += jnp.sum(pool * raw, axis=0, keepdims=True)
    normed_grad = contract_last(projected_ref[:, : 2 * width], qk_s[...])
    normed_grad = normed_grad + contract_last(projected_ref[:, 2 * width :], v_s[...])
    unit, scale = standard(embedded_ref[...])
    sums_ref[1:2] += jnp.sum(normed_grad * unit, axis=0, keepdims=True)
    sums_ref[2:3] += jnp.sum(normed_grad, axis=0, keepdims=True)
    grad = standard_back(normed_grad * vec_ref[1:2], unit, scale) + first_ref[...]
    grad = grad.astype(bf16)
    grad_ref[...] = grad
    sums_ref[0:1] += jnp.sum(grad.astype(f32), axis=0, keepdims=True)


def embed_back(dq, pool, keys, values, taps, embedded, first_grad, vec, weights, events=()):
    total, width = embedded.shape
    rows = total // MICRO

    def tile(columns):
        return pl.BlockSpec((rows, columns), lambda i: (i, 0))

    return call(
        functools.partial(embed_back_kernel, len(weights)),
        (MICRO,),
        [
            tile(width),
            pl.BlockSpec((1, 2, rows // 4, width), lambda i: (i, 0, 0, 0)),
            tile(width),
            tile(width),
            whole(taps),
            tile(width),
            tile(width),
            whole(vec),
        ]
        + [pl.BlockSpec(memory_space=pl.ANY)] * len(weights),
        [
            tile(3 * width),
            tile(width),
            pl.BlockSpec((8, width), lambda i: (0, 0)),
            pl.BlockSpec((8, width), lambda i: (0, 0)),
        ],
        [
            jax.ShapeDtypeStruct((total, 3 * width), bf16),
            jax.ShapeDtypeStruct((total, width), bf16),
            jax.ShapeDtypeStruct((8, width), f32),
            jax.ShapeDtypeStruct((8, width), f32),
        ],
        (dq, pool, keys, values, taps, embedded, first_grad, vec) + weights,
        2 * total * width * 3 * width,
        scratch=[
            pltpu.VMEM((width, 2 * width), bf16),
            pltpu.VMEM((width, width), bf16),
            pltpu.SemaphoreType.DMA((2 * len(weights),)),
        ],
        events=events,
    )


def squares_kernel(count, *refs):
    grads = refs[:count]
    names = refs[count:]
    rest_ref, share_ref, place_ref = names[:3]
    attn_out, small_out, total_out = names[3:]
    attn = grads[0][...].astype(f32)
    small = grads[count // 2][...].astype(f32)
    for i in range(1, count // 2):
        attn = attn + grads[i][...].astype(f32)
        small = small + grads[count // 2 + i][...].astype(f32)
    attn_out[...] = attn
    small_out[...] = small
    share = share_ref[...] * place_ref[...]
    total = (
        jnp.sum(attn * attn)
        + jnp.sum(small * small)
        + jnp.sum(rest_ref[...] * rest_ref[...])
        + jnp.sum(share * share_ref[...])
    )
    total_out[...] = jnp.zeros_like(total_out) + total


def squares_of(attn, small, rest, share, place):
    operands = attn + small + (rest, share, place)
    return call(
        functools.partial(squares_kernel, len(attn) + len(small)),
        (1,),
        [whole(o) for o in operands],
        [whole(attn[0]), whole(small[0]), pl.BlockSpec((8, 128), lambda i: (0, 0))],
        [
            jax.ShapeDtypeStruct(attn[0].shape, f32),
            jax.ShapeDtypeStruct(small[0].shape, f32),
            jax.ShapeDtypeStruct((8, 128), f32),
        ],
        operands,
        0,
    )


def update_kernel(rates, one_ref, two_ref, boxes_ref, *refs):
    count = len(rates)
    grads, weights, moments, averages = (refs[i * count : (i + 1) * count] for i in range(4))
    outs = refs[4 * count :]
    boxes = boxes_ref[0:1, 0:1]
    norm = jnp.sqrt(one_ref[0:1, 0:1] + two_ref[0:1, 0:1]) / boxes
    outs[0][...] = norm
    scaling = jnp.minimum(1.0, THRESHOLD / norm) / boxes
    for i, rate in enumerate(rates):
        factor = scaling if weights[i].ndim == 2 else scaling[None]
        grad = grads[i][...] * factor
        moment = MOMENTUM * moments[i][...] + grad
        updated = weights[i][...] - rate * (grad + MOMENTUM * moment)
        outs[1 + i][...] = updated
        outs[1 + count + i][...] = moment
        outs[1 + 2 * count + i][...] = AVERAGING * averages[i][...] + (1.0 - AVERAGING) * updated
        if i < 2:
            outs[1 + 3 * count + i][...] = updated.astype(bf16)


def update(one, two, boxes, grads, weights, moments, averages, rates):
    operands = (one, two, boxes) + grads + weights + moments + averages
    kept = [jax.ShapeDtypeStruct(w.shape, f32) for w in weights]
    shapes = [jax.ShapeDtypeStruct((1, 1), f32)] + kept * 3
    shapes = shapes + [jax.ShapeDtypeStruct(w.shape, bf16) for w in weights[:2]]
    return call(
        functools.partial(update_kernel, rates),
        (1,),
        [whole(o) for o in operands],
        [pl.BlockSpec(o.shape, lambda i, n=len(o.shape): (0,) * n) for o in shapes],
        shapes,
        operands,
        0,
    )


def one_hot_rows(index, count):
    return (index[:, None] == jnp.arange(count)[None, :]).astype(bf16)


def shards(
    patches,
    clip_len,
    box_count,
    box_bounds,
    box_labels,
    memory,
    up_weight,
    down_weight,
    embed_weight,
    head_weight,
    vector_weight,
    conv_weight,
    position_bias,
    up_moment,
    down_moment,
    embed_moment,
    head_moment,
    vector_moment,
    conv_moment,
    position_moment,
    up_average,
    down_average,
    embed_average,
    head_average,
    vector_average,
    conv_average,
    position_average,
):
    dp_index = lax.axis_index("dp")
    mp_index = lax.axis_index("mp")
    dp_count = lax.axis_size("dp")
    across, core = mp_index % 2, dp_index % 2
    upper = mp_index - across
    quarter = 2 * core + across
    rows = patches.shape[1]
    eighth = rows // 8
    pooled = rows // 4
    half_pool = pooled // 2
    head_cols = conv_weight.shape[2]
    width = 4 * head_cols
    sub = embed_weight.shape[1]
    patch = embed_weight.shape[0]
    classes = head_weight.shape[0]
    boxes = box_bounds.shape[2]
    own_heads = position_bias.shape[0]
    heads = own_heads * 4
    hidden_cols = up_weight.shape[1] - 3 * head_cols

    ints = jnp.concatenate(
        [clip_len.reshape(-1), box_count.reshape(-1), box_bounds.reshape(-1), box_labels.reshape(-1)]
    )
    total_ints = ints.shape[0]
    ints = jnp.pad(ints, (0, -total_ints % 1024)).reshape(-1, 128)
    ints = regroup(ints).reshape(-1)
    lengths_all = ints[:5]
    counts = ints[5:8]
    bounds = ints[8 : 8 + MICRO * boxes * 2].reshape(MICRO, boxes, 2)
    labels = ints[8 + MICRO * boxes * 2 : total_ints].reshape(MICRO * boxes, classes)

    def in_three(array):
        high = lax.reduce_precision(array, 8, 7)
        middle = lax.reduce_precision(array - high, 8, 7)
        return [high, middle, array - high - middle]

    edge = patch + (-patch % 128)
    columns_in = [jnp.pad(embed_weight, ((0, edge - patch), (0, 0)))]
    columns_in += [jnp.pad(v, ((0, 1), (0, 0))) for v in in_three(vector_weight)]
    columns_in += [jnp.pad(head_weight, ((0, 128 - 24 - classes), (0, 0)))]
    taps_pos = jnp.concatenate(
        [
            conv_weight.reshape(12, head_cols),
            jnp.pad(position_bias.reshape(1, -1), ((0, 0), (0, head_cols - position_bias.size))),
        ]
    )
    taps_pos = jnp.concatenate(in_three(taps_pos)).reshape(sub, -1)
    small = jnp.concatenate([jnp.concatenate(columns_in).T, taps_pos], axis=1).astype(bf16)
    up_low = up_weight.astype(bf16)
    down_low = down_weight.astype(bf16)
    pieces = gather_mp(up_low[:, : 3 * head_cols])
    small = gather_mp(small)
    place = jnp.arange(4 * sub)
    small_mine = product(
        one_hot_rows(((place // sub) ^ mp_index) * sub + place % sub, 4 * sub),
        jnp.concatenate([p[:, : edge + 128] for p in small]),
    ).astype(bf16)
    taps_pos = jnp.stack(pick([p[:, edge + 128 :] for p in small])).reshape(4, 3, 13, head_cols)
    taps_pos = jnp.sum(taps_pos.astype(f32), axis=1)
    conv_all = taps_pos[:, :12].transpose(1, 0, 2).reshape(2, 6, width)
    rel_bias = taps_pos[:, 12, : position_bias.size].reshape(heads, 3)
    weights = jnp.concatenate(
        [p[:, j * head_cols : (j + 1) * head_cols] for j in range(3) for p in pick(pieces)]
        + [small_mine],
        axis=1,
    )
    weights = spread_core(spread_dp(weights))
    q_pieces = pieces
    pieces = gather_mp(
        after(
            jnp.concatenate([down_low, up_low[:, 3 * head_cols :]], axis=1), *pieces, *small
        )
    )
    patches_t = regroup(after(patches.transpose(0, 2, 1), *q_pieces, *small))
    pieces = [after(p, *weights, patches_t) for p in pieces]
    edges = (head_cols, head_cols + hidden_cols, head_cols + 2 * hidden_cols)
    rest = spread_dp(
        jnp.concatenate(
            [p[:, edges[0] : edges[1]] for p in pieces]
            + [p[:, edges[1] :] for p in pieces]
            + pick([p[:, : edges[0]] for p in pieces]),
            axis=1,
        )
    )

    place = jnp.arange(rows)
    token = 8 * (place % eighth) + 4 * ((place // eighth) % 2) + place // (2 * eighth)
    token_order = one_hot_rows(token, rows)
    mem_rows = memory.shape[2]
    half_mem = mem_rows // 2
    mem_place = jnp.arange(mem_rows)
    mem_order = one_hot_rows(2 * (mem_place % half_mem) + mem_place // half_mem, mem_rows)
    (
        patches_in,
        embedded,
        normed,
        query,
        raw_keys,
        raw_values,
        pools,
        vectors,
        head_low,
    ) = embed(patches_t, token_order, conv_all, weights, classes)
    stored = []
    for m in range(MICRO):
        one = swap_dp(pools[m : m + 1], 1)
        two = swap_mp(pools[m : m + 1], 1)
        three = swap_dp(two, 1)
        stored.append([(pools, m), (one, 0), (two, 0), (three, 0)])
    memory_t = regroup(after(memory.transpose(0, 1, 3, 2), patches_t))
    mem_two = swap_mp(memory_t, 1)
    mem_parts = (memory_t, swap_dp(memory_t, 1), mem_two, swap_dp(mem_two, 1))
    mem_full = memory_in(
        jnp.stack(
            [
                (((c ^ upper) // 2) ^ core) + 2 * (((c ^ upper) % 2) ^ across)
                for c in range(4)
            ]
        ),
        mem_order,
        mem_parts,
    )

    stored = [[(mem_full, 0)], [(mem_full, 1)]] + stored

    part_quarter = [2 * (core ^ (s % 2)) + (across ^ (s // 2)) for s in range(4)]
    pool_place = jnp.arange(pooled)
    pool_token = 2 * (pool_place % half_pool) + pool_place // half_pool
    now_index = jnp.concatenate([pq * pooled + pool_token for pq in part_quarter])
    pool_index = jnp.concatenate([pq * half_pool + jnp.arange(half_pool) for pq in part_quarter])
    mem_index = jnp.arange(half_mem)

    def key_bias(m):
        sides = [
            (now_index, lengths_all[2 + m] // 4),
            (mem_index if m == 0 else pool_index, lengths_all[1 + m] // 8),
            (mem_index if m < 2 else pool_index, lengths_all[m] // 8),
        ]
        return jnp.concatenate(
            [
                jnp.where((index < limit)[None, :], rel_bias[:, g : g + 1], -1e30)
                for g, (index, limit) in enumerate(sides)
            ],
            axis=1,
        ).reshape(heads // QUAD, QUAD, -1)

    attended, saved = None, {}
    for m in (2, 1, 0):
        attended, probs, keys, values = attend(
            m, query, conv_all, key_bias(m), stored[m + 2], stored[m + 1], stored[m], attended
        )
        saved[m] = (keys, values, probs)
    rest = spread_core([after(p, attended) for p in rest])

    position = quarter * rows + token
    within = position % FRAME
    live = position[None, :] < lengths_all[2:, None]
    inside = (
        (within[None, None, :] >= bounds[:, :, 0:1])
        & (within[None, None, :] < bounds[:, :, 1:2])
        & live[:, None, :]
    )
    denominator = ((bounds[:, :, 1] - bounds[:, :, 0]) * (lengths_all[2:, None] // FRAME)).astype(
        f32
    )
    select = inside.astype(f32) / denominator[:, :, None]
    target_row = jnp.arange(4 * pooled)
    target_quarter, target_rest = target_row // pooled, target_row % pooled
    source_row = (
        (((target_quarter // 2) ^ core) + 2 * ((target_quarter % 2) ^ across)) * pooled
        + (target_rest % 2) * half_pool
        + target_rest // 2
    )
    new_memory = memory_out(
        (quarter ^ upper)[None],
        one_hot_rows(source_row, 4 * pooled).T,
        stored[3] + stored[4],
    )
    first_res, normed_mlp, active, slope, second_res, feature = mlp(
        attended, embedded, vectors, select, rest, events=(new_memory,)
    )
    new_memory = regroup(new_memory)
    feature = after(feature.reshape(MICRO * boxes, width), new_memory)
    feature = group_sum_features(feature).astype(bf16)
    logits = contract_last(feature, head_low)
    target = labels.astype(f32)
    keep = (jnp.arange(boxes)[None, :] < counts[:, None]).astype(f32).reshape(-1, 1)
    lead = (quarter == 0).astype(f32)
    loss_part = jnp.sum((jax.nn.softplus(logits) - target * logits) * keep) * lead
    grad_logits = ((jax.nn.sigmoid(logits) - target) * keep).astype(bf16)

    grad_head = contract_rows(feature, grad_logits) * lead
    grad_feature = product(grad_logits, head_low).reshape(MICRO, boxes, width)
    grad_branch, grad_hidden, grad_attn, grad_first, grad_attended, sums = mlp_back(
        grad_feature, select, second_res, first_res, slope, vectors, rest
    )
    half = width // 2

    def weight_grad(left, right, at):
        return contract_rows(left[:, at : at + half], right).astype(bf16)

    sides = ((grad_branch, active), (normed_mlp, grad_hidden), (grad_attn, attended))
    rest_far = [weight_grad(*side, half) for side in sides]
    rest_near = [weight_grad(*side, 0) for side in sides]
    rest_pieces = halve_dp(rest_near, rest_far)

    dq, pool_grads, bias_grad, mem_taps = None, [], 0.0, 0.0
    events = tuple(rest_pieces)
    for m in range(MICRO):
        keys, values, probs = saved[m]
        dq, kept, sent, taps_part, bias_part = attend_back(
            m, query, keys, values, probs, grad_attended, stored[m + 1], stored[m], dq, events
        )
        got = swap_dp(sent, 1)
        away = (kept[:, 1].astype(f32) + got[:, 1].astype(f32)).astype(bf16)
        mine = kept[:, 0].astype(f32) + got[:, 0].astype(f32)
        pool_grads.append(mine + swap_mp(away, 1).astype(f32))
        bias_grad = bias_grad + bias_part
        mem_taps = mem_taps + taps_part
        events = (away,)
    projected_grad, embedded_grad, embed_sums, taps_grad = embed_back(
        dq,
        jnp.stack(pool_grads),
        raw_keys,
        raw_values,
        conv_all,
        embedded,
        grad_first,
        vectors,
        weights,
    )
    rest_total = collect_dp(rest_pieces)
    grad_vectors = jnp.concatenate([embed_sums[:3], sums[:4]])

    def small_grad(at):
        return jnp.concatenate(
            [
                contract_rows(embedded_grad[:, at : at + half], patches_in),
                grad_head[at : at + half],
                grad_vectors[:, at : at + half].T,
            ],
            axis=1,
        ).astype(bf16)

    attn_far = [small_grad(half), weight_grad(normed, projected_grad, half)]
    attn_near = [small_grad(0), weight_grad(normed, projected_grad, 0)]
    rest_total = after(rest_total, *attn_far)
    units = 4 * hidden_cols
    rest_pieces = []
    out_blocks = pick(
        [
            rest_total[:, 2 * units + c * head_cols : 2 * units + (c + 1) * head_cols]
            for c in range(4)
        ]
    )
    for s in range(4):
        piece = jnp.concatenate(
            [
                out_blocks[s],
                rest_total[:, s * hidden_cols : (s + 1) * hidden_cols],
                rest_total[:, units + s * hidden_cols : units + (s + 1) * hidden_cols],
            ],
            axis=1,
        )
        rest_pieces.append(piece if s == 0 else piece.astype(bf16))
    rest_mine = scatter_mp(rest_pieces)
    attn_total = collect_dp(halve_dp(attn_near, attn_far))
    small_size = patch + classes + 7
    small_total = attn_total[:, :small_size].astype(bf16)
    small_parts = trade_mp(
        [
            lax.dynamic_slice_in_dim(small_total, (mp_index ^ s) * sub, sub, axis=0)
            for s in range(4)
        ]
    )
    attn_parts = trade_mp(
        pick(
            [
                jnp.concatenate(
                    [
                        attn_total[
                            :,
                            small_size + (4 * j + c) * head_cols : small_size
                            + (4 * j + c + 1) * head_cols,
                        ]
                        for j in range(3)
                    ],
                    axis=1,
                ).astype(bf16)
                for c in range(4)
            ]
        )
    )

    count_local = jnp.sum(box_count).astype(f32) * (mp_index == 0).astype(f32)
    taps_rows = jnp.stack(
        [
            jnp.concatenate([taps_grad[4 * ch : 4 * ch + 4], mem_taps[ch]], axis=0)
            for ch in range(2)
        ],
        axis=1,
    ).reshape(12, 4, head_cols)
    scalars = jnp.stack([loss_part, count_local])
    last = jnp.concatenate(
        [
            bias_grad.reshape(heads, 128)[:, :3].reshape(4, -1),
            jnp.broadcast_to(scalars[None], (4, 2)),
        ],
        axis=1,
    )
    last = jnp.pad(last, ((0, 0), (0, head_cols - last.shape[1])))
    flat = jnp.concatenate([taps_rows, last[None]]).transpose(1, 0, 2)
    flat = sum_dp(flat)
    flat = scatter_mp(pick([flat[c] for c in range(4)]))
    loss_global = flat[12, own_heads * 3]
    box_total = flat[12, own_heads * 3 + 1]
    spot_row = jnp.arange(13)[:, None]
    spot_column = jnp.arange(head_cols)[None, :]
    counted = ((spot_row < 12) | (spot_column < own_heads * 3)).astype(f32) / dp_count
    attn_mine, small_mine, squares = squares_of(attn_parts, small_parts, rest_mine, flat, counted)
    for bit in range(dp_bits()):
        squares = squares + swap_dp(squares, 1 << bit)
    squares = squares + swap_mp(squares, 1)
    squares_two = swap_mp(squares, 2)

    def turned(arrays):
        up, down, embed_part, head, vector, conv, position = arrays
        return (up, down, embed_part.T, head.T, vector, conv.transpose(1, 0, 2), position)

    grads = (
        jnp.concatenate([attn_mine, rest_mine[:, head_cols + hidden_cols :]], axis=1),
        rest_mine[:, : head_cols + hidden_cols],
        small_mine[:, :patch],
        small_mine[:, patch : patch + classes],
        small_mine[:, patch + classes :].T,
        flat[:12].reshape(6, 2, head_cols),
        flat[12, : own_heads * 3].reshape(own_heads, 3),
    )
    masters = (
        up_weight,
        down_weight,
        embed_weight,
        head_weight,
        vector_weight,
        conv_weight,
        position_bias,
    )
    moments = (
        up_moment,
        down_moment,
        embed_moment,
        head_moment,
        vector_moment,
        conv_moment,
        position_moment,
    )
    averages = (
        up_average,
        down_average,
        embed_average,
        head_average,
        vector_average,
        conv_average,
        position_average,
    )
    rates = (LEARNING,) * 4 + (VECTOR_LEARNING,) * 3
    made = update(
        squares,
        squares_two,
        box_total.reshape(1, 1),
        grads,
        turned(masters),
        turned(moments),
        turned(averages),
        rates,
    )
    grad_norm = made[0].reshape(())
    results = []
    for i in range(3):
        results.extend(turned(made[1 + 7 * i : 8 + 7 * i]))

    return (
        (loss_global, box_total, grad_norm, new_memory.transpose(0, 1, 3, 2)) + tuple(results) + tuple(made[22:24])
    )


def solution(mesh):
    both = ("dp", "mp")
    weight_specs = (
        P("dp", "mp"),
        P("dp", "mp"),
        P(None, both),
        P(None, both),
        P(None, both),
        P(None, None, "mp"),
        P("mp", None),
    )
    memory_spec = P(None, None, "dp", "mp")
    return jax.shard_map(
        shards,
        mesh=mesh,
        in_specs=(
            P(None, both, None),
            P("dp", None),
            P("dp", None),
            P("dp", None, None, None),
            P("dp", None, None, None),
            memory_spec,
        )
        + weight_specs * 3,
        out_specs=(P(), P(), P(), memory_spec)
        + weight_specs * 3
        + (P("dp", "mp"), P("dp", "mp")),
        check_vma=False,
    )
```

```python
import functools

import jax
import jax.numpy as jnp
from jax import lax
from jax.experimental import pallas as pl
from jax.experimental.pallas import tpu as pltpu
from jax.sharding import PartitionSpec as P

MICRO = 3
FRAME = 64
EPSILON = 1e-06
LEARNING = 300.0
VECTOR_LEARNING = 6000.0
MOMENTUM = 0.5
AVERAGING = 0.5
THRESHOLD = 0.05
PRECISE = lax.Precision.HIGHEST
QUAD = 4
bf16 = jnp.bfloat16
f32 = jnp.float32


NEAR = 60 * 1024 * 1024


def product(first_operand, second_operand):
    return jnp.dot(first_operand, second_operand, preferred_element_type=f32)


def contract_last(first_operand, second_operand):
    return lax.dot_general(
        first_operand, second_operand, (((1,), (1,)), ((), ())), preferred_element_type=f32
    )


def contract_rows(first_operand, second_operand):
    return lax.dot_general(
        first_operand, second_operand, (((0,), (0,)), ((), ())), preferred_element_type=f32
    )


def swap_dp(inputs, mask):
    size = lax.axis_size("dp")
    return lax.ppermute(inputs, "dp", [(i, i ^ mask) for i in range(size)])


def swap_mp(inputs, mask):
    size = lax.axis_size("mp")
    return lax.ppermute(inputs, "mp", [(i, i ^ mask) for i in range(size)])


def dp_bits():
    return lax.axis_size("dp").bit_length() - 1


def regroup(inputs):
    count = lax.axis_size("dp")
    pairs = []
    for d in range(count):
        for z in range(4):
            moved = (d % 2) ^ (z // 2)
            pairs.append((d * 4 + z, (d ^ moved) * 4 + (z ^ (2 * moved))))
    return lax.ppermute(inputs, ("dp", "mp"), pairs)


def pick(pieces):
    odd = lax.axis_index("mp") % 2 == 1
    return [jnp.where(odd, pieces[c ^ 1], pieces[c]) for c in range(4)]


def gather_mp(inputs):
    return [inputs] + [swap_mp(inputs, s) for s in (1, 2, 3)]


def halve_mp(pieces):
    sent = jnp.concatenate([pieces[1], pieces[3]], axis=1).astype(bf16)
    return pieces[0], (pieces[2], sent), swap_mp(sent, 1)


def halve_more(near, far, got):
    columns = near.shape[1]
    far = far[0].astype(f32) + got[:, columns:].astype(f32)
    return near.astype(f32) + got[:, :columns].astype(f32), swap_mp(far.astype(bf16), 2)


def spread_dp(inputs):
    return [inputs] + [swap_dp(inputs, b) for b in range(2, lax.axis_size("dp"), 2)]


def spread_core(pieces):
    return one_or_all(pieces + [swap_dp(p, 1) for p in pieces])


def one_or_all(pieces):
    if pieces[0].shape[0] % 16:
        pieces = [jnp.concatenate(pieces)]
    return tuple(pieces)


def halve_dp(near, far):
    got = [swap_dp(f, 1) for f in far]
    count = lax.axis_size("dp") // 2
    rows = near[0].shape[0] // count
    return [
        jnp.concatenate(
            [
                n[i * rows : (i + 1) * rows].astype(f32) + g[i * rows : (i + 1) * rows].astype(f32)
                for n, g in zip(near, got)
            ],
            axis=1,
        ).astype(bf16)
        for i in range(count)
    ]


def trade_dp(pieces, first, last):
    return [swap_dp(piece, 2 * first + 2 * i) for i, piece in enumerate(pieces[first:last])]


def after(value, *events):
    return lax.optimization_barrier((value,) + events)[0]


def group_sum_features(inputs):
    count = lax.axis_size("dp")
    width = inputs.shape[1] // count
    order = [b for b in range(count) if b % 2 == 0] + [b for b in range(count) if b % 2]
    at = [order.index(b ^ 1) for b in order]
    got = swap_dp(inputs, 1)
    inputs = inputs + jnp.concatenate([got[:, p * width : (p + 1) * width] for p in at], axis=1)
    return inputs + swap_mp(inputs, 1)


def call(
    body, grid, in_specs, out_specs, out_shape, operands, flops, scratch=(), alias=None, events=()
):
    known, late = len(operands), len(operands) + len(events)

    def run(*refs):
        body(*refs[:known], *refs[late:])

    return pl.pallas_call(
        run,
        grid=grid,
        in_specs=list(in_specs) + [pl.BlockSpec(memory_space=pl.ANY)] * len(events),
        out_specs=out_specs,
        out_shape=out_shape,
        scratch_shapes=list(scratch),
        input_output_aliases=alias or {},
        compiler_params=pltpu.CompilerParams(vmem_limit_bytes=NEAR),
        cost_estimate=pl.CostEstimate(flops=1000, bytes_accessed=1000, transcendentals=0),
    )(*operands, *events)


def whole(array):
    return pl.BlockSpec(array.shape, lambda *i, n=len(array.shape): (0,) * n)


def transfers(pieces, targets, sems):
    copies, at = [], 0
    for piece in pieces:
        rows = piece.shape[0]
        for column, target in targets:
            copies.append(
                pltpu.make_async_copy(
                    piece.at[:, column : column + target.shape[1]],
                    target.at[at : at + rows],
                    sems.at[len(copies)],
                )
            )
        at += rows
    return copies


def begin(copies):
    for copy in copies:
        copy.start()


def finish(copies):
    for copy in copies:
        copy.wait()


def fetch(pieces, targets, sems):
    copies = transfers(pieces, targets, sems)
    begin(copies)
    finish(copies)


def standard(inputs):
    centered = inputs - jnp.mean(inputs, axis=-1, keepdims=True)
    scale = lax.rsqrt(jnp.mean(centered * centered, axis=-1, keepdims=True) + EPSILON)
    return centered * scale, scale


def standard_back(grad, unit, scale):
    return scale * (
        grad
        - jnp.mean(grad, axis=-1, keepdims=True)
        - unit * jnp.mean(grad * unit, axis=-1, keepdims=True)
    )


def memory_in_kernel(index_ref, order_ref, one_ref, two_ref, three_ref, four_ref, out_ref):
    parts = [r[0, 0] for r in (one_ref, two_ref, three_ref, four_ref)]
    blocks = []
    for c in range(4):
        s = index_ref[c]
        chosen = parts[3]
        for p in (2, 1, 0):
            chosen = jnp.where(s == p, parts[p], chosen)
        blocks.append(chosen)
    out_ref[0, 0] = contract_last(order_ref[...], jnp.concatenate(blocks)).astype(bf16)


def memory_in(index, order, parts, events=()):
    _, _, columns, rows = parts[0].shape
    return call(
        memory_in_kernel,
        (2, 2),
        [pl.BlockSpec(memory_space=pltpu.SMEM), pl.BlockSpec((rows, rows), lambda i, j: (0, 0))]
        + [pl.BlockSpec((1, 1, columns, rows), lambda i, j: (i, j, 0, 0))] * 4,
        pl.BlockSpec((1, 1, rows, 4 * columns), lambda i, j: (i, j, 0, 0)),
        jax.ShapeDtypeStruct((2, 2, rows, 4 * columns), bf16),
        (index, order) + tuple(parts),
        8 * rows * rows * 4 * columns,
        events=events,
    )


def memory_out_kernel(index_ref, order_ref, *refs):
    out_ref = refs[-1]
    chosen = index_ref[0]
    for m in range(2):
        rows = jnp.concatenate([r[0, 0] for r in refs[4 * m : 4 * m + 4]])
        turned = contract_rows(rows, order_ref[...]).astype(bf16)
        columns = turned.shape[0] // 4
        blocks = [turned[c * columns : (c + 1) * columns] for c in range(4)]
        block = blocks[3]
        for c in (2, 1, 0):
            block = jnp.where(chosen == c, blocks[c], block)
        out_ref[m, 0] = block


def memory_out(index, order, parts):
    _, _, rows, width = parts[0][0].shape
    return call(
        memory_out_kernel,
        (2,),
        [
            pl.BlockSpec(memory_space=pltpu.SMEM),
            pl.BlockSpec((4 * rows, 4 * rows), lambda i: (0, 0)),
        ]
        + [pl.BlockSpec((1, 1, rows, width), lambda i, m=m: (m, i, 0, 0)) for _, m in parts],
        pl.BlockSpec((2, 1, width // 4, 4 * rows), lambda i: (0, i, 0, 0)),
        jax.ShapeDtypeStruct((2, 2, width // 4, 4 * rows), bf16),
        (index, order) + tuple(a for a, _ in parts),
        8 * (4 * rows) ** 2 * width,
    )


def join_kernel(main, odd_ref, *refs):
    pieces, out_ref = refs[:-1], refs[-1]
    odd = odd_ref[0] == 1
    for c in range(4):
        out_ref[:, c * main : (c + 1) * main] = pieces[c][:, :main]
    tails = [p[:, main:].astype(f32) for p in pieces]
    heads = [jnp.where(odd, tails[c ^ 1], tails[c]) for c in range(4)]
    out_ref[:, 4 * main :] = jnp.concatenate(heads, axis=1).astype(bf16)


def join(main, odd, pieces):
    rows, columns = pieces[0].shape
    return call(
        functools.partial(join_kernel, main),
        (1,),
        [pl.BlockSpec(memory_space=pltpu.SMEM)] + [whole(p) for p in pieces],
        pl.BlockSpec((rows, 4 * columns), lambda i: (0, 0)),
        jax.ShapeDtypeStruct((rows, 4 * columns), bf16),
        (odd,) + tuple(pieces),
        0,
    )


def embed_kernel(count, patch_ref, order_ref, taps_ref, *refs):
    pieces = refs[:count]
    (
        sorted_ref, embedded_ref, normed_ref, query_ref, key_ref, value_ref, pool_ref,
        vec_ref, head_ref, qk_s, v_s, small_s, sems,
    ) = refs[count:]
    width = embedded_ref.shape[1]
    edge = small_s.shape[1] - 128

    @pl.when(pl.program_id(0) == 0)
    def _():
        fetch(pieces, ((0, qk_s), (2 * width, v_s), (3 * width, small_s)), sems)
        turned = small_s[:, edge:].astype(f32).T
        vec_ref[...] = turned[0:8] + turned[8:16] + turned[16:24]
        head_ref[...] = turned[24 : 24 + head_ref.shape[0]].astype(bf16)

    patch = contract_last(order_ref[...], patch_ref[0]).astype(bf16)
    sorted_ref[...] = patch
    embedded = contract_last(patch, small_s[:, : patch.shape[1]]) + vec_ref[0:1]
    embedded_ref[...] = embedded
    unit, _ = standard(embedded)
    normed = (unit * vec_ref[1:2] + vec_ref[2:3]).astype(bf16)
    normed_ref[...] = normed
    query_ref[...] = product(normed, qk_s[:, :width]).astype(bf16)
    for ch, weight, raw_ref in ((0, qk_s[:, width:], key_ref), (1, v_s[...], value_ref)):
        raw = product(normed, weight)
        raw_ref[...] = raw.astype(bf16)
        rows = raw.shape[0] // 4
        pooled = raw[:rows] * taps_ref[ch, 0:1]
        for t in range(1, 4):
            pooled = pooled + raw[t * rows : (t + 1) * rows] * taps_ref[ch, t : t + 1]
        pool_ref[0, ch] = pooled.astype(bf16)


def embed(patches_t, order, taps, weights, classes, events=()):
    _, patch, rows = patches_t.shape
    width = taps.shape[2]
    total = MICRO * rows
    edge = weights[0].shape[1] - 3 * width

    def tile(columns):
        return pl.BlockSpec((rows, columns), lambda i: (i, 0))

    return call(
        functools.partial(embed_kernel, len(weights)),
        (MICRO,),
        [pl.BlockSpec((1, patch, rows), lambda i: (i, 0, 0)), whole(order), whole(taps)]
        + [pl.BlockSpec(memory_space=pl.ANY)] * len(weights),
        [tile(patch), tile(width), tile(width), tile(width), tile(width), tile(width)]
        + [
            pl.BlockSpec((1, 2, rows // 4, width), lambda i: (i, 0, 0, 0)),
            pl.BlockSpec((8, width), lambda i: (0, 0)),
            pl.BlockSpec((classes, width), lambda i: (0, 0)),
        ],
        [
            jax.ShapeDtypeStruct((total, patch), bf16),
            jax.ShapeDtypeStruct((total, width), f32),
        ]
        + [jax.ShapeDtypeStruct((total, width), bf16)] * 4
        + [
            jax.ShapeDtypeStruct((MICRO, 2, rows // 4, width), bf16),
            jax.ShapeDtypeStruct((8, width), f32),
            jax.ShapeDtypeStruct((classes, width), bf16),
        ],
        (patches_t, order, taps) + weights,
        2 * total * width * (patch + 3 * width),
        scratch=[
            pltpu.VMEM((width, 2 * width), bf16),
            pltpu.VMEM((width, width), bf16),
            pltpu.VMEM((width, edge), bf16),
            pltpu.SemaphoreType.DMA((3 * len(weights),)),
        ],
        events=events,
    )


def attend_kernel(sources, q_ref, taps_ref, bias_ref, *refs):
    count = sum(sources)
    now, newer = refs[: sources[0]], refs[sources[0] : sources[0] + sources[1]]
    older = refs[sources[0] + sources[1] : count]
    out_ref, prob_ref, key_ref, value_ref = refs[-4:]
    query = q_ref[...]
    rows, width = query.shape
    size = width // QUAD
    for ch, target in ((0, key_ref), (1, value_ref)):
        at = 0
        for r in now:
            n = r.shape[2]
            target[at : at + n] = r[0, ch]
            at += n
        first, second = taps_ref[ch, 4:5], taps_ref[ch, 5:6]
        for r in newer + older:
            n = r.shape[2] // 2
            target[at : at + n] = (
                r[0, ch, :n].astype(f32) * first + r[0, ch, n:].astype(f32) * second
            ).astype(bf16)
            at += n
    keys_t = key_ref[...].T
    values = value_ref[...]
    lane = lax.broadcasted_iota(jnp.int32, (rows, width), 1) // size
    scaled = query * (size**-0.5)
    total = query.astype(f32)
    for h in range(QUAD):
        own = jnp.where(lane == h, scaled, jnp.zeros_like(scaled))
        scores = product(own, keys_t) + bias_ref[0, h : h + 1, :]
        top = jnp.max(scores, axis=-1, keepdims=True)
        exponent = jnp.exp(scores - top)
        denominator = jnp.sum(exponent, axis=-1, keepdims=True)
        probs = (exponent * (1.0 / denominator)).astype(bf16)
        prob_ref[h] = probs
        total = total + jnp.where(lane == h, product(probs, values), 0.0)
    out_ref[...] = total.astype(bf16)


def source_specs(entries, block):
    return [
        pl.BlockSpec((1, 2, a.shape[2], block), lambda i, m=m: (m, 0, 0, i)) for a, m in entries
    ]


def attend(micro, query, taps, bias, now, newer, older, before, events=()):
    rows = query.shape[0] // MICRO
    width = query.shape[1]
    count = bias.shape[2]
    quads = bias.shape[0]
    block = width // quads
    entries = now + newer + older
    operands = (query, taps, bias) + tuple(a for a, _ in entries)
    specs = [
        pl.BlockSpec((rows, block), lambda i: (micro, i)),
        pl.BlockSpec((2, 6, block), lambda i: (0, 0, i)),
        pl.BlockSpec((1, QUAD, count), lambda i: (i, 0, 0)),
    ] + source_specs(entries, block)
    alias = {}
    if before is not None:
        alias = {len(operands): 0}
        operands = operands + (before,)
        specs.append(pl.BlockSpec(memory_space=pl.ANY))
    return call(
        functools.partial(attend_kernel, (len(now), len(newer), len(older))),
        (quads,),
        specs,
        [
            pl.BlockSpec((rows, block), lambda i: (micro, i)),
            pl.BlockSpec((QUAD, rows, count), lambda i: (i, 0, 0)),
            pl.BlockSpec((count, block), lambda i: (0, i)),
            pl.BlockSpec((count, block), lambda i: (0, i)),
        ],
        [
            jax.ShapeDtypeStruct(query.shape, bf16),
            jax.ShapeDtypeStruct((quads * QUAD, rows, count), bf16),
            jax.ShapeDtypeStruct((count, width), bf16),
            jax.ShapeDtypeStruct((count, width), bf16),
        ],
        operands,
        4 * rows * count * width * 4,
        alias=alias,
        events=events,
    )


def attend_back_kernel(sources, q_ref, k_ref, v_ref, prob_ref, grad_ref, *refs):
    entries = refs[: sum(sources)]
    dq_ref, keep_ref, send_ref, taps_ref, bias_ref = refs[-5:]
    query = q_ref[...]
    grad = grad_ref[...]
    rows, width = query.shape
    size = width // QUAD
    keys = k_ref[...]
    count = keys.shape[0]
    values_t = v_ref[...].T
    query_t = query.T
    grad_t = grad.T
    scaling = size**-0.5
    lane = lax.broadcasted_iota(jnp.int32, (rows, width), 1) // size
    total = jnp.zeros((rows, width), f32)
    ones = jnp.ones((16, rows), bf16)
    half = count // 2
    spot = lax.broadcasted_iota(jnp.int32, (1, 128), 1)
    key_parts, value_parts = [], []
    for h in range(QUAD):
        own = jnp.where(lane == h, grad, jnp.zeros_like(grad))
        probs_low = prob_ref[h]
        probs = probs_low.astype(f32)
        pulled = probs * product(own, values_t)
        shift = jnp.sum(pulled, axis=-1, keepdims=True)
        score_grad = (pulled - probs * shift).astype(bf16)
        total = total + jnp.where(lane == h, product(score_grad, keys), 0.0)
        left = jnp.concatenate([query_t[h * size : (h + 1) * size], ones])
        found = product(left, score_grad)
        key_parts.append(found[:size])
        sums = found[size : size + 1]
        row = jnp.zeros((1, 128), f32)
        for g, (a, b) in enumerate(((0, half), (half, half + half // 2), (half + half // 2, count))):
            row = row + jnp.where(spot == g, jnp.sum(sums[:, a:b], axis=1, keepdims=True), 0.0)
        bias_ref[0, h : h + 1, :] = row
        value_parts.append(product(grad_t[h * size : (h + 1) * size], probs_low))
    dq_ref[...] = (total * scaling + grad.astype(f32)).astype(bf16)
    part = keep_ref.shape[2]
    for ch, parts, factor in ((0, key_parts, scaling), (1, value_parts, 1.0)):
        found = jnp.concatenate(parts).T * factor
        for s in range(4):
            target = send_ref if s % 2 else keep_ref
            target[s // 2, ch] = found[s * part : (s + 1) * part].astype(bf16)
        at = half
        first = jnp.zeros((1, width), f32)
        second = jnp.zeros((1, width), f32)
        for r in entries:
            n = r.shape[2] // 2
            piece = found[at : at + n]
            first = first + jnp.sum(piece * r[0, ch, :n].astype(f32), axis=0, keepdims=True)
            second = second + jnp.sum(piece * r[0, ch, n:].astype(f32), axis=0, keepdims=True)
            at += n
        taps_ref[ch, 0:1] = first
        taps_ref[ch, 1:2] = second


def attend_back(micro, query, keys, values, probs, grad, newer, older, before, events=()):
    heads, rows, count = probs.shape
    width = query.shape[1]
    quads = heads // QUAD
    block = width // quads
    entries = newer + older
    operands = (query, keys, values, probs, grad) + tuple(a for a, _ in entries)
    specs = [
        pl.BlockSpec((rows, block), lambda i: (micro, i)),
        pl.BlockSpec((count, block), lambda i: (0, i)),
        pl.BlockSpec((count, block), lambda i: (0, i)),
        pl.BlockSpec((QUAD, rows, count), lambda i: (i, 0, 0)),
        pl.BlockSpec((rows, block), lambda i: (micro, i)),
    ] + source_specs(entries, block)
    alias = {}
    if before is not None:
        alias = {len(operands): 0}
        operands = operands + (before,)
        specs.append(pl.BlockSpec(memory_space=pl.ANY))
    part = count // 8
    return call(
        functools.partial(attend_back_kernel, (len(newer), len(older))),
        (quads,),
        specs,
        [
            pl.BlockSpec((rows, block), lambda i: (micro, i)),
            pl.BlockSpec((2, 2, part, block), lambda i: (0, 0, 0, i)),
            pl.BlockSpec((2, 2, part, block), lambda i: (0, 0, 0, i)),
            pl.BlockSpec((2, 2, block), lambda i: (0, 0, i)),
            pl.BlockSpec((1, QUAD, 128), lambda i: (i, 0, 0)),
        ],
        [
            jax.ShapeDtypeStruct(query.shape, bf16),
            jax.ShapeDtypeStruct((2, 2, part, width), bf16),
            jax.ShapeDtypeStruct((2, 2, part, width), bf16),
            jax.ShapeDtypeStruct((2, 2, width), f32),
            jax.ShapeDtypeStruct((quads, QUAD, 128), f32),
        ],
        operands,
        8 * rows * count * width * 4,
        alias=alias,
        events=events,
    )


def gelu_pair(inputs):
    size = jnp.abs(inputs)
    t = 1.0 / (1.0 + (0.3275911 * 0.5**0.5) * size)
    bell = jnp.exp(-0.5 * inputs * inputs)
    tail = (
        t
        * (
            0.5 * 0.254829592
            + t
            * (
                0.5 * -0.284496736
                + t * (0.5 * 1.421413741 + t * (0.5 * -1.453152027 + t * (0.5 * 1.061405429)))
            )
        )
        * bell
    )
    share = jnp.where(inputs > 0.0, 1.0 - tail, tail)
    return inputs * share, share + inputs * bell * 0.3989422804014327


def mlp_weights(width, units, count):
    return [
        pltpu.VMEM((width, width), bf16),
        pltpu.VMEM((width, 2 * units), bf16),
        pltpu.SemaphoreType.DMA((count,)),
        pltpu.SemaphoreType.DMA((count,)),
    ]


def mlp_kernel(count, attended_ref, embedded_ref, vec_ref, select_ref, *refs):
    (
        first_ref, normed_ref, active_ref, slope_ref, second_ref, feature_ref,
        out_s, both_s, out_sems, sems,
    ) = refs[count:]
    units = both_s.shape[1] // 2
    out_copies = transfers(refs[:count], ((2 * units, out_s),), out_sems)
    copies = transfers(refs[:count], ((0, both_s),), sems)
    starting = pl.program_id(0) == 0

    @pl.when(starting)
    def _():
        begin(out_copies)
        begin(copies)
        finish(out_copies)

    first = embedded_ref[...] + contract_last(attended_ref[...], out_s[...])
    first_ref[...] = first
    unit, _ = standard(first)
    normed = (unit * vec_ref[3:4] + vec_ref[4:5]).astype(bf16)
    normed_ref[...] = normed
    total = first

    @pl.when(starting)
    def _():
        finish(copies)

    chunk = units // 4
    for s in range(4):
        at = s * chunk
        hidden = product(normed, both_s[:, 2 * at + chunk : 2 * at + 2 * chunk])
        value, slope = gelu_pair(hidden)
        value = value.astype(bf16)
        active_ref[:, at : at + chunk] = value
        slope_ref[:, at : at + chunk] = slope.astype(bf16)
        total = total + contract_last(value, both_s[:, 2 * at : 2 * at + chunk])
    second_ref[...] = total
    unit, _ = standard(total)
    final = unit * vec_ref[5:6] + vec_ref[6:7]
    feature_ref[0] = jnp.dot(
        select_ref[0], final, precision=PRECISE, preferred_element_type=f32
    )


def mlp(attended, embedded, vec, select, weights, events=()):
    total, width = embedded.shape
    rows = total // MICRO
    units = (weights[0].shape[1] - width) // 2
    boxes = select.shape[1]

    def tile(columns):
        return pl.BlockSpec((rows, columns), lambda i: (i, 0))

    return call(
        functools.partial(mlp_kernel, len(weights)),
        (MICRO,),
        [
            tile(width),
            tile(width),
            whole(vec),
            pl.BlockSpec((1, boxes, rows), lambda i: (i, 0, 0)),
        ]
        + [pl.BlockSpec(memory_space=pl.ANY)] * len(weights),
        [tile(width), tile(width), tile(units), tile(units), tile(width)]
        + [pl.BlockSpec((1, boxes, width), lambda i: (i, 0, 0))],
        [
            jax.ShapeDtypeStruct((total, width), f32),
            jax.ShapeDtypeStruct((total, width), bf16),
            jax.ShapeDtypeStruct((total, units), bf16),
            jax.ShapeDtypeStruct((total, units), bf16),
            jax.ShapeDtypeStruct((total, width), f32),
            jax.ShapeDtypeStruct((MICRO, boxes, width), f32),
        ],
        (attended, embedded, vec, select) + weights,
        2 * total * width * (width + 2 * units),
        scratch=mlp_weights(width, units, len(weights)),
        events=events,
    )


def mlp_back_kernel(
    count, pull_ref, select_ref, second_ref, first_ref, slope_ref, vec_ref, *refs
):
    (
        branch_ref, hidden_ref, attn_ref, first_grad_ref, attended_ref, sums_ref,
        out_s, both_s, out_sems, sems,
    ) = refs[count:]
    units = both_s.shape[1] // 2
    out_copies = transfers(refs[:count], ((2 * units, out_s),), out_sems)
    copies = transfers(refs[:count], ((0, both_s),), sems)
    starting = pl.program_id(0) == 0

    @pl.when(starting)
    def _():
        begin(copies)
        begin(out_copies)
        sums_ref[...] = jnp.zeros_like(sums_ref)

    pull = lax.dot_general(
        select_ref[0],
        pull_ref[0],
        (((0,), (0,)), ((), ())),
        precision=PRECISE,
        preferred_element_type=f32,
    )
    unit, scale = standard(second_ref[...])
    sums_ref[2:3] += jnp.sum(pull * unit, axis=0, keepdims=True)
    sums_ref[3:4] += jnp.sum(pull, axis=0, keepdims=True)
    second_grad = standard_back(pull * vec_ref[5:6], unit, scale)
    branch = second_grad.astype(bf16)
    branch_ref[...] = branch

    @pl.when(starting)
    def _():
        finish(copies)

    chunk = units // 4
    normed_grad = jnp.zeros(second_grad.shape, f32)
    for s in range(4):
        at = s * chunk
        active_grad = product(branch, both_s[:, 2 * at : 2 * at + chunk])
        hidden_grad = (active_grad * slope_ref[:, at : at + chunk].astype(f32)).astype(bf16)
        hidden_ref[:, at : at + chunk] = hidden_grad
        normed_grad = normed_grad + contract_last(
            hidden_grad, both_s[:, 2 * at + chunk : 2 * at + 2 * chunk]
        )

    @pl.when(starting)
    def _():
        finish(out_copies)

    unit, scale = standard(first_ref[...])
    sums_ref[0:1] += jnp.sum(normed_grad * unit, axis=0, keepdims=True)
    sums_ref[1:2] += jnp.sum(normed_grad, axis=0, keepdims=True)
    first_grad = standard_back(normed_grad * vec_ref[3:4], unit, scale) + second_grad
    first_grad_ref[...] = first_grad
    attn = first_grad.astype(bf16)
    attn_ref[...] = attn
    attended_ref[...] = product(attn, out_s[...]).astype(bf16)


def mlp_back(pull, select, second, first, slope, vec, weights, events=()):
    total, width = second.shape
    rows = total // MICRO
    units = (weights[0].shape[1] - width) // 2
    boxes = select.shape[1]

    def tile(columns):
        return pl.BlockSpec((rows, columns), lambda i: (i, 0))

    return call(
        functools.partial(mlp_back_kernel, len(weights)),
        (MICRO,),
        [
            pl.BlockSpec((1, boxes, width), lambda i: (i, 0, 0)),
            pl.BlockSpec((1, boxes, rows), lambda i: (i, 0, 0)),
            tile(width),
            tile(width),
            tile(units),
            whole(vec),
        ]
        + [pl.BlockSpec(memory_space=pl.ANY)] * len(weights),
        [tile(width), tile(units), tile(width), tile(width), tile(width)]
        + [pl.BlockSpec((8, width), lambda i: (0, 0))],
        [
            jax.ShapeDtypeStruct((total, width), bf16),
            jax.ShapeDtypeStruct((total, units), bf16),
            jax.ShapeDtypeStruct((total, width), bf16),
            jax.ShapeDtypeStruct((total, width), f32),
            jax.ShapeDtypeStruct((total, width), bf16),
            jax.ShapeDtypeStruct((8, width), f32),
        ],
        (pull, select, second, first, slope, vec) + weights,
        2 * total * width * (width + 2 * units),
        scratch=mlp_weights(width, units, len(weights)),
        events=events,
    )


def embed_back_kernel(
    count, dq_ref, key_ref, value_ref, taps_ref, embedded_ref, first_ref, normed_ref, patch_ref,
    vec_ref, head_ref, more_ref, *refs
):
    pools = refs[: 3 * MICRO]
    (
        near_ref, far_ref, taps_out, qk_s, v_s, pool_s, sums_s, normed_s, projected_s, grad_s,
        patch_s, sems,
    ) = refs[3 * MICRO + count :]
    rows, width = embedded_ref.shape
    step = pl.program_id(0)

    @pl.when(step == 0)
    def _():
        sums_s[...] = jnp.zeros_like(sums_s)
        sums_s[3:7] = more_ref[0:4]
        sums_s[8 : 8 + head_ref.shape[0]] = head_ref[...]
        taps_out[...] = jnp.zeros_like(taps_out)
        patch_s[...] = jnp.zeros_like(patch_s)
        for m in range(MICRO):
            kept, got, far = pools[3 * m : 3 * m + 3]
            for ch in range(2):
                pool_s[m, ch] = (
                    kept[0, ch].astype(f32) + got[0, ch].astype(f32) + far[ch].astype(f32)
                )
        fetch(refs[3 * MICRO : 3 * MICRO + count], ((0, qk_s), (2 * width, v_s)), sems)

    at = pl.multiple_of(step * rows, 128)
    here = pl.ds(at, rows)
    projected_s[here, :width] = dq_ref[...]
    pooled = rows // 4
    for ch, raw_ref in ((0, key_ref), (1, value_ref)):
        pool = pool_s[step, ch]
        for t in range(4):
            projected_s[
                pl.ds(at + t * pooled, pooled), (1 + ch) * width : (2 + ch) * width
            ] = (pool * taps_ref[ch, t : t + 1]).astype(bf16)
            raw = raw_ref[t * pooled : (t + 1) * pooled].astype(f32)
            taps_out[4 * ch + t : 4 * ch + t + 1] += jnp.sum(pool * raw, axis=0, keepdims=True)
    normed_grad = contract_last(projected_s[here, : 2 * width], qk_s[...])
    normed_grad = normed_grad + contract_last(projected_s[here, 2 * width :], v_s[...])
    unit, scale = standard(embedded_ref[...])
    sums_s[1:2] += jnp.sum(normed_grad * unit, axis=0, keepdims=True)
    sums_s[2:3] += jnp.sum(normed_grad, axis=0, keepdims=True)
    grad = standard_back(normed_grad * vec_ref[1:2], unit, scale) + first_ref[...]
    grad = grad.astype(bf16)
    sums_s[0:1] += jnp.sum(grad.astype(f32), axis=0, keepdims=True)
    normed_s[:, here] = normed_ref[...].T
    grad_s[:, here] = grad.T
    patch_s[here, : patch_ref.shape[1]] = patch_ref[...]

    @pl.when(step == MICRO - 1)
    def _():
        half = width // 2
        edge = 3 * width + patch_s.shape[1]
        for out_ref, top in ((far_ref, half), (near_ref, 0)):
            part = slice(top, top + half)
            for c in range(3):
                out_ref[:, c * width : (c + 1) * width] = product(
                    normed_s[part], projected_s[:, c * width : (c + 1) * width]
                ).astype(bf16)
            out_ref[:, 3 * width : edge] = product(grad_s[part], patch_s[...]).astype(bf16)
            out_ref[:, edge:] = sums_s[:, part].T.astype(bf16)


def embed_back(
    dq, keys, values, taps, embedded, first_grad, normed, patches, vec, head, more, pools, weights,
    events=(),
):
    total, width = embedded.shape
    rows = total // MICRO
    patch = patches.shape[1]
    edge = patch + (-patch % 128)
    columns = 3 * width + edge + 128

    def tile(columns):
        return pl.BlockSpec((rows, columns), lambda i: (i, 0))

    operands = (dq, keys, values, taps, embedded, first_grad, normed, patches, vec, head, more)
    half = pl.BlockSpec((width // 2, columns), lambda i: (0, 0))
    return call(
        functools.partial(embed_back_kernel, len(weights)),
        (MICRO,),
        [tile(width)] * 3
        + [whole(taps)]
        + [tile(width)] * 3
        + [tile(patch)]
        + [whole(a) for a in (vec, head, more) + pools]
        + [pl.BlockSpec(memory_space=pl.ANY)] * len(weights),
        [half, half, pl.BlockSpec((8, width), lambda i: (0, 0))],
        [
            jax.ShapeDtypeStruct((width // 2, columns), bf16),
            jax.ShapeDtypeStruct((width // 2, columns), bf16),
            jax.ShapeDtypeStruct((8, width), f32),
        ],
        operands + pools + weights,
        2 * total * width * 3 * width,
        scratch=[
            pltpu.VMEM((width, 2 * width), bf16),
            pltpu.VMEM((width, width), bf16),
            pltpu.VMEM((MICRO, 2, rows // 4, width), f32),
            pltpu.VMEM((128, width), f32),
            pltpu.VMEM((width, total), bf16),
            pltpu.VMEM((total, 3 * width), bf16),
            pltpu.VMEM((width, total), bf16),
            pltpu.VMEM((total, edge), bf16),
            pltpu.SemaphoreType.DMA((2 * len(weights),)),
        ],
        events=events,
    )


def squares_kernel(*refs):
    grads, flat_ref, outs = refs[:6], refs[6], refs[7:]
    total = 0.0
    for i in range(3):
        found = grads[2 * i][...].astype(f32) + grads[2 * i + 1][...].astype(f32)
        outs[i][...] = found
        total = total + jnp.sum(found * found)
    rows = flat_ref.shape[0]
    outs[3][...] = jnp.zeros_like(outs[3]) + total
    outs[3][:rows] = flat_ref[...]


def squares_of(attn, small, rest, flat):
    operands = tuple(attn) + tuple(small) + tuple(rest) + (flat,)
    rows = flat.shape[0] + (-flat.shape[0] % 8)
    rows += 8 * (rows == flat.shape[0])
    shapes = [jax.ShapeDtypeStruct(g[0].shape, f32) for g in (attn, small, rest)]
    shapes.append(jax.ShapeDtypeStruct((rows, flat.shape[1]), f32))
    return call(
        squares_kernel,
        (1,),
        [whole(o) for o in operands],
        [whole(o) for o in shapes],
        shapes,
        operands,
        0,
    )


def update_kernel(rates, patch, odd_ref, one_ref, two_ref, *refs):
    count = len(rates)
    attn_ref, small_ref, rest_ref = refs[:3]
    weights, moments, averages = (refs[3 + i * count : 3 + (i + 1) * count] for i in range(3))
    outs = refs[3 + 3 * count :]
    heads = weights[6].shape[0] * 3
    blocks = []
    square = one_ref[52:53, 0:1] + two_ref[52:53, 0:1]
    spot = lax.broadcasted_iota(jnp.int32, (13, one_ref.shape[1]), 1)
    row = lax.broadcasted_iota(jnp.int32, (13, one_ref.shape[1]), 0)
    counted = (row < 12) | (spot < heads)
    for c in range(4):
        far = 13 * (c ^ 2)
        block = one_ref[13 * c : 13 * c + 13] + two_ref[far : far + 13]
        kept = jnp.where(counted, block, 0.0)
        square = square + jnp.sum(kept * kept)
        blocks.append(block)
    mine = jnp.where(odd_ref[0] == 1, blocks[1], blocks[0])
    boxes = blocks[0][12:13, heads + 1 : heads + 2]
    norm = jnp.sqrt(square) / boxes
    lane = lax.broadcasted_iota(jnp.int32, (1, 128), 1)
    loss = blocks[0][12:13, heads : heads + 1]
    outs[0][...] = jnp.where(lane == 0, loss, jnp.where(lane == 1, boxes, norm))
    scaling = jnp.minimum(1.0, THRESHOLD / norm) / boxes
    hidden = weights[0].shape[1] - attn_ref.shape[1]
    edge = small_ref.shape[1] - 128
    classes = weights[3].shape[1]
    tail = small_ref[:, edge:]

    def step(i, at, grad):
        grad = grad * scaling
        moment = MOMENTUM * moments[i][at] + grad
        updated = weights[i][at] - rates[i] * (grad + MOMENTUM * moment)
        outs[1 + i][at] = updated
        outs[1 + count + i][at] = moment
        outs[1 + 2 * count + i][at] = AVERAGING * averages[i][at] + (1.0 - AVERAGING) * updated
        if i < 2:
            outs[1 + 3 * count + i][at] = updated.astype(bf16)

    step(0, ..., jnp.concatenate([attn_ref[...], rest_ref[:, :hidden]], axis=1))
    step(1, ..., rest_ref[:, hidden:])
    step(2, ..., small_ref[:, :patch])
    step(3, ..., tail[:, 8 : 8 + classes])
    step(4, ..., tail.T[:7])
    for t in range(6):
        step(5, t, mine[2 * t : 2 * t + 2])
    for h in range(heads // 3):
        step(6, slice(h, h + 1), mine[12:13, 3 * h : 3 * h + 3])


def update(odd, one, two, grads, patch, weights, moments, averages, rates):
    operands = (odd, one, two) + grads + weights + moments + averages
    kept = [jax.ShapeDtypeStruct(w.shape, f32) for w in weights]
    shapes = [jax.ShapeDtypeStruct((1, 128), f32)] + kept * 3
    shapes = shapes + [jax.ShapeDtypeStruct(w.shape, bf16) for w in weights[:2]]
    return call(
        functools.partial(update_kernel, rates, patch),
        (1,),
        [pl.BlockSpec(memory_space=pltpu.SMEM)] + [whole(o) for o in operands[1:]],
        [pl.BlockSpec(o.shape, lambda i, n=len(o.shape): (0,) * n) for o in shapes],
        shapes,
        operands,
        0,
    )


def one_hot_rows(index, count):
    return (index[:, None] == jnp.arange(count)[None, :]).astype(bf16)


def shards(
    patches,
    clip_len,
    box_count,
    box_bounds,
    box_labels,
    memory,
    up_weight,
    down_weight,
    embed_weight,
    head_weight,
    vector_weight,
    conv_weight,
    position_bias,
    up_moment,
    down_moment,
    embed_moment,
    head_moment,
    vector_moment,
    conv_moment,
    position_moment,
    up_average,
    down_average,
    embed_average,
    head_average,
    vector_average,
    conv_average,
    position_average,
):
    dp_index = lax.axis_index("dp")
    mp_index = lax.axis_index("mp")
    dp_count = lax.axis_size("dp")
    across, core = mp_index % 2, dp_index % 2
    upper = mp_index - across
    quarter = 2 * core + across
    rows = patches.shape[1]
    eighth = rows // 8
    pooled = rows // 4
    half_pool = pooled // 2
    head_cols = conv_weight.shape[2]
    width = 4 * head_cols
    sub = embed_weight.shape[1]
    patch = embed_weight.shape[0]
    classes = head_weight.shape[0]
    boxes = box_bounds.shape[2]
    own_heads = position_bias.shape[0]
    heads = own_heads * 4
    hidden_cols = up_weight.shape[1] - 3 * head_cols

    ints = jnp.concatenate(
        [clip_len.reshape(-1), box_count.reshape(-1), box_bounds.reshape(-1), box_labels.reshape(-1)]
    )
    total_ints = ints.shape[0]
    ints = jnp.pad(ints, (0, -total_ints % 1024)).reshape(-1, 128)
    ints = regroup(ints).reshape(-1)
    lengths_all = ints[:5]
    counts = ints[5:8]
    bounds = ints[8 : 8 + MICRO * boxes * 2].reshape(MICRO, boxes, 2)
    labels = ints[8 + MICRO * boxes * 2 : total_ints].reshape(MICRO * boxes, classes)

    def in_three(array):
        high = lax.reduce_precision(array, 8, 7)
        middle = lax.reduce_precision(array - high, 8, 7)
        return [high, middle, array - high - middle]

    edge = patch + (-patch % 128)
    columns_in = [jnp.pad(embed_weight, ((0, edge - patch), (0, 0)))]
    columns_in += [jnp.pad(v, ((0, 1), (0, 0))) for v in in_three(vector_weight)]
    columns_in += [jnp.pad(head_weight, ((0, 128 - 24 - classes), (0, 0)))]
    taps_pos = jnp.concatenate(
        [
            conv_weight.reshape(12, head_cols),
            jnp.pad(position_bias.reshape(1, -1), ((0, 0), (0, head_cols - position_bias.size))),
        ]
    )
    taps_pos = jnp.concatenate(in_three(taps_pos)).reshape(sub, -1)
    small = jnp.concatenate([jnp.concatenate(columns_in).T, taps_pos], axis=1).astype(bf16)
    strip = -(-small.shape[1] // 512) * 128
    small = jnp.pad(small, ((0, 0), (0, 4 * strip - small.shape[1])))
    small = jnp.concatenate([small[:, i * strip : (i + 1) * strip] for i in range(4)])
    up_low = up_weight.astype(bf16)
    down_low = down_weight.astype(bf16)
    pieces = gather_mp(jnp.concatenate([up_low[:, : 3 * head_cols], small], axis=1))
    place = jnp.arange(16 * sub)
    source = (
        (((place // sub) % 4) ^ mp_index) * 4 * sub + place // (4 * sub) * sub + place % sub
    )
    small = product(
        one_hot_rows(source, 16 * sub), jnp.concatenate([p[:, 3 * head_cols :] for p in pieces])
    ).astype(bf16)
    small = jnp.concatenate(
        [small[i * 4 * sub : (i + 1) * 4 * sub] for i in range(4)], axis=1
    )
    small_mine = small[:, : edge + 128]
    taps_pos = small[:, edge + 128 : edge + 128 + 39 * head_cols // sub]
    taps_pos = jnp.sum(taps_pos.reshape(4, 3, 13, head_cols).astype(f32), axis=1)
    taps_pos = jnp.where(upper == 2, jnp.roll(taps_pos, 2, axis=0), taps_pos)
    conv_all = taps_pos[:, :12].transpose(1, 0, 2).reshape(2, 6, width)
    rel_bias = taps_pos[:, 12, : position_bias.size].reshape(heads, 3)
    weights = jnp.concatenate(
        [p[:, j * head_cols : (j + 1) * head_cols] for j in range(3) for p in pick(pieces)]
        + [small_mine],
        axis=1,
    )
    weights = spread_core(spread_dp(weights))
    pieces = gather_mp(
        after(
            jnp.concatenate(
                [down_low[:, head_cols:], up_low[:, 3 * head_cols :], down_low[:, :head_cols]],
                axis=1,
            ),
            *pieces,
        )
    )
    rest = join(2 * hidden_cols, across[None], pieces)
    patches_t = regroup(after(patches.transpose(0, 2, 1), rest))
    rest = [rest, swap_dp(rest, 2), swap_dp(rest, 4)]

    place = jnp.arange(rows)
    token = 8 * (place % eighth) + 4 * ((place // eighth) % 2) + place // (2 * eighth)
    token_order = one_hot_rows(token, rows)
    mem_rows = memory.shape[2]
    half_mem = mem_rows // 2
    mem_place = jnp.arange(mem_rows)
    mem_order = one_hot_rows(2 * (mem_place % half_mem) + mem_place // half_mem, mem_rows)
    (
        patches_in,
        embedded,
        normed,
        query,
        raw_keys,
        raw_values,
        pools,
        vectors,
        head_low,
    ) = embed(patches_t, token_order, conv_all, weights, classes, events=tuple(rest[1:]))
    rest_late = after(rest[0], *rest[1:])
    rest_late = [swap_dp(rest_late, b) for b in range(6, dp_count, 2)]
    two = swap_mp(pools, 1)
    gathered = (pools, swap_dp(pools, 1), two, swap_dp(two, 1))
    stored = [[(a, m) for a in gathered] for m in range(MICRO)]
    memory_t = regroup(after(memory.transpose(0, 1, 3, 2), pools))
    mem_two = swap_mp(after(memory_t, two), 1)
    stored = [None, None] + stored

    part_quarter = [2 * (core ^ (s % 2)) + (across ^ (s // 2)) for s in range(4)]
    pool_place = jnp.arange(pooled)
    pool_token = 2 * (pool_place % half_pool) + pool_place // half_pool
    now_index = jnp.concatenate([pq * pooled + pool_token for pq in part_quarter])
    pool_index = jnp.concatenate([pq * half_pool + jnp.arange(half_pool) for pq in part_quarter])
    mem_index = jnp.arange(half_mem)

    def key_bias(m):
        sides = [
            (now_index, lengths_all[2 + m] // 4),
            (mem_index if m == 0 else pool_index, lengths_all[1 + m] // 8),
            (mem_index if m < 2 else pool_index, lengths_all[m] // 8),
        ]
        return jnp.concatenate(
            [
                jnp.where((index < limit)[None, :], rel_bias[:, g : g + 1], -1e30)
                for g, (index, limit) in enumerate(sides)
            ],
            axis=1,
        ).reshape(heads // QUAD, QUAD, -1)

    attended, saved = None, {}
    for m in (2, 1, 0):
        attended, probs, keys, values = attend(
            m, query, conv_all, key_bias(m), stored[m + 2], stored[m + 1], stored[m], attended,
            events=tuple(rest_late) if m == 0 else (),
        )
        saved[m] = (keys, values, probs)
        if m == 2:
            rest_core = [swap_dp(after(p, attended), 1) for p in rest]
        if m == 1:
            late_core = [swap_dp(after(p, attended), 1) for p in rest_late]
        if m > 1:
            target_row = jnp.arange(4 * pooled)
            target_quarter, target_rest = target_row // pooled, target_row % pooled
            source_row = (
                (((target_quarter // 2) ^ core) + 2 * ((target_quarter % 2) ^ across)) * pooled
                + (target_rest % 2) * half_pool
                + target_rest // 2
            )
            new_memory = memory_out(
                (quarter ^ upper)[None],
                one_hot_rows(source_row, 4 * pooled).T,
                stored[3] + stored[4],
            )
            mem_two = after(mem_two, attended)
            mem_parts = (
                memory_t,
                swap_dp(after(memory_t, attended), 1),
                mem_two,
                swap_dp(mem_two, 1),
            )
            mem_full = memory_in(
                jnp.stack(
                    [
                        (((c ^ upper) // 2) ^ core) + 2 * (((c ^ upper) % 2) ^ across)
                        for c in range(4)
                    ]
                ),
                mem_order,
                mem_parts,
                events=(new_memory,),
            )
            new_memory = regroup(new_memory)
            stored[:2] = [[(mem_full, 0)], [(mem_full, 1)]]
    rest = one_or_all(rest + rest_late + rest_core + late_core)

    position = quarter * rows + token
    within = position % FRAME
    live = position[None, :] < lengths_all[2:, None]
    inside = (
        (within[None, None, :] >= bounds[:, :, 0:1])
        & (within[None, None, :] < bounds[:, :, 1:2])
        & live[:, None, :]
    )
    denominator = ((bounds[:, :, 1] - bounds[:, :, 0]) * (lengths_all[2:, None] // FRAME)).astype(
        f32
    )
    select = inside.astype(f32) / denominator[:, :, None]
    first_res, normed_mlp, active, slope, second_res, feature = mlp(
        attended, embedded, vectors, select, rest
    )
    feature = after(feature.reshape(MICRO * boxes, width), new_memory)
    feature = group_sum_features(feature).astype(bf16)
    logits = contract_last(feature, head_low)
    target = labels.astype(f32)
    keep = (jnp.arange(boxes)[None, :] < counts[:, None]).astype(f32).reshape(-1, 1)
    lead = (quarter == 0).astype(f32)
    loss_part = jnp.sum((jax.nn.softplus(logits) - target * logits) * keep) * lead
    grad_logits = ((jax.nn.sigmoid(logits) - target) * keep).astype(bf16)

    grad_head = contract_rows(grad_logits, feature) * lead
    grad_feature = product(grad_logits, head_low).reshape(MICRO, boxes, width)
    grad_branch, grad_hidden, grad_attn, grad_first, grad_attended, sums = mlp_back(
        grad_feature, select, second_res, first_res, slope, vectors, rest
    )
    half = width // 2

    def weight_grad(left, right, at):
        return contract_rows(left[:, at : at + half], right).astype(bf16)

    sides = ((grad_branch, active), (normed_mlp, grad_hidden), (grad_attn, attended))
    rest_far = [weight_grad(*side, half) for side in sides]
    rest_near = [weight_grad(*side, 0) for side in sides]
    rest_pieces = halve_dp(rest_near, rest_far)

    dq, pool_grads, bias_grad, mem_taps = None, [], 0.0, 0.0
    events = tuple(rest_pieces)
    rest_found = trade_dp(rest_pieces, 1, 3)
    for m in range(MICRO):
        keys, values, probs = saved[m]
        dq, kept, sent, taps_part, bias_part = attend_back(
            m, query, keys, values, probs, grad_attended, stored[m + 1], stored[m], dq, events
        )
        got = swap_dp(sent, 1)
        away = (kept[1].astype(f32) + got[1].astype(f32)).astype(bf16)
        pool_grads.extend([kept, got, swap_mp(away, 1)])
        bias_grad = bias_grad + bias_part
        mem_taps = mem_taps + taps_part
        events = (away,)
        if m == 1:
            events = (away, pool_grads[2]) + tuple(rest_found)
            rest_pieces[3:] = [after(p, *rest_found) for p in rest_pieces[3:]]
            rest_found += trade_dp(rest_pieces, 3, None)
    rest_total = sum((f.astype(f32) for f in rest_found), rest_pieces[0].astype(f32))
    units = 4 * hidden_cols
    rest_pieces = []
    out_blocks = pick(
        [
            rest_total[:, 2 * units + c * head_cols : 2 * units + (c + 1) * head_cols]
            for c in range(4)
        ]
    )
    for s in range(4):
        piece = jnp.concatenate(
            [
                rest_total[:, units + s * hidden_cols : units + (s + 1) * hidden_cols],
                out_blocks[s],
                rest_total[:, s * hidden_cols : (s + 1) * hidden_cols],
            ],
            axis=1,
        )
        rest_pieces.append(piece)
    rest_near, rest_far, rest_got = halve_mp(rest_pieces)
    attn_near, attn_far, taps_grad = embed_back(
        dq,
        raw_keys,
        raw_values,
        conv_all,
        embedded,
        grad_first,
        normed,
        patches_in,
        vectors,
        grad_head,
        sums,
        tuple(pool_grads),
        weights,
        events=(rest_near,) + rest_far,
    )
    attn_pieces = halve_dp([attn_near], [attn_far])
    attn_found = trade_dp(attn_pieces, 1, None)
    rest_got = after(rest_got, *attn_pieces)
    columns = rest_near.shape[1]
    far = (rest_far[0].astype(f32) + rest_got[:, columns:].astype(f32)).astype(bf16)
    rest_mine = (rest_near + rest_got[:, :columns].astype(f32), swap_mp(far, 2))
    attn_found[-1] = after(attn_found[-1], far)
    attn_total = sum((f.astype(f32) for f in attn_found), attn_pieces[0].astype(f32))
    small_total = attn_total[:, 3 * width :]
    small_parts = halve_more(*halve_mp(
        [
            lax.dynamic_slice_in_dim(small_total, (mp_index ^ s) * sub, sub, axis=0)
            for s in range(4)
        ]
    ))
    attn_parts = halve_more(*halve_mp(
        pick(
            [
                jnp.concatenate(
                    [
                        attn_total[:, (4 * j + c) * head_cols : (4 * j + c + 1) * head_cols]
                        for j in range(3)
                    ],
                    axis=1,
                )
                for c in range(4)
            ]
        )
    ))

    count_local = jnp.sum(box_count).astype(f32) * (mp_index == 0).astype(f32)
    taps_rows = jnp.stack(
        [
            jnp.concatenate([taps_grad[4 * ch : 4 * ch + 4], mem_taps[ch]], axis=0)
            for ch in range(2)
        ],
        axis=1,
    ).reshape(12, 4, head_cols)
    scalars = jnp.stack([loss_part, count_local])
    last = jnp.concatenate(
        [
            bias_grad.reshape(heads, 128)[:, :3].reshape(4, -1),
            jnp.broadcast_to(scalars[None], (4, 2)),
        ],
        axis=1,
    )
    last = jnp.pad(last, ((0, 0), (0, head_cols - last.shape[1])))
    flat = jnp.concatenate([taps_rows, last[None]]).transpose(1, 0, 2)
    attn_mine, small_mine, rest_mine, both = squares_of(
        attn_parts, small_parts, rest_mine, flat.reshape(52, head_cols)
    )
    for bit in range(dp_bits()):
        both = both + swap_dp(both, 1 << bit)
    both = both + swap_mp(both, 1)
    both_two = swap_mp(both, 2)

    def turned(arrays):
        up, down, embed_part, head, vector, conv, position = arrays
        return (up, down, embed_part.T, head.T, vector, conv.transpose(1, 0, 2), position)

    masters = (
        up_weight,
        down_weight,
        embed_weight,
        head_weight,
        vector_weight,
        conv_weight,
        position_bias,
    )
    moments = (
        up_moment,
        down_moment,
        embed_moment,
        head_moment,
        vector_moment,
        conv_moment,
        position_moment,
    )
    averages = (
        up_average,
        down_average,
        embed_average,
        head_average,
        vector_average,
        conv_average,
        position_average,
    )
    rates = (LEARNING,) * 4 + (VECTOR_LEARNING,) * 3
    made = update(
        across[None],
        both,
        both_two,
        (attn_mine, small_mine, rest_mine),
        patch,
        turned(masters),
        turned(moments),
        turned(averages),
        rates,
    )
    loss_global, box_total, grad_norm = (made[0][0, i] for i in range(3))
    results = []
    for i in range(3):
        results.extend(turned(made[1 + 7 * i : 8 + 7 * i]))

    return (
        (loss_global, box_total, grad_norm, new_memory.transpose(0, 1, 3, 2)) + tuple(results) + tuple(made[22:24])
    )


def solution(mesh):
    both = ("dp", "mp")
    weight_specs = (
        P("dp", "mp"),
        P("dp", "mp"),
        P(None, both),
        P(None, both),
        P(None, both),
        P(None, None, "mp"),
        P("mp", None),
    )
    memory_spec = P(None, None, "dp", "mp")
    return jax.shard_map(
        shards,
        mesh=mesh,
        in_specs=(
            P(None, both, None),
            P("dp", None),
            P("dp", None),
            P("dp", None, None, None),
            P("dp", None, None, None),
            memory_spec,
        )
        + weight_specs * 3,
        out_specs=(P(), P(), P(), memory_spec)
        + weight_specs * 3
        + (P("dp", "mp"), P("dp", "mp")),
        check_vma=False,
    )
```

```python
import functools

import jax
import jax.numpy as jnp
from jax import lax
from jax.experimental import pallas as pl
from jax.experimental.pallas import tpu as pltpu
from jax.sharding import PartitionSpec as P

MICRO = 3
FRAME = 64
EPSILON = 1e-06
LEARNING = 300.0
VECTOR_LEARNING = 6000.0
MOMENTUM = 0.5
AVERAGING = 0.5
THRESHOLD = 0.05
PRECISE = lax.Precision.HIGHEST
QUAD = 4
bf16 = jnp.bfloat16
f32 = jnp.float32


NEAR = 60 * 1024 * 1024


def product(first_operand, second_operand):
    return jnp.dot(first_operand, second_operand, preferred_element_type=f32)


def contract_last(first_operand, second_operand):
    return lax.dot_general(
        first_operand, second_operand, (((1,), (1,)), ((), ())), preferred_element_type=f32
    )


def contract_rows(first_operand, second_operand):
    return lax.dot_general(
        first_operand, second_operand, (((0,), (0,)), ((), ())), preferred_element_type=f32
    )


def swap_dp(inputs, mask):
    size = lax.axis_size("dp")
    return lax.ppermute(inputs, "dp", [(i, i ^ mask) for i in range(size)])


def swap_mp(inputs, mask):
    size = lax.axis_size("mp")
    return lax.ppermute(inputs, "mp", [(i, i ^ mask) for i in range(size)])


def dp_bits():
    return lax.axis_size("dp").bit_length() - 1


def regroup(inputs):
    count = lax.axis_size("dp")
    pairs = []
    for d in range(count):
        for z in range(4):
            moved = (d % 2) ^ (z // 2)
            pairs.append((d * 4 + z, (d ^ moved) * 4 + (z ^ (2 * moved))))
    return lax.ppermute(inputs, ("dp", "mp"), pairs)


def pick(pieces):
    odd = lax.axis_index("mp") % 2 == 1
    return [jnp.where(odd, pieces[c ^ 1], pieces[c]) for c in range(4)]


def gather_mp(inputs):
    return [inputs] + [swap_mp(inputs, s) for s in (1, 2, 3)]


def halve_mp(pieces):
    sent = jnp.concatenate([pieces[1], pieces[3]], axis=1).astype(bf16)
    return pieces[0], (pieces[2], sent), swap_mp(sent, 1)


def halve_more(near, far, got):
    columns = near.shape[1]
    far = far[0].astype(f32) + got[:, columns:].astype(f32)
    return near.astype(f32) + got[:, :columns].astype(f32), swap_mp(far.astype(bf16), 2)


def spread_dp(inputs):
    return [inputs] + [swap_dp(inputs, b) for b in range(2, lax.axis_size("dp"), 2)]


def spread_core(pieces):
    return one_or_all(pieces + [swap_dp(p, 1) for p in pieces])


def one_or_all(pieces):
    if pieces[0].shape[0] % 16:
        pieces = [jnp.concatenate(pieces)]
    return tuple(pieces)


def halve_dp(near, far):
    got = [swap_dp(f, 1) for f in far]
    count = lax.axis_size("dp") // 2
    rows = near[0].shape[0] // count
    return [
        jnp.concatenate(
            [
                n[i * rows : (i + 1) * rows].astype(f32) + g[i * rows : (i + 1) * rows].astype(f32)
                for n, g in zip(near, got)
            ],
            axis=1,
        ).astype(bf16)
        for i in range(count)
    ]


def trade_dp(pieces, first, last):
    return [swap_dp(piece, 2 * first + 2 * i) for i, piece in enumerate(pieces[first:last])]


def after(value, *events):
    return lax.optimization_barrier((value,) + events)[0]


def group_sum_features(inputs):
    count = lax.axis_size("dp")
    width = inputs.shape[1] // count
    order = [b for b in range(count) if b % 2 == 0] + [b for b in range(count) if b % 2]
    at = [order.index(b ^ 1) for b in order]
    got = swap_dp(inputs, 1)
    inputs = inputs + jnp.concatenate([got[:, p * width : (p + 1) * width] for p in at], axis=1)
    return inputs + swap_mp(inputs, 1)


def call(
    body, grid, in_specs, out_specs, out_shape, operands, flops, scratch=(), alias=None, events=()
):
    known, late = len(operands), len(operands) + len(events)

    def run(*refs):
        body(*refs[:known], *refs[late:])

    return pl.pallas_call(
        run,
        grid=grid,
        in_specs=list(in_specs) + [pl.BlockSpec(memory_space=pl.ANY)] * len(events),
        out_specs=out_specs,
        out_shape=out_shape,
        scratch_shapes=list(scratch),
        input_output_aliases=alias or {},
        compiler_params=pltpu.CompilerParams(vmem_limit_bytes=NEAR),
        cost_estimate=pl.CostEstimate(flops=1000, bytes_accessed=1000, transcendentals=0),
    )(*operands, *events)


def whole(array):
    return pl.BlockSpec(array.shape, lambda *i, n=len(array.shape): (0,) * n)


def transfers(pieces, targets, sems):
    copies, at = [], 0
    for piece in pieces:
        rows = piece.shape[0]
        for column, target in targets:
            copies.append(
                pltpu.make_async_copy(
                    piece.at[:, column : column + target.shape[1]],
                    target.at[at : at + rows],
                    sems.at[len(copies)],
                )
            )
        at += rows
    return copies


def begin(copies):
    for copy in copies:
        copy.start()


def finish(copies):
    for copy in copies:
        copy.wait()


def fetch(pieces, targets, sems):
    copies = transfers(pieces, targets, sems)
    begin(copies)
    finish(copies)


def standard(inputs):
    centered = inputs - jnp.mean(inputs, axis=-1, keepdims=True)
    scale = lax.rsqrt(jnp.mean(centered * centered, axis=-1, keepdims=True) + EPSILON)
    return centered * scale, scale


def standard_back(grad, unit, scale):
    return scale * (
        grad
        - jnp.mean(grad, axis=-1, keepdims=True)
        - unit * jnp.mean(grad * unit, axis=-1, keepdims=True)
    )


def memory_in_kernel(index_ref, order_ref, *refs):
    parts, (out_ref, held, sems) = refs[:4], refs[4:]
    columns = parts[0].shape[2]

    def copy(p, c):
        target = held.at[:, :, c * columns : (c + 1) * columns]
        return pltpu.make_async_copy(parts[p], target, sems.at[c])

    for c in range(4):
        for p in range(4):

            @pl.when(index_ref[c] == p)
            def _(p=p, c=c):
                copy(p, c).start()

    for c in range(4):
        copy(0, c).wait()
    order = order_ref[...]
    for m in range(2):
        for ch in range(2):
            out_ref[m, ch] = contract_last(order, held[m, ch]).astype(bf16)


def memory_in(index, order, parts, events=()):
    _, _, columns, rows = parts[0].shape
    return call(
        memory_in_kernel,
        (1,),
        [pl.BlockSpec(memory_space=pltpu.SMEM), whole(order)]
        + [pl.BlockSpec(memory_space=pl.ANY)] * 4,
        pl.BlockSpec((2, 2, rows, 4 * columns), lambda i: (0, 0, 0, 0)),
        jax.ShapeDtypeStruct((2, 2, rows, 4 * columns), bf16),
        (index, order) + tuple(parts),
        0,
        scratch=[
            pltpu.VMEM((2, 2, 4 * columns, rows), bf16),
            pltpu.SemaphoreType.DMA((4,)),
        ],
        events=events,
    )


def memory_out_kernel(index_ref, order_ref, *refs):
    out_ref, turned = refs[-2:]
    columns = turned.shape[0] // 4
    at = pl.multiple_of(index_ref[0] * columns, 64)
    for m in range(2):
        rows = jnp.concatenate([r[0, 0] for r in refs[4 * m : 4 * m + 4]])
        turned[...] = contract_rows(rows, order_ref[...])
        out_ref[m, 0] = turned[pl.ds(at, columns)].astype(bf16)


def memory_out(index, order, parts, events=()):
    _, _, rows, width = parts[0][0].shape
    return call(
        memory_out_kernel,
        (2,),
        [
            pl.BlockSpec(memory_space=pltpu.SMEM),
            pl.BlockSpec((4 * rows, 4 * rows), lambda i: (0, 0)),
        ]
        + [pl.BlockSpec((1, 1, rows, width), lambda i, m=m: (m, i, 0, 0)) for _, m in parts],
        pl.BlockSpec((2, 1, width // 4, 4 * rows), lambda i: (0, i, 0, 0)),
        jax.ShapeDtypeStruct((2, 2, width // 4, 4 * rows), bf16),
        (index, order) + tuple(a for a, _ in parts),
        8 * (4 * rows) ** 2 * width,
        scratch=[pltpu.VMEM((width, 4 * rows), f32)],
        events=events,
    )


def join_kernel(main, odd_ref, *refs):
    pieces, out_ref = refs[:-1], refs[-1]
    odd = odd_ref[0] == 1
    for c in range(4):
        out_ref[:, c * main : (c + 1) * main] = pieces[c][:, :main]
    tails = [p[:, main:].astype(f32) for p in pieces]
    heads = [jnp.where(odd, tails[c ^ 1], tails[c]) for c in range(4)]
    out_ref[:, 4 * main :] = jnp.concatenate(heads, axis=1).astype(bf16)


def join(main, odd, pieces):
    rows, columns = pieces[0].shape
    return call(
        functools.partial(join_kernel, main),
        (1,),
        [pl.BlockSpec(memory_space=pltpu.SMEM)] + [whole(p) for p in pieces],
        pl.BlockSpec((rows, 4 * columns), lambda i: (0, 0)),
        jax.ShapeDtypeStruct((rows, 4 * columns), bf16),
        (odd,) + tuple(pieces),
        0,
    )


def embed_kernel(count, patch_ref, order_ref, taps_ref, *refs):
    pieces = refs[:count]
    (
        sorted_ref, embedded_ref, normed_ref, query_ref, key_ref, value_ref, pool_ref,
        vec_ref, head_ref, qk_s, v_s, small_s, sems,
    ) = refs[count:]
    width = embedded_ref.shape[1]
    edge = small_s.shape[1] - 128

    @pl.when(pl.program_id(0) == 0)
    def _():
        fetch(pieces, ((0, qk_s), (2 * width, v_s), (3 * width, small_s)), sems)
        turned = small_s[:, edge:].astype(f32).T
        vec_ref[...] = turned[0:8] + turned[8:16] + turned[16:24]
        head_ref[...] = turned[24 : 24 + head_ref.shape[0]].astype(bf16)

    patch = contract_last(order_ref[...], patch_ref[0]).astype(bf16)
    sorted_ref[...] = patch
    embedded = contract_last(patch, small_s[:, : patch.shape[1]]) + vec_ref[0:1]
    embedded_ref[...] = embedded
    unit, _ = standard(embedded)
    normed = (unit * vec_ref[1:2] + vec_ref[2:3]).astype(bf16)
    normed_ref[...] = normed
    query_ref[...] = product(normed, qk_s[:, :width]).astype(bf16)
    for ch, weight, raw_ref in ((0, qk_s[:, width:], key_ref), (1, v_s[...], value_ref)):
        raw = product(normed, weight)
        raw_ref[...] = raw.astype(bf16)
        rows = raw.shape[0] // 4
        pooled = raw[:rows] * taps_ref[ch, 0:1]
        for t in range(1, 4):
            pooled = pooled + raw[t * rows : (t + 1) * rows] * taps_ref[ch, t : t + 1]
        pool_ref[0, ch] = pooled.astype(bf16)


def embed(patches_t, order, taps, weights, classes, events=()):
    _, patch, rows = patches_t.shape
    width = taps.shape[2]
    total = MICRO * rows
    edge = weights[0].shape[1] - 3 * width

    def tile(columns):
        return pl.BlockSpec((rows, columns), lambda i: (i, 0))

    return call(
        functools.partial(embed_kernel, len(weights)),
        (MICRO,),
        [pl.BlockSpec((1, patch, rows), lambda i: (i, 0, 0)), whole(order), whole(taps)]
        + [pl.BlockSpec(memory_space=pl.ANY)] * len(weights),
        [tile(patch), tile(width), tile(width), tile(width), tile(width), tile(width)]
        + [
            pl.BlockSpec((1, 2, rows // 4, width), lambda i: (i, 0, 0, 0)),
            pl.BlockSpec((8, width), lambda i: (0, 0)),
            pl.BlockSpec((classes, width), lambda i: (0, 0)),
        ],
        [
            jax.ShapeDtypeStruct((total, patch), bf16),
            jax.ShapeDtypeStruct((total, width), f32),
        ]
        + [jax.ShapeDtypeStruct((total, width), bf16)] * 4
        + [
            jax.ShapeDtypeStruct((MICRO, 2, rows // 4, width), bf16),
            jax.ShapeDtypeStruct((8, width), f32),
            jax.ShapeDtypeStruct((classes, width), bf16),
        ],
        (patches_t, order, taps) + weights,
        2 * total * width * (patch + 3 * width),
        scratch=[
            pltpu.VMEM((width, 2 * width), bf16),
            pltpu.VMEM((width, width), bf16),
            pltpu.VMEM((width, edge), bf16),
            pltpu.SemaphoreType.DMA((3 * len(weights),)),
        ],
        events=events,
    )


def attend_kernel(sources, q_ref, taps_ref, bias_ref, *refs):
    count = sum(sources)
    now, newer = refs[: sources[0]], refs[sources[0] : sources[0] + sources[1]]
    older = refs[sources[0] + sources[1] : count]
    out_ref, prob_ref, key_ref, value_ref = refs[-4:]
    query = q_ref[...]
    rows, width = query.shape
    size = width // QUAD
    for ch, target in ((0, key_ref), (1, value_ref)):
        at = 0
        for r in now:
            n = r.shape[2]
            target[at : at + n] = r[0, ch]
            at += n
        first, second = taps_ref[ch, 4:5], taps_ref[ch, 5:6]
        for r in newer + older:
            n = r.shape[2] // 2
            target[at : at + n] = (
                r[0, ch, :n].astype(f32) * first + r[0, ch, n:].astype(f32) * second
            ).astype(bf16)
            at += n
    keys_t = key_ref[...].T
    values = value_ref[...]
    lane = lax.broadcasted_iota(jnp.int32, (rows, width), 1) // size
    scaled = query * (size**-0.5)
    total = query.astype(f32)
    def score(h):
        own = jnp.where(lane == h, scaled, jnp.zeros_like(scaled))
        return product(own, keys_t) + bias_ref[0, h : h + 1, :]

    following = score(0)
    for h in range(QUAD):
        scores = following
        if h + 1 < QUAD:
            following = score(h + 1)
        top = jnp.max(scores, axis=-1, keepdims=True)
        exponent = jnp.exp(scores - top)
        denominator = jnp.sum(exponent, axis=-1, keepdims=True)
        probs = (exponent * (1.0 / denominator)).astype(bf16)
        prob_ref[h] = probs
        total = total + jnp.where(lane == h, product(probs, values), 0.0)
    out_ref[...] = total.astype(bf16)


def source_specs(entries, block):
    return [
        pl.BlockSpec((1, 2, a.shape[2], block), lambda i, m=m: (m, 0, 0, i)) for a, m in entries
    ]


def attend(micro, query, taps, bias, now, newer, older, before, events=()):
    rows = query.shape[0] // MICRO
    width = query.shape[1]
    count = bias.shape[2]
    quads = bias.shape[0]
    block = width // quads
    entries = now + newer + older
    operands = (query, taps, bias) + tuple(a for a, _ in entries)
    specs = [
        pl.BlockSpec((rows, block), lambda i: (micro, i)),
        pl.BlockSpec((2, 6, block), lambda i: (0, 0, i)),
        pl.BlockSpec((1, QUAD, count), lambda i: (i, 0, 0)),
    ] + source_specs(entries, block)
    alias = {}
    if before is not None:
        alias = {len(operands): 0}
        operands = operands + (before,)
        specs.append(pl.BlockSpec(memory_space=pl.ANY))
    return call(
        functools.partial(attend_kernel, (len(now), len(newer), len(older))),
        (quads,),
        specs,
        [
            pl.BlockSpec((rows, block), lambda i: (micro, i)),
            pl.BlockSpec((QUAD, rows, count), lambda i: (i, 0, 0)),
            pl.BlockSpec((count, block), lambda i: (0, i)),
            pl.BlockSpec((count, block), lambda i: (0, i)),
        ],
        [
            jax.ShapeDtypeStruct(query.shape, bf16),
            jax.ShapeDtypeStruct((quads * QUAD, rows, count), bf16),
            jax.ShapeDtypeStruct((count, width), bf16),
            jax.ShapeDtypeStruct((count, width), bf16),
        ],
        operands,
        4 * rows * count * width * 4,
        alias=alias,
        events=events,
    )


def attend_back_kernel(sources, q_ref, k_ref, v_ref, prob_ref, grad_ref, *refs):
    entries = refs[: sum(sources)]
    dq_ref, keep_ref, send_ref, taps_ref, bias_ref = refs[-5:]
    query = q_ref[...]
    grad = grad_ref[...]
    rows, width = query.shape
    size = width // QUAD
    keys = k_ref[...]
    count = keys.shape[0]
    values_t = v_ref[...].T
    query_t = query.T
    grad_t = grad.T
    scaling = size**-0.5
    lane = lax.broadcasted_iota(jnp.int32, (rows, width), 1) // size
    total = jnp.zeros((rows, width), f32)
    ones = jnp.ones((16, rows), bf16)
    half = count // 2
    spot = lax.broadcasted_iota(jnp.int32, (1, 128), 1)
    key_parts, value_parts = [], []
    def pull(h):
        own = jnp.where(lane == h, grad, jnp.zeros_like(grad))
        return product(own, values_t)

    following = pull(0)
    for h in range(QUAD):
        current = following
        if h + 1 < QUAD:
            following = pull(h + 1)
        probs_low = prob_ref[h]
        probs = probs_low.astype(f32)
        pulled = probs * current
        shift = jnp.sum(pulled, axis=-1, keepdims=True)
        score_grad = (pulled - probs * shift).astype(bf16)
        total = total + jnp.where(lane == h, product(score_grad, keys), 0.0)
        left = jnp.concatenate([query_t[h * size : (h + 1) * size], ones])
        found = product(left, score_grad)
        key_parts.append(found[:size])
        sums = found[size : size + 1]
        row = jnp.zeros((1, 128), f32)
        for g, (a, b) in enumerate(((0, half), (half, half + half // 2), (half + half // 2, count))):
            row = row + jnp.where(spot == g, jnp.sum(sums[:, a:b], axis=1, keepdims=True), 0.0)
        bias_ref[0, h : h + 1, :] = row
        value_parts.append(product(grad_t[h * size : (h + 1) * size], probs_low))
    dq_ref[...] = (total * scaling + grad.astype(f32)).astype(bf16)
    part = keep_ref.shape[2]
    for ch, parts, factor in ((0, key_parts, scaling), (1, value_parts, 1.0)):
        found = jnp.concatenate(parts).T * factor
        for s in range(4):
            target = send_ref if s % 2 else keep_ref
            target[s // 2, ch] = found[s * part : (s + 1) * part].astype(bf16)
        at = half
        first = jnp.zeros((1, width), f32)
        second = jnp.zeros((1, width), f32)
        for r in entries:
            n = r.shape[2] // 2
            piece = found[at : at + n]
            first = first + jnp.sum(piece * r[0, ch, :n].astype(f32), axis=0, keepdims=True)
            second = second + jnp.sum(piece * r[0, ch, n:].astype(f32), axis=0, keepdims=True)
            at += n
        taps_ref[ch, 0:1] = first
        taps_ref[ch, 1:2] = second


def attend_back(micro, query, keys, values, probs, grad, newer, older, before, events=()):
    heads, rows, count = probs.shape
    width = query.shape[1]
    quads = heads // QUAD
    block = width // quads
    entries = newer + older
    operands = (query, keys, values, probs, grad) + tuple(a for a, _ in entries)
    specs = [
        pl.BlockSpec((rows, block), lambda i: (micro, i)),
        pl.BlockSpec((count, block), lambda i: (0, i)),
        pl.BlockSpec((count, block), lambda i: (0, i)),
        pl.BlockSpec((QUAD, rows, count), lambda i: (i, 0, 0)),
        pl.BlockSpec((rows, block), lambda i: (micro, i)),
    ] + source_specs(entries, block)
    alias = {}
    if before is not None:
        alias = {len(operands): 0}
        operands = operands + (before,)
        specs.append(pl.BlockSpec(memory_space=pl.ANY))
    part = count // 8
    return call(
        functools.partial(attend_back_kernel, (len(newer), len(older))),
        (quads,),
        specs,
        [
            pl.BlockSpec((rows, block), lambda i: (micro, i)),
            pl.BlockSpec((2, 2, part, block), lambda i: (0, 0, 0, i)),
            pl.BlockSpec((2, 2, part, block), lambda i: (0, 0, 0, i)),
            pl.BlockSpec((2, 2, block), lambda i: (0, 0, i)),
            pl.BlockSpec((1, QUAD, 128), lambda i: (i, 0, 0)),
        ],
        [
            jax.ShapeDtypeStruct(query.shape, bf16),
            jax.ShapeDtypeStruct((2, 2, part, width), bf16),
            jax.ShapeDtypeStruct((2, 2, part, width), bf16),
            jax.ShapeDtypeStruct((2, 2, width), f32),
            jax.ShapeDtypeStruct((quads, QUAD, 128), f32),
        ],
        operands,
        8 * rows * count * width * 4,
        alias=alias,
        events=events,
    )


def gelu_pair(inputs):
    size = jnp.abs(inputs)
    t = 1.0 / (1.0 + (0.3275911 * 0.5**0.5) * size)
    bell = jnp.exp(-0.5 * inputs * inputs)
    tail = (
        t
        * (
            0.5 * 0.254829592
            + t
            * (
                0.5 * -0.284496736
                + t * (0.5 * 1.421413741 + t * (0.5 * -1.453152027 + t * (0.5 * 1.061405429)))
            )
        )
        * bell
    )
    share = jnp.where(inputs > 0.0, 1.0 - tail, tail)
    return inputs * share, share + inputs * bell * 0.3989422804014327


def mlp_weights(width, units, count):
    return [
        pltpu.VMEM((width, width), bf16),
        pltpu.VMEM((width, 2 * units), bf16),
        pltpu.SemaphoreType.DMA((count,)),
        pltpu.SemaphoreType.DMA((count,)),
    ]


def mlp_kernel(count, attended_ref, embedded_ref, vec_ref, select_ref, *refs):
    (
        first_ref, normed_ref, active_ref, slope_ref, second_ref, feature_ref,
        out_s, both_s, out_sems, sems,
    ) = refs[count:]
    units = both_s.shape[1] // 2
    out_copies = transfers(refs[:count], ((2 * units, out_s),), out_sems)
    copies = transfers(refs[:count], ((0, both_s),), sems)
    starting = pl.program_id(0) == 0

    @pl.when(starting)
    def _():
        begin(out_copies)
        begin(copies)
        finish(out_copies)

    first = embedded_ref[...] + contract_last(attended_ref[...], out_s[...])
    first_ref[...] = first
    unit, _ = standard(first)
    normed = (unit * vec_ref[3:4] + vec_ref[4:5]).astype(bf16)
    normed_ref[...] = normed
    total = first

    @pl.when(starting)
    def _():
        finish(copies)

    chunk = units // 4

    def entry(s):
        return product(normed, both_s[:, (2 * s + 1) * chunk : (2 * s + 2) * chunk])

    following = entry(0)
    for s in range(4):
        at = s * chunk
        hidden = following
        if s < 3:
            following = entry(s + 1)
        value, slope = gelu_pair(hidden)
        value = value.astype(bf16)
        active_ref[:, at : at + chunk] = value
        slope_ref[:, at : at + chunk] = slope.astype(bf16)
        total = total + contract_last(value, both_s[:, 2 * at : 2 * at + chunk])
    second_ref[...] = total
    unit, _ = standard(total)
    final = unit * vec_ref[5:6] + vec_ref[6:7]
    feature_ref[0] = jnp.dot(
        select_ref[0], final, precision=PRECISE, preferred_element_type=f32
    )


def mlp(attended, embedded, vec, select, weights, events=()):
    total, width = embedded.shape
    rows = total // MICRO
    units = (weights[0].shape[1] - width) // 2
    boxes = select.shape[1]

    def tile(columns):
        return pl.BlockSpec((rows, columns), lambda i: (i, 0))

    return call(
        functools.partial(mlp_kernel, len(weights)),
        (MICRO,),
        [
            tile(width),
            tile(width),
            whole(vec),
            pl.BlockSpec((1, boxes, rows), lambda i: (i, 0, 0)),
        ]
        + [pl.BlockSpec(memory_space=pl.ANY)] * len(weights),
        [tile(width), tile(width), tile(units), tile(units), tile(width)]
        + [pl.BlockSpec((1, boxes, width), lambda i: (i, 0, 0))],
        [
            jax.ShapeDtypeStruct((total, width), f32),
            jax.ShapeDtypeStruct((total, width), bf16),
            jax.ShapeDtypeStruct((total, units), bf16),
            jax.ShapeDtypeStruct((total, units), bf16),
            jax.ShapeDtypeStruct((total, width), f32),
            jax.ShapeDtypeStruct((MICRO, boxes, width), f32),
        ],
        (attended, embedded, vec, select) + weights,
        2 * total * width * (width + 2 * units),
        scratch=mlp_weights(width, units, len(weights)),
        events=events,
    )


def mlp_back_kernel(
    count, pull_ref, select_ref, second_ref, first_ref, slope_ref, vec_ref, *refs
):
    (
        branch_ref, hidden_ref, attn_ref, first_grad_ref, attended_ref, sums_ref,
        out_s, both_s, out_sems, sems,
    ) = refs[count:]
    units = both_s.shape[1] // 2
    out_copies = transfers(refs[:count], ((2 * units, out_s),), out_sems)
    copies = transfers(refs[:count], ((0, both_s),), sems)
    starting = pl.program_id(0) == 0

    @pl.when(starting)
    def _():
        begin(copies)
        begin(out_copies)
        sums_ref[...] = jnp.zeros_like(sums_ref)

    pull = lax.dot_general(
        select_ref[0],
        pull_ref[0],
        (((0,), (0,)), ((), ())),
        precision=PRECISE,
        preferred_element_type=f32,
    )
    unit, scale = standard(second_ref[...])
    sums_ref[2:3] += jnp.sum(pull * unit, axis=0, keepdims=True)
    sums_ref[3:4] += jnp.sum(pull, axis=0, keepdims=True)
    second_grad = standard_back(pull * vec_ref[5:6], unit, scale)
    branch = second_grad.astype(bf16)
    branch_ref[...] = branch

    @pl.when(starting)
    def _():
        finish(copies)

    chunk = units // 4
    normed_grad = jnp.zeros(second_grad.shape, f32)

    for s in range(4):
        at = s * chunk
        active_grad = product(branch, both_s[:, 2 * at : 2 * at + chunk])
        hidden_grad = (active_grad * slope_ref[:, at : at + chunk].astype(f32)).astype(bf16)
        hidden_ref[:, at : at + chunk] = hidden_grad
        normed_grad = normed_grad + contract_last(
            hidden_grad, both_s[:, 2 * at + chunk : 2 * at + 2 * chunk]
        )

    @pl.when(starting)
    def _():
        finish(out_copies)

    unit, scale = standard(first_ref[...])
    sums_ref[0:1] += jnp.sum(normed_grad * unit, axis=0, keepdims=True)
    sums_ref[1:2] += jnp.sum(normed_grad, axis=0, keepdims=True)
    first_grad = standard_back(normed_grad * vec_ref[3:4], unit, scale) + second_grad
    first_grad_ref[...] = first_grad
    attn = first_grad.astype(bf16)
    attn_ref[...] = attn
    attended_ref[...] = product(attn, out_s[...]).astype(bf16)


def mlp_back(pull, select, second, first, slope, vec, weights, events=()):
    total, width = second.shape
    rows = total // MICRO
    units = (weights[0].shape[1] - width) // 2
    boxes = select.shape[1]

    def tile(columns):
        return pl.BlockSpec((rows, columns), lambda i: (i, 0))

    return call(
        functools.partial(mlp_back_kernel, len(weights)),
        (MICRO,),
        [
            pl.BlockSpec((1, boxes, width), lambda i: (i, 0, 0)),
            pl.BlockSpec((1, boxes, rows), lambda i: (i, 0, 0)),
            tile(width),
            tile(width),
            tile(units),
            whole(vec),
        ]
        + [pl.BlockSpec(memory_space=pl.ANY)] * len(weights),
        [tile(width), tile(units), tile(width), tile(width), tile(width)]
        + [pl.BlockSpec((8, width), lambda i: (0, 0))],
        [
            jax.ShapeDtypeStruct((total, width), bf16),
            jax.ShapeDtypeStruct((total, units), bf16),
            jax.ShapeDtypeStruct((total, width), bf16),
            jax.ShapeDtypeStruct((total, width), f32),
            jax.ShapeDtypeStruct((total, width), bf16),
            jax.ShapeDtypeStruct((8, width), f32),
        ],
        (pull, select, second, first, slope, vec) + weights,
        2 * total * width * (width + 2 * units),
        scratch=mlp_weights(width, units, len(weights)),
        events=events,
    )


def embed_back_kernel(
    count, dq_ref, key_ref, value_ref, taps_ref, embedded_ref, first_ref, normed_ref, patch_ref,
    vec_ref, head_ref, more_ref, *refs
):
    pools = refs[: 3 * MICRO]
    (
        near_ref, far_ref, taps_out, qk_s, v_s, pool_s, sums_s, normed_s, projected_s, grad_s,
        patch_s, sems,
    ) = refs[3 * MICRO + count :]
    rows, width = embedded_ref.shape
    step = pl.program_id(0)

    @pl.when(step == 0)
    def _():
        sums_s[...] = jnp.zeros_like(sums_s)
        sums_s[3:7] = more_ref[0:4]
        sums_s[8 : 8 + head_ref.shape[0]] = head_ref[...]
        taps_out[...] = jnp.zeros_like(taps_out)
        patch_s[...] = jnp.zeros_like(patch_s)
        for m in range(MICRO):
            kept, got, far = pools[3 * m : 3 * m + 3]
            for ch in range(2):
                pool_s[m, ch] = (
                    kept[0, ch].astype(f32) + got[0, ch].astype(f32) + far[ch].astype(f32)
                )
        fetch(refs[3 * MICRO : 3 * MICRO + count], ((0, qk_s), (2 * width, v_s)), sems)

    at = pl.multiple_of(step * rows, 128)
    here = pl.ds(at, rows)
    projected_s[here, :width] = dq_ref[...]
    pooled = rows // 4
    for ch, raw_ref in ((0, key_ref), (1, value_ref)):
        pool = pool_s[step, ch]
        for t in range(4):
            projected_s[
                pl.ds(at + t * pooled, pooled), (1 + ch) * width : (2 + ch) * width
            ] = (pool * taps_ref[ch, t : t + 1]).astype(bf16)
            raw = raw_ref[t * pooled : (t + 1) * pooled].astype(f32)
            taps_out[4 * ch + t : 4 * ch + t + 1] += jnp.sum(pool * raw, axis=0, keepdims=True)
    normed_grad = contract_last(projected_s[here, : 2 * width], qk_s[...])
    normed_grad = normed_grad + contract_last(projected_s[here, 2 * width :], v_s[...])
    unit, scale = standard(embedded_ref[...])
    sums_s[1:2] += jnp.sum(normed_grad * unit, axis=0, keepdims=True)
    sums_s[2:3] += jnp.sum(normed_grad, axis=0, keepdims=True)
    grad = standard_back(normed_grad * vec_ref[1:2], unit, scale) + first_ref[...]
    grad = grad.astype(bf16)
    sums_s[0:1] += jnp.sum(grad.astype(f32), axis=0, keepdims=True)
    normed_s[:, here] = normed_ref[...].T
    grad_s[:, here] = grad.T
    patch_s[here, : patch_ref.shape[1]] = patch_ref[...]

    @pl.when(step == MICRO - 1)
    def _():
        half = width // 2
        edge = 3 * width + patch_s.shape[1]
        for out_ref, top in ((far_ref, half), (near_ref, 0)):
            part = slice(top, top + half)
            for c in range(3):
                out_ref[:, c * width : (c + 1) * width] = product(
                    normed_s[part], projected_s[:, c * width : (c + 1) * width]
                ).astype(bf16)
            out_ref[:, 3 * width : edge] = product(grad_s[part], patch_s[...]).astype(bf16)
            out_ref[:, edge:] = sums_s[:, part].T.astype(bf16)


def embed_back(
    dq, keys, values, taps, embedded, first_grad, normed, patches, vec, head, more, pools, weights,
    events=(),
):
    total, width = embedded.shape
    rows = total // MICRO
    patch = patches.shape[1]
    edge = patch + (-patch % 128)
    columns = 3 * width + edge + 128

    def tile(columns):
        return pl.BlockSpec((rows, columns), lambda i: (i, 0))

    operands = (dq, keys, values, taps, embedded, first_grad, normed, patches, vec, head, more)
    half = pl.BlockSpec((width // 2, columns), lambda i: (0, 0))
    return call(
        functools.partial(embed_back_kernel, len(weights)),
        (MICRO,),
        [tile(width)] * 3
        + [whole(taps)]
        + [tile(width)] * 3
        + [tile(patch)]
        + [whole(a) for a in (vec, head, more) + pools]
        + [pl.BlockSpec(memory_space=pl.ANY)] * len(weights),
        [half, half, pl.BlockSpec((8, width), lambda i: (0, 0))],
        [
            jax.ShapeDtypeStruct((width // 2, columns), bf16),
            jax.ShapeDtypeStruct((width // 2, columns), bf16),
            jax.ShapeDtypeStruct((8, width), f32),
        ],
        operands + pools + weights,
        2 * total * width * 3 * width,
        scratch=[
            pltpu.VMEM((width, 2 * width), bf16),
            pltpu.VMEM((width, width), bf16),
            pltpu.VMEM((MICRO, 2, rows // 4, width), f32),
            pltpu.VMEM((128, width), f32),
            pltpu.VMEM((width, total), bf16),
            pltpu.VMEM((total, 3 * width), bf16),
            pltpu.VMEM((width, total), bf16),
            pltpu.VMEM((total, edge), bf16),
            pltpu.SemaphoreType.DMA((2 * len(weights),)),
        ],
        events=events,
    )


def squares_kernel(*refs):
    grads, flat_ref, outs = refs[:6], refs[6], refs[7:]
    total = 0.0
    for i in range(3):
        found = grads[2 * i][...].astype(f32) + grads[2 * i + 1][...].astype(f32)
        outs[i][...] = found
        total = total + jnp.sum(found * found)
    rows = flat_ref.shape[0]
    outs[3][...] = jnp.zeros_like(outs[3]) + total
    outs[3][:rows] = flat_ref[...]


def squares_of(attn, small, rest, flat):
    operands = tuple(attn) + tuple(small) + tuple(rest) + (flat,)
    rows = flat.shape[0] + (-flat.shape[0] % 8)
    rows += 8 * (rows == flat.shape[0])
    shapes = [jax.ShapeDtypeStruct(g[0].shape, f32) for g in (attn, small, rest)]
    shapes.append(jax.ShapeDtypeStruct((rows, flat.shape[1]), f32))
    return call(
        squares_kernel,
        (1,),
        [whole(o) for o in operands],
        [whole(o) for o in shapes],
        shapes,
        operands,
        0,
    )


def update_kernel(rates, patch, odd_ref, one_ref, two_ref, *refs):
    count = len(rates)
    attn_ref, small_ref, rest_ref = refs[:3]
    weights, moments, averages = (refs[3 + i * count : 3 + (i + 1) * count] for i in range(3))
    outs = refs[3 + 3 * count :]
    heads = weights[6].shape[0] * 3
    blocks = []
    square = one_ref[52:53, 0:1] + two_ref[52:53, 0:1]
    spot = lax.broadcasted_iota(jnp.int32, (13, one_ref.shape[1]), 1)
    row = lax.broadcasted_iota(jnp.int32, (13, one_ref.shape[1]), 0)
    counted = (row < 12) | (spot < heads)
    for c in range(4):
        far = 13 * (c ^ 2)
        block = one_ref[13 * c : 13 * c + 13] + two_ref[far : far + 13]
        kept = jnp.where(counted, block, 0.0)
        square = square + jnp.sum(kept * kept)
        blocks.append(block)
    mine = jnp.where(odd_ref[0] == 1, blocks[1], blocks[0])
    boxes = blocks[0][12:13, heads + 1 : heads + 2]
    norm = jnp.sqrt(square) / boxes
    lane = lax.broadcasted_iota(jnp.int32, (1, 128), 1)
    loss = blocks[0][12:13, heads : heads + 1]
    outs[0][...] = jnp.where(lane == 0, loss, jnp.where(lane == 1, boxes, norm))
    scaling = jnp.minimum(1.0, THRESHOLD / norm) / boxes
    hidden = weights[0].shape[1] - attn_ref.shape[1]
    edge = small_ref.shape[1] - 128
    classes = weights[3].shape[1]
    tail = small_ref[:, edge:]

    def step(i, at, grad):
        grad = grad * scaling
        moment = MOMENTUM * moments[i][at] + grad
        updated = weights[i][at] - rates[i] * (grad + MOMENTUM * moment)
        outs[1 + i][at] = updated
        outs[1 + count + i][at] = moment
        outs[1 + 2 * count + i][at] = AVERAGING * averages[i][at] + (1.0 - AVERAGING) * updated
        if i < 2:
            outs[1 + 3 * count + i][at] = updated.astype(bf16)

    step(0, ..., jnp.concatenate([attn_ref[...], rest_ref[:, :hidden]], axis=1))
    step(1, ..., rest_ref[:, hidden:])
    step(2, ..., small_ref[:, :patch])
    step(3, ..., tail[:, 8 : 8 + classes])
    step(4, ..., tail.T[:7])
    for t in range(6):
        step(5, t, mine[2 * t : 2 * t + 2])
    for h in range(heads // 3):
        step(6, slice(h, h + 1), mine[12:13, 3 * h : 3 * h + 3])


def update(odd, one, two, grads, patch, weights, moments, averages, rates):
    operands = (odd, one, two) + grads + weights + moments + averages
    kept = [jax.ShapeDtypeStruct(w.shape, f32) for w in weights]
    shapes = [jax.ShapeDtypeStruct((1, 128), f32)] + kept * 3
    shapes = shapes + [jax.ShapeDtypeStruct(w.shape, bf16) for w in weights[:2]]
    return call(
        functools.partial(update_kernel, rates, patch),
        (1,),
        [pl.BlockSpec(memory_space=pltpu.SMEM)] + [whole(o) for o in operands[1:]],
        [pl.BlockSpec(o.shape, lambda i, n=len(o.shape): (0,) * n) for o in shapes],
        shapes,
        operands,
        0,
    )


def one_hot_rows(index, count):
    return (index[:, None] == jnp.arange(count)[None, :]).astype(bf16)


def shards(
    patches,
    clip_len,
    box_count,
    box_bounds,
    box_labels,
    memory,
    up_weight,
    down_weight,
    embed_weight,
    head_weight,
    vector_weight,
    conv_weight,
    position_bias,
    up_moment,
    down_moment,
    embed_moment,
    head_moment,
    vector_moment,
    conv_moment,
    position_moment,
    up_average,
    down_average,
    embed_average,
    head_average,
    vector_average,
    conv_average,
    position_average,
):
    dp_index = lax.axis_index("dp")
    mp_index = lax.axis_index("mp")
    dp_count = lax.axis_size("dp")
    across, core = mp_index % 2, dp_index % 2
    upper = mp_index - across
    quarter = 2 * core + across
    rows = patches.shape[1]
    eighth = rows // 8
    pooled = rows // 4
    half_pool = pooled // 2
    head_cols = conv_weight.shape[2]
    width = 4 * head_cols
    sub = embed_weight.shape[1]
    patch = embed_weight.shape[0]
    classes = head_weight.shape[0]
    boxes = box_bounds.shape[2]
    own_heads = position_bias.shape[0]
    heads = own_heads * 4
    hidden_cols = up_weight.shape[1] - 3 * head_cols

    ints = jnp.concatenate(
        [clip_len.reshape(-1), box_count.reshape(-1), box_bounds.reshape(-1), box_labels.reshape(-1)]
    )
    total_ints = ints.shape[0]
    ints = jnp.pad(ints, (0, -total_ints % 1024)).reshape(-1, 128)
    ints = regroup(ints).reshape(-1)
    lengths_all = ints[:5]
    counts = ints[5:8]
    bounds = ints[8 : 8 + MICRO * boxes * 2].reshape(MICRO, boxes, 2)
    labels = ints[8 + MICRO * boxes * 2 : total_ints].reshape(MICRO * boxes, classes)

    def in_three(array):
        high = lax.reduce_precision(array, 8, 7)
        middle = lax.reduce_precision(array - high, 8, 7)
        return [high, middle, array - high - middle]

    edge = patch + (-patch % 128)
    columns_in = [jnp.pad(embed_weight, ((0, edge - patch), (0, 0)))]
    columns_in += [jnp.pad(v, ((0, 1), (0, 0))) for v in in_three(vector_weight)]
    columns_in += [jnp.pad(head_weight, ((0, 128 - 24 - classes), (0, 0)))]
    taps_pos = jnp.concatenate(
        [
            conv_weight.reshape(12, head_cols),
            jnp.pad(position_bias.reshape(1, -1), ((0, 0), (0, head_cols - position_bias.size))),
        ]
    )
    taps_pos = jnp.concatenate(in_three(taps_pos)).reshape(sub, -1)
    small = jnp.concatenate([jnp.concatenate(columns_in).T, taps_pos], axis=1).astype(bf16)
    strip = -(-small.shape[1] // 512) * 128
    small = jnp.pad(small, ((0, 0), (0, 4 * strip - small.shape[1])))
    small = jnp.concatenate([small[:, i * strip : (i + 1) * strip] for i in range(4)])
    up_low = up_weight.astype(bf16)
    down_low = down_weight.astype(bf16)
    pieces = gather_mp(jnp.concatenate([up_low[:, : 3 * head_cols], small], axis=1))
    place = jnp.arange(16 * sub)
    source = (
        (((place // sub) % 4) ^ mp_index) * 4 * sub + place // (4 * sub) * sub + place % sub
    )
    small = product(
        one_hot_rows(source, 16 * sub), jnp.concatenate([p[:, 3 * head_cols :] for p in pieces])
    ).astype(bf16)
    small = jnp.concatenate(
        [small[i * 4 * sub : (i + 1) * 4 * sub] for i in range(4)], axis=1
    )
    small_mine = small[:, : edge + 128]
    taps_pos = small[:, edge + 128 : edge + 128 + 39 * head_cols // sub]
    taps_pos = jnp.sum(taps_pos.reshape(4, 3, 13, head_cols).astype(f32), axis=1)
    taps_pos = jnp.where(upper == 2, jnp.roll(taps_pos, 2, axis=0), taps_pos)
    conv_all = taps_pos[:, :12].transpose(1, 0, 2).reshape(2, 6, width)
    rel_bias = taps_pos[:, 12, : position_bias.size].reshape(heads, 3)
    weights = jnp.concatenate(
        [p[:, j * head_cols : (j + 1) * head_cols] for j in range(3) for p in pick(pieces)]
        + [small_mine],
        axis=1,
    )
    weights = spread_core(spread_dp(weights))
    patches_t = regroup(after(patches.transpose(0, 2, 1), *pieces))
    pieces = gather_mp(
        after(
            jnp.concatenate(
                [down_low[:, head_cols:], up_low[:, 3 * head_cols :], down_low[:, :head_cols]],
                axis=1,
            ),
            patches_t,
        )
    )

    place = jnp.arange(rows)
    token = 8 * (place % eighth) + 4 * ((place // eighth) % 2) + place // (2 * eighth)
    token_order = one_hot_rows(token, rows)
    mem_rows = memory.shape[2]
    half_mem = mem_rows // 2
    mem_place = jnp.arange(mem_rows)
    mem_order = one_hot_rows(2 * (mem_place % half_mem) + mem_place // half_mem, mem_rows)
    part_quarter = [2 * (core ^ (s % 2)) + (across ^ (s // 2)) for s in range(4)]
    pool_place = jnp.arange(pooled)
    pool_token = 2 * (pool_place % half_pool) + pool_place // half_pool
    now_index = jnp.concatenate([pq * pooled + pool_token for pq in part_quarter])
    pool_index = jnp.concatenate([pq * half_pool + jnp.arange(half_pool) for pq in part_quarter])
    mem_index = jnp.arange(half_mem)

    def key_bias(m):
        sides = [
            (now_index, lengths_all[2 + m] // 4),
            (mem_index if m == 0 else pool_index, lengths_all[1 + m] // 8),
            (mem_index if m < 2 else pool_index, lengths_all[m] // 8),
        ]
        return jnp.concatenate(
            [
                jnp.where((index < limit)[None, :], rel_bias[:, g : g + 1], -1e30)
                for g, (index, limit) in enumerate(sides)
            ],
            axis=1,
        ).reshape(heads // QUAD, QUAD, -1)

    biases = [key_bias(m) for m in range(MICRO)]

    (
        patches_in,
        embedded,
        normed,
        query,
        raw_keys,
        raw_values,
        pools,
        vectors,
        head_low,
    ) = embed(patches_t, token_order, conv_all, weights, classes)
    two = swap_mp(pools, 1)
    rest = join(2 * hidden_cols, across[None], [after(p, pools) for p in pieces])
    rest = [rest, swap_dp(rest, 2), swap_dp(rest, 4)]
    rest_late = after(rest[0], *rest[1:])
    rest_late = [swap_dp(rest_late, b) for b in range(6, dp_count, 2)]
    gathered = (pools, swap_dp(pools, 1), two, swap_dp(after(two, *biases), 1))
    stored = [[(a, m) for a in gathered] for m in range(MICRO)]
    memory_t = regroup(after(memory.transpose(0, 1, 3, 2), rest[0]))
    mem_two = swap_mp(after(memory_t, two), 1)
    stored = [None, None] + stored

    attended, saved = None, {}
    for m in (2, 1, 0):
        attended, probs, keys, values = attend(
            m, query, conv_all, biases[m], stored[m + 2], stored[m + 1], stored[m], attended,
            events=tuple(rest_late) if m == 0 else (),
        ) if m < 2 else attend(
            m, after(query, *rest[1:]), conv_all, biases[m], stored[m + 2], stored[m + 1], stored[m], attended,
        )
        saved[m] = (keys, values, probs)
        if m == 2:
            rest_core = [swap_dp(after(p, attended), 1) for p in rest]
        if m == 1:
            late_core = [swap_dp(after(p, attended), 1) for p in rest_late]
        if m > 1:
            mem_two = after(mem_two, attended)
            mem_parts = (
                memory_t,
                swap_dp(after(memory_t, attended), 1),
                mem_two,
                swap_dp(mem_two, 1),
            )
            mem_full = memory_in(
                jnp.stack(
                    [
                        (((c ^ upper) // 2) ^ core) + 2 * (((c ^ upper) % 2) ^ across)
                        for c in range(4)
                    ]
                ),
                mem_order,
                mem_parts,
            )
            stored[:2] = [[(mem_full, 0)], [(mem_full, 1)]]
    rest = one_or_all(rest + rest_late + rest_core + late_core)

    position = quarter * rows + token
    within = position % FRAME
    live = position[None, :] < lengths_all[2:, None]
    inside = (
        (within[None, None, :] >= bounds[:, :, 0:1])
        & (within[None, None, :] < bounds[:, :, 1:2])
        & live[:, None, :]
    )
    denominator = ((bounds[:, :, 1] - bounds[:, :, 0]) * (lengths_all[2:, None] // FRAME)).astype(
        f32
    )
    select = inside.astype(f32) / denominator[:, :, None]
    first_res, normed_mlp, active, slope, second_res, feature = mlp(
        attended, embedded, vectors, select, rest
    )
    target_row = jnp.arange(4 * pooled)
    target_quarter, target_rest = target_row // pooled, target_row % pooled
    source_row = (
        (((target_quarter // 2) ^ core) + 2 * ((target_quarter % 2) ^ across)) * pooled
        + (target_rest % 2) * half_pool
        + target_rest // 2
    )
    new_memory = memory_out(
        (quarter ^ upper)[None],
        one_hot_rows(source_row, 4 * pooled).T,
        stored[3] + stored[4],
        events=(feature,),
    )
    feature = feature.reshape(MICRO * boxes, width)
    feature = group_sum_features(feature).astype(bf16)
    logits = contract_last(feature, head_low)
    target = labels.astype(f32)
    keep = (jnp.arange(boxes)[None, :] < counts[:, None]).astype(f32).reshape(-1, 1)
    lead = (quarter == 0).astype(f32)
    loss_part = jnp.sum((jax.nn.softplus(logits) - target * logits) * keep) * lead
    grad_logits = ((jax.nn.sigmoid(logits) - target) * keep).astype(bf16)

    grad_head = contract_rows(grad_logits, feature) * lead
    grad_feature = product(grad_logits, head_low).reshape(MICRO, boxes, width)
    grad_branch, grad_hidden, grad_attn, grad_first, grad_attended, sums = mlp_back(
        grad_feature, select, second_res, first_res, slope, vectors, rest, (new_memory,)
    )
    new_memory = regroup(new_memory)
    grad_branch = after(grad_branch, new_memory)

    half = width // 2

    def weight_grad(left, right, at):
        return contract_rows(left[:, at : at + half], right).astype(bf16)

    sides = ((grad_branch, active), (normed_mlp, grad_hidden), (grad_attn, attended))
    rest_far = [weight_grad(*side, half) for side in sides]
    rest_near = [weight_grad(*side, 0) for side in sides]
    rest_pieces = halve_dp(rest_near, rest_far)

    dq, pool_grads, bias_grad, mem_taps = None, [], 0.0, 0.0
    events = tuple(rest_pieces)
    rest_found = trade_dp(rest_pieces, 1, 3)
    for m in range(MICRO):
        keys, values, probs = saved[m]
        dq, kept, sent, taps_part, bias_part = attend_back(
            m, query, keys, values, probs, grad_attended, stored[m + 1], stored[m], dq, events
        )
        got = swap_dp(sent, 1)
        away = (kept[1].astype(f32) + got[1].astype(f32)).astype(bf16)
        pool_grads.extend([kept, got, swap_mp(away, 1)])
        bias_grad = bias_grad + bias_part
        mem_taps = mem_taps + taps_part
        events = (away,)
        if m == 1:
            events = (away, pool_grads[2]) + tuple(rest_found)
            rest_pieces[3:] = [after(p, *rest_found) for p in rest_pieces[3:]]
            rest_found += trade_dp(rest_pieces, 3, None)
    rest_total = sum((f.astype(f32) for f in rest_found), rest_pieces[0].astype(f32))
    units = 4 * hidden_cols
    rest_pieces = []
    out_blocks = pick(
        [
            rest_total[:, 2 * units + c * head_cols : 2 * units + (c + 1) * head_cols]
            for c in range(4)
        ]
    )
    for s in range(4):
        piece = jnp.concatenate(
            [
                rest_total[:, units + s * hidden_cols : units + (s + 1) * hidden_cols],
                out_blocks[s],
                rest_total[:, s * hidden_cols : (s + 1) * hidden_cols],
            ],
            axis=1,
        )
        rest_pieces.append(piece)
    rest_near, rest_far, rest_got = halve_mp(rest_pieces)
    attn_near, attn_far, taps_grad = embed_back(
        dq,
        raw_keys,
        raw_values,
        conv_all,
        embedded,
        grad_first,
        normed,
        patches_in,
        vectors,
        grad_head,
        sums,
        tuple(pool_grads),
        weights,
        events=(rest_near,) + rest_far,
    )
    attn_pieces = halve_dp([attn_near], [attn_far])
    attn_found = trade_dp(attn_pieces, 1, None)
    rest_got = after(rest_got, *attn_pieces)
    columns = rest_near.shape[1]
    far = (rest_far[0].astype(f32) + rest_got[:, columns:].astype(f32)).astype(bf16)
    rest_mine = (rest_near + rest_got[:, :columns].astype(f32), swap_mp(far, 2))
    attn_found[-1] = after(attn_found[-1], far)
    attn_total = sum((f.astype(f32) for f in attn_found), attn_pieces[0].astype(f32))
    small_total = attn_total[:, 3 * width :]
    small_parts = halve_more(*halve_mp(
        [
            lax.dynamic_slice_in_dim(small_total, (mp_index ^ s) * sub, sub, axis=0)
            for s in range(4)
        ]
    ))
    attn_parts = halve_more(*halve_mp(
        pick(
            [
                jnp.concatenate(
                    [
                        attn_total[:, (4 * j + c) * head_cols : (4 * j + c + 1) * head_cols]
                        for j in range(3)
                    ],
                    axis=1,
                )
                for c in range(4)
            ]
        )
    ))

    count_local = jnp.sum(box_count).astype(f32) * (mp_index == 0).astype(f32)
    taps_rows = jnp.stack(
        [
            jnp.concatenate([taps_grad[4 * ch : 4 * ch + 4], mem_taps[ch]], axis=0)
            for ch in range(2)
        ],
        axis=1,
    ).reshape(12, 4, head_cols)
    scalars = jnp.stack([loss_part, count_local])
    last = jnp.concatenate(
        [
            bias_grad.reshape(heads, 128)[:, :3].reshape(4, -1),
            jnp.broadcast_to(scalars[None], (4, 2)),
        ],
        axis=1,
    )
    last = jnp.pad(last, ((0, 0), (0, head_cols - last.shape[1])))
    flat = jnp.concatenate([taps_rows, last[None]]).transpose(1, 0, 2)
    attn_mine, small_mine, rest_mine, both = squares_of(
        attn_parts, small_parts, rest_mine, flat.reshape(52, head_cols)
    )
    for bit in range(dp_bits()):
        both = both + swap_dp(both, 1 << bit)
    both = both + swap_mp(both, 1)
    both_two = swap_mp(both, 2)

    def turned(arrays):
        up, down, embed_part, head, vector, conv, position = arrays
        return (up, down, embed_part.T, head.T, vector, conv.transpose(1, 0, 2), position)

    masters = (
        up_weight,
        down_weight,
        embed_weight,
        head_weight,
        vector_weight,
        conv_weight,
        position_bias,
    )
    moments = (
        up_moment,
        down_moment,
        embed_moment,
        head_moment,
        vector_moment,
        conv_moment,
        position_moment,
    )
    averages = (
        up_average,
        down_average,
        embed_average,
        head_average,
        vector_average,
        conv_average,
        position_average,
    )
    rates = (LEARNING,) * 4 + (VECTOR_LEARNING,) * 3
    made = update(
        across[None],
        both,
        both_two,
        (attn_mine, small_mine, rest_mine),
        patch,
        turned(masters),
        turned(moments),
        turned(averages),
        rates,
    )
    loss_global, box_total, grad_norm = (made[0][0, i] for i in range(3))
    results = []
    for i in range(3):
        results.extend(turned(made[1 + 7 * i : 8 + 7 * i]))

    return (
        (loss_global, box_total, grad_norm, new_memory.transpose(0, 1, 3, 2)) + tuple(results) + tuple(made[22:24])
    )


def solution(mesh):
    both = ("dp", "mp")
    weight_specs = (
        P("dp", "mp"),
        P("dp", "mp"),
        P(None, both),
        P(None, both),
        P(None, both),
        P(None, None, "mp"),
        P("mp", None),
    )
    memory_spec = P(None, None, "dp", "mp")
    return jax.shard_map(
        shards,
        mesh=mesh,
        in_specs=(
            P(None, both, None),
            P("dp", None),
            P("dp", None),
            P("dp", None, None, None),
            P("dp", None, None, None),
            memory_spec,
        )
        + weight_specs * 3,
        out_specs=(P(), P(), P(), memory_spec)
        + weight_specs * 3
        + (P("dp", "mp"), P("dp", "mp")),
        check_vma=False,
    )
```

```python
import functools

import jax
import jax.numpy as jnp
from jax import lax
from jax.experimental import pallas as pl
from jax.experimental.pallas import tpu as pltpu
from jax.sharding import PartitionSpec as P

MICRO = 3
FRAME = 64
EPSILON = 1e-06
LEARNING = 300.0
VECTOR_LEARNING = 6000.0
MOMENTUM = 0.5
AVERAGING = 0.5
THRESHOLD = 0.05
PRECISE = lax.Precision.HIGHEST
QUAD = 4
bf16 = jnp.bfloat16
f32 = jnp.float32


NEAR = 60 * 1024 * 1024


def product(first_operand, second_operand):
    return jnp.dot(first_operand, second_operand, preferred_element_type=f32)


def contract_last(first_operand, second_operand):
    return lax.dot_general(
        first_operand, second_operand, (((1,), (1,)), ((), ())), preferred_element_type=f32
    )


def contract_rows(first_operand, second_operand):
    return lax.dot_general(
        first_operand, second_operand, (((0,), (0,)), ((), ())), preferred_element_type=f32
    )


def swap_dp(inputs, mask):
    size = lax.axis_size("dp")
    return lax.ppermute(inputs, "dp", [(i, i ^ mask) for i in range(size)])


def swap_mp(inputs, mask):
    size = lax.axis_size("mp")
    return lax.ppermute(inputs, "mp", [(i, i ^ mask) for i in range(size)])


def dp_bits():
    return lax.axis_size("dp").bit_length() - 1


def regroup(inputs):
    count = lax.axis_size("dp")
    pairs = []
    for d in range(count):
        for z in range(4):
            moved = (d % 2) ^ (z // 2)
            pairs.append((d * 4 + z, (d ^ moved) * 4 + (z ^ (2 * moved))))
    return lax.ppermute(inputs, ("dp", "mp"), pairs)


def pick(pieces):
    odd = lax.axis_index("mp") % 2 == 1
    return [jnp.where(odd, pieces[c ^ 1], pieces[c]) for c in range(4)]


def gather_mp(inputs):
    return [inputs] + [swap_mp(inputs, s) for s in (1, 2, 3)]


def halve_mp(pieces):
    sent = jnp.concatenate([pieces[1], pieces[3]], axis=1).astype(bf16)
    return pieces[0], (pieces[2], sent), swap_mp(sent, 1)


def halve_more(near, far, got):
    columns = near.shape[1]
    far = far[0].astype(f32) + got[:, columns:].astype(f32)
    return near.astype(f32) + got[:, :columns].astype(f32), swap_mp(far.astype(bf16), 2)


def spread_dp(inputs):
    return [inputs] + [swap_dp(inputs, b) for b in range(2, lax.axis_size("dp"), 2)]


def spread_core(pieces):
    return one_or_all(pieces + [swap_dp(p, 1) for p in pieces])


def one_or_all(pieces):
    if pieces[0].shape[0] % 16:
        pieces = [jnp.concatenate(pieces)]
    return tuple(pieces)


def halve_dp(near, far):
    got = [swap_dp(f, 1) for f in far]
    count = lax.axis_size("dp") // 2
    rows = near[0].shape[0] // count
    return [
        jnp.concatenate(
            [
                n[i * rows : (i + 1) * rows].astype(f32) + g[i * rows : (i + 1) * rows].astype(f32)
                for n, g in zip(near, got)
            ],
            axis=1,
        ).astype(bf16)
        for i in range(count)
    ]


def trade_dp(pieces, first, last):
    return [swap_dp(piece, 2 * first + 2 * i) for i, piece in enumerate(pieces[first:last])]


def after(value, *events):
    return lax.optimization_barrier((value,) + events)[0]


def group_sum_features(inputs):
    count = lax.axis_size("dp")
    width = inputs.shape[1] // count
    order = [b for b in range(count) if b % 2 == 0] + [b for b in range(count) if b % 2]
    at = [order.index(b ^ 1) for b in order]
    got = swap_dp(inputs, 1)
    inputs = inputs + jnp.concatenate([got[:, p * width : (p + 1) * width] for p in at], axis=1)
    return inputs + swap_mp(inputs, 1)


def call(
    body, grid, in_specs, out_specs, out_shape, operands, flops, scratch=(), alias=None, events=()
):
    known, late = len(operands), len(operands) + len(events)

    def run(*refs):
        body(*refs[:known], *refs[late:])

    return pl.pallas_call(
        run,
        grid=grid,
        in_specs=list(in_specs) + [pl.BlockSpec(memory_space=pl.ANY)] * len(events),
        out_specs=out_specs,
        out_shape=out_shape,
        scratch_shapes=list(scratch),
        input_output_aliases=alias or {},
        compiler_params=pltpu.CompilerParams(vmem_limit_bytes=NEAR),
        cost_estimate=pl.CostEstimate(flops=1000, bytes_accessed=1000, transcendentals=0),
    )(*operands, *events)


def whole(array):
    return pl.BlockSpec(array.shape, lambda *i, n=len(array.shape): (0,) * n)


def transfers(pieces, targets, sems):
    copies, at = [], 0
    for piece in pieces:
        rows = piece.shape[0]
        for column, target in targets:
            copies.append(
                pltpu.make_async_copy(
                    piece.at[:, column : column + target.shape[1]],
                    target.at[at : at + rows],
                    sems.at[len(copies)],
                )
            )
        at += rows
    return copies


def begin(copies):
    for copy in copies:
        copy.start()


def finish(copies):
    for copy in copies:
        copy.wait()


def fetch(pieces, targets, sems):
    copies = transfers(pieces, targets, sems)
    begin(copies)
    finish(copies)


def standard(inputs):
    centered = inputs - jnp.mean(inputs, axis=-1, keepdims=True)
    scale = lax.rsqrt(jnp.mean(centered * centered, axis=-1, keepdims=True) + EPSILON)
    return centered * scale, scale


def standard_back(grad, unit, scale):
    return scale * (
        grad
        - jnp.mean(grad, axis=-1, keepdims=True)
        - unit * jnp.mean(grad * unit, axis=-1, keepdims=True)
    )


def memory_in_kernel(index_ref, order_ref, *refs):
    parts, (out_ref, held, sems) = refs[:4], refs[4:]
    columns = parts[0].shape[2]

    def copy(p, c):
        target = held.at[:, :, c * columns : (c + 1) * columns]
        return pltpu.make_async_copy(parts[p], target, sems.at[c])

    for c in range(4):
        for p in range(4):

            @pl.when(index_ref[c] == p)
            def _(p=p, c=c):
                copy(p, c).start()

    for c in range(4):
        copy(0, c).wait()
    order = order_ref[...]
    for m in range(2):
        for ch in range(2):
            out_ref[m, ch] = contract_last(order, held[m, ch]).astype(bf16)


def memory_in(index, order, parts, events=()):
    _, _, columns, rows = parts[0].shape
    return call(
        memory_in_kernel,
        (1,),
        [pl.BlockSpec(memory_space=pltpu.SMEM), whole(order)]
        + [pl.BlockSpec(memory_space=pl.ANY)] * 4,
        pl.BlockSpec((2, 2, rows, 4 * columns), lambda i: (0, 0, 0, 0)),
        jax.ShapeDtypeStruct((2, 2, rows, 4 * columns), bf16),
        (index, order) + tuple(parts),
        0,
        scratch=[
            pltpu.VMEM((2, 2, 4 * columns, rows), bf16),
            pltpu.SemaphoreType.DMA((4,)),
        ],
        events=events,
    )


def memory_out_kernel(index_ref, order_ref, *refs):
    out_ref, turned = refs[-2:]
    columns = turned.shape[0] // 4
    at = pl.multiple_of(index_ref[0] * columns, 64)
    for m in range(2):
        rows = jnp.concatenate([r[0, 0] for r in refs[4 * m : 4 * m + 4]])
        turned[...] = contract_rows(rows, order_ref[...])
        out_ref[m, 0] = turned[pl.ds(at, columns)].astype(bf16)


def memory_out(index, order, parts, events=()):
    _, _, rows, width = parts[0][0].shape
    return call(
        memory_out_kernel,
        (2,),
        [
            pl.BlockSpec(memory_space=pltpu.SMEM),
            pl.BlockSpec((4 * rows, 4 * rows), lambda i: (0, 0)),
        ]
        + [pl.BlockSpec((1, 1, rows, width), lambda i, m=m: (m, i, 0, 0)) for _, m in parts],
        pl.BlockSpec((2, 1, width // 4, 4 * rows), lambda i: (0, i, 0, 0)),
        jax.ShapeDtypeStruct((2, 2, width // 4, 4 * rows), bf16),
        (index, order) + tuple(a for a, _ in parts),
        8 * (4 * rows) ** 2 * width,
        scratch=[pltpu.VMEM((width, 4 * rows), f32)],
        events=events,
    )


def join_kernel(main, odd_ref, *refs):
    pieces, out_ref = refs[:-1], refs[-1]
    odd = odd_ref[0] == 1
    for c in range(4):
        out_ref[:, c * main : (c + 1) * main] = pieces[c][:, :main]
    tails = [p[:, main:].astype(f32) for p in pieces]
    heads = [jnp.where(odd, tails[c ^ 1], tails[c]) for c in range(4)]
    out_ref[:, 4 * main :] = jnp.concatenate(heads, axis=1).astype(bf16)


def join(main, odd, pieces):
    rows, columns = pieces[0].shape
    return call(
        functools.partial(join_kernel, main),
        (1,),
        [pl.BlockSpec(memory_space=pltpu.SMEM)] + [whole(p) for p in pieces],
        pl.BlockSpec((rows, 4 * columns), lambda i: (0, 0)),
        jax.ShapeDtypeStruct((rows, 4 * columns), bf16),
        (odd,) + tuple(pieces),
        0,
    )


def embed_kernel(count, patch_ref, order_ref, taps_ref, *refs):
    pieces = refs[:count]
    (
        sorted_ref, embedded_ref, normed_ref, query_ref, key_ref, value_ref, pool_ref,
        vec_ref, head_ref, qk_s, v_s, small_s, sems,
    ) = refs[count:]
    width = embedded_ref.shape[1]
    edge = small_s.shape[1] - 128

    @pl.when(pl.program_id(0) == 0)
    def _():
        fetch(pieces, ((0, qk_s), (2 * width, v_s), (3 * width, small_s)), sems)
        turned = small_s[:, edge:].astype(f32).T
        vec_ref[...] = turned[0:8] + turned[8:16] + turned[16:24]
        head_ref[...] = turned[24 : 24 + head_ref.shape[0]].astype(bf16)

    patch = contract_last(order_ref[...], patch_ref[0]).astype(bf16)
    sorted_ref[...] = patch
    embedded = contract_last(patch, small_s[:, : patch.shape[1]]) + vec_ref[0:1]
    embedded_ref[...] = embedded
    unit, _ = standard(embedded)
    normed = (unit * vec_ref[1:2] + vec_ref[2:3]).astype(bf16)
    normed_ref[...] = normed
    query_ref[...] = product(normed, qk_s[:, :width]).astype(bf16)
    for ch, weight, raw_ref in ((0, qk_s[:, width:], key_ref), (1, v_s[...], value_ref)):
        raw = product(normed, weight)
        raw_ref[...] = raw.astype(bf16)
        rows = raw.shape[0] // 4
        pooled = raw[:rows] * taps_ref[ch, 0:1]
        for t in range(1, 4):
            pooled = pooled + raw[t * rows : (t + 1) * rows] * taps_ref[ch, t : t + 1]
        pool_ref[0, ch] = pooled.astype(bf16)


def embed(patches_t, order, taps, weights, classes, events=()):
    _, patch, rows = patches_t.shape
    width = taps.shape[2]
    total = MICRO * rows
    edge = weights[0].shape[1] - 3 * width

    def tile(columns):
        return pl.BlockSpec((rows, columns), lambda i: (i, 0))

    return call(
        functools.partial(embed_kernel, len(weights)),
        (MICRO,),
        [pl.BlockSpec((1, patch, rows), lambda i: (i, 0, 0)), whole(order), whole(taps)]
        + [pl.BlockSpec(memory_space=pl.ANY)] * len(weights),
        [tile(patch), tile(width), tile(width), tile(width), tile(width), tile(width)]
        + [
            pl.BlockSpec((1, 2, rows // 4, width), lambda i: (i, 0, 0, 0)),
            pl.BlockSpec((8, width), lambda i: (0, 0)),
            pl.BlockSpec((classes, width), lambda i: (0, 0)),
        ],
        [
            jax.ShapeDtypeStruct((total, patch), bf16),
            jax.ShapeDtypeStruct((total, width), f32),
        ]
        + [jax.ShapeDtypeStruct((total, width), bf16)] * 4
        + [
            jax.ShapeDtypeStruct((MICRO, 2, rows // 4, width), bf16),
            jax.ShapeDtypeStruct((8, width), f32),
            jax.ShapeDtypeStruct((classes, width), bf16),
        ],
        (patches_t, order, taps) + weights,
        2 * total * width * (patch + 3 * width),
        scratch=[
            pltpu.VMEM((width, 2 * width), bf16),
            pltpu.VMEM((width, width), bf16),
            pltpu.VMEM((width, edge), bf16),
            pltpu.SemaphoreType.DMA((3 * len(weights),)),
        ],
        events=events,
    )


def attend_kernel(sources, q_ref, taps_ref, bias_ref, *refs):
    count = sum(sources)
    now, newer = refs[: sources[0]], refs[sources[0] : sources[0] + sources[1]]
    older = refs[sources[0] + sources[1] : count]
    out_ref, prob_ref, key_ref, value_ref = refs[-4:]
    query = q_ref[...]
    rows, width = query.shape
    size = width // QUAD
    for ch, target in ((0, key_ref), (1, value_ref)):
        at = 0
        for r in now:
            n = r.shape[2]
            target[at : at + n] = r[0, ch]
            at += n
        first, second = taps_ref[ch, 4:5], taps_ref[ch, 5:6]
        for r in newer + older:
            n = r.shape[2] // 2
            target[at : at + n] = (
                r[0, ch, :n].astype(f32) * first + r[0, ch, n:].astype(f32) * second
            ).astype(bf16)
            at += n
    keys_t = key_ref[...].T
    values = value_ref[...]
    lane = lax.broadcasted_iota(jnp.int32, (rows, width), 1) // size
    scaled = query * (size**-0.5)
    total = query.astype(f32)
    def score(h):
        own = jnp.where(lane == h, scaled, jnp.zeros_like(scaled))
        return product(own, keys_t) + bias_ref[0, h : h + 1, :]

    following = score(0)
    for h in range(QUAD):
        scores = following
        if h + 1 < QUAD:
            following = score(h + 1)
        top = jnp.max(scores, axis=-1, keepdims=True)
        exponent = jnp.exp(scores - top)
        denominator = jnp.sum(exponent, axis=-1, keepdims=True)
        probs = (exponent * (1.0 / denominator)).astype(bf16)
        prob_ref[h] = probs
        total = total + jnp.where(lane == h, product(probs, values), 0.0)
    out_ref[...] = total.astype(bf16)


def source_specs(entries, block):
    return [
        pl.BlockSpec((1, 2, a.shape[2], block), lambda i, m=m: (m, 0, 0, i)) for a, m in entries
    ]


def attend(micro, query, taps, bias, now, newer, older, before, events=()):
    rows = query.shape[0] // MICRO
    width = query.shape[1]
    count = bias.shape[2]
    quads = bias.shape[0]
    block = width // quads
    entries = now + newer + older
    operands = (query, taps, bias) + tuple(a for a, _ in entries)
    specs = [
        pl.BlockSpec((rows, block), lambda i: (micro, i)),
        pl.BlockSpec((2, 6, block), lambda i: (0, 0, i)),
        pl.BlockSpec((1, QUAD, count), lambda i: (i, 0, 0)),
    ] + source_specs(entries, block)
    alias = {}
    if before is not None:
        alias = {len(operands): 0}
        operands = operands + (before,)
        specs.append(pl.BlockSpec(memory_space=pl.ANY))
    return call(
        functools.partial(attend_kernel, (len(now), len(newer), len(older))),
        (quads,),
        specs,
        [
            pl.BlockSpec((rows, block), lambda i: (micro, i)),
            pl.BlockSpec((QUAD, rows, count), lambda i: (i, 0, 0)),
            pl.BlockSpec((count, block), lambda i: (0, i)),
            pl.BlockSpec((count, block), lambda i: (0, i)),
        ],
        [
            jax.ShapeDtypeStruct(query.shape, bf16),
            jax.ShapeDtypeStruct((quads * QUAD, rows, count), bf16),
            jax.ShapeDtypeStruct((count, width), bf16),
            jax.ShapeDtypeStruct((count, width), bf16),
        ],
        operands,
        4 * rows * count * width * 4,
        alias=alias,
        events=events,
    )


def attend_back_kernel(sources, q_ref, k_ref, v_ref, prob_ref, grad_ref, *refs):
    entries = refs[: sum(sources)]
    dq_ref, keep_ref, send_ref, taps_ref, bias_ref = refs[-5:]
    query = q_ref[...]
    grad = grad_ref[...]
    rows, width = query.shape
    size = width // QUAD
    keys = k_ref[...]
    count = keys.shape[0]
    values_t = v_ref[...].T
    query_t = query.T
    grad_t = grad.T
    scaling = size**-0.5
    lane = lax.broadcasted_iota(jnp.int32, (rows, width), 1) // size
    total = jnp.zeros((rows, width), f32)
    ones = jnp.ones((16, rows), bf16)
    half = count // 2
    spot = lax.broadcasted_iota(jnp.int32, (1, 128), 1)
    key_parts, value_parts = [], []
    def pull(h):
        own = jnp.where(lane == h, grad, jnp.zeros_like(grad))
        return product(own, values_t)

    following = pull(0)
    for h in range(QUAD):
        current = following
        if h + 1 < QUAD:
            following = pull(h + 1)
        probs_low = prob_ref[h]
        probs = probs_low.astype(f32)
        pulled = probs * current
        shift = jnp.sum(pulled, axis=-1, keepdims=True)
        score_grad = (pulled - probs * shift).astype(bf16)
        total = total + jnp.where(lane == h, product(score_grad, keys), 0.0)
        left = jnp.concatenate([query_t[h * size : (h + 1) * size], ones])
        found = product(left, score_grad)
        key_parts.append(found[:size])
        sums = found[size : size + 1]
        row = jnp.zeros((1, 128), f32)
        for g, (a, b) in enumerate(((0, half), (half, half + half // 2), (half + half // 2, count))):
            row = row + jnp.where(spot == g, jnp.sum(sums[:, a:b], axis=1, keepdims=True), 0.0)
        bias_ref[0, h : h + 1, :] = row
        value_parts.append(product(grad_t[h * size : (h + 1) * size], probs_low))
    dq_ref[...] = (total * scaling + grad.astype(f32)).astype(bf16)
    part = keep_ref.shape[2]
    for ch, parts, factor in ((0, key_parts, scaling), (1, value_parts, 1.0)):
        found = jnp.concatenate(parts).T * factor
        for s in range(4):
            target = send_ref if s % 2 else keep_ref
            target[s // 2, ch] = found[s * part : (s + 1) * part].astype(bf16)
        at = half
        first = jnp.zeros((1, width), f32)
        second = jnp.zeros((1, width), f32)
        for r in entries:
            n = r.shape[2] // 2
            piece = found[at : at + n]
            first = first + jnp.sum(piece * r[0, ch, :n].astype(f32), axis=0, keepdims=True)
            second = second + jnp.sum(piece * r[0, ch, n:].astype(f32), axis=0, keepdims=True)
            at += n
        taps_ref[ch, 0:1] = first
        taps_ref[ch, 1:2] = second


def attend_back(micro, query, keys, values, probs, grad, newer, older, before, events=()):
    heads, rows, count = probs.shape
    width = query.shape[1]
    quads = heads // QUAD
    block = width // quads
    entries = newer + older
    operands = (query, keys, values, probs, grad) + tuple(a for a, _ in entries)
    specs = [
        pl.BlockSpec((rows, block), lambda i: (micro, i)),
        pl.BlockSpec((count, block), lambda i: (0, i)),
        pl.BlockSpec((count, block), lambda i: (0, i)),
        pl.BlockSpec((QUAD, rows, count), lambda i: (i, 0, 0)),
        pl.BlockSpec((rows, block), lambda i: (micro, i)),
    ] + source_specs(entries, block)
    alias = {}
    if before is not None:
        alias = {len(operands): 0}
        operands = operands + (before,)
        specs.append(pl.BlockSpec(memory_space=pl.ANY))
    part = count // 8
    return call(
        functools.partial(attend_back_kernel, (len(newer), len(older))),
        (quads,),
        specs,
        [
            pl.BlockSpec((rows, block), lambda i: (micro, i)),
            pl.BlockSpec((2, 2, part, block), lambda i: (0, 0, 0, i)),
            pl.BlockSpec((2, 2, part, block), lambda i: (0, 0, 0, i)),
            pl.BlockSpec((2, 2, block), lambda i: (0, 0, i)),
            pl.BlockSpec((1, QUAD, 128), lambda i: (i, 0, 0)),
        ],
        [
            jax.ShapeDtypeStruct(query.shape, bf16),
            jax.ShapeDtypeStruct((2, 2, part, width), bf16),
            jax.ShapeDtypeStruct((2, 2, part, width), bf16),
            jax.ShapeDtypeStruct((2, 2, width), f32),
            jax.ShapeDtypeStruct((quads, QUAD, 128), f32),
        ],
        operands,
        8 * rows * count * width * 4,
        alias=alias,
        events=events,
    )


def gelu_pair(inputs):
    size = jnp.abs(inputs)
    t = 1.0 / (1.0 + (0.3275911 * 0.5**0.5) * size)
    bell = jnp.exp(-0.5 * inputs * inputs)
    tail = (
        t
        * (
            0.5 * 0.254829592
            + t
            * (
                0.5 * -0.284496736
                + t * (0.5 * 1.421413741 + t * (0.5 * -1.453152027 + t * (0.5 * 1.061405429)))
            )
        )
        * bell
    )
    share = jnp.where(inputs > 0.0, 1.0 - tail, tail)
    return inputs * share, share + inputs * bell * 0.3989422804014327


def mlp_weights(width, units, count):
    return [
        pltpu.VMEM((width, width), bf16),
        pltpu.VMEM((width, 2 * units), bf16),
        pltpu.SemaphoreType.DMA((count,)),
        pltpu.SemaphoreType.DMA((count,)),
    ]


def mlp_kernel(count, attended_ref, embedded_ref, vec_ref, select_ref, *refs):
    (
        first_ref, normed_ref, active_ref, slope_ref, second_ref, feature_ref,
        out_s, both_s, out_sems, sems,
    ) = refs[count:]
    units = both_s.shape[1] // 2
    out_copies = transfers(refs[:count], ((2 * units, out_s),), out_sems)
    copies = transfers(refs[:count], ((0, both_s),), sems)
    starting = pl.program_id(0) == 0

    @pl.when(starting)
    def _():
        begin(out_copies)
        begin(copies)
        finish(out_copies)

    first = embedded_ref[...] + contract_last(attended_ref[...], out_s[...])
    first_ref[...] = first
    unit, _ = standard(first)
    normed = (unit * vec_ref[3:4] + vec_ref[4:5]).astype(bf16)
    normed_ref[...] = normed
    total = first

    @pl.when(starting)
    def _():
        finish(copies)

    chunk = units // 4

    def entry(s):
        return product(normed, both_s[:, (2 * s + 1) * chunk : (2 * s + 2) * chunk])

    following = entry(0)
    for s in range(4):
        at = s * chunk
        hidden = following
        if s < 3:
            following = entry(s + 1)
        value, slope = gelu_pair(hidden)
        value = value.astype(bf16)
        active_ref[:, at : at + chunk] = value
        slope_ref[:, at : at + chunk] = slope.astype(bf16)
        total = total + contract_last(value, both_s[:, 2 * at : 2 * at + chunk])
    second_ref[...] = total
    unit, _ = standard(total)
    final = unit * vec_ref[5:6] + vec_ref[6:7]
    feature_ref[0] = jnp.dot(
        select_ref[0], final, precision=PRECISE, preferred_element_type=f32
    )


def mlp(attended, embedded, vec, select, weights, events=()):
    total, width = embedded.shape
    rows = total // MICRO
    units = (weights[0].shape[1] - width) // 2
    boxes = select.shape[1]

    def tile(columns):
        return pl.BlockSpec((rows, columns), lambda i: (i, 0))

    return call(
        functools.partial(mlp_kernel, len(weights)),
        (MICRO,),
        [
            tile(width),
            tile(width),
            whole(vec),
            pl.BlockSpec((1, boxes, rows), lambda i: (i, 0, 0)),
        ]
        + [pl.BlockSpec(memory_space=pl.ANY)] * len(weights),
        [tile(width), tile(width), tile(units), tile(units), tile(width)]
        + [pl.BlockSpec((1, boxes, width), lambda i: (i, 0, 0))],
        [
            jax.ShapeDtypeStruct((total, width), f32),
            jax.ShapeDtypeStruct((total, width), bf16),
            jax.ShapeDtypeStruct((total, units), bf16),
            jax.ShapeDtypeStruct((total, units), bf16),
            jax.ShapeDtypeStruct((total, width), f32),
            jax.ShapeDtypeStruct((MICRO, boxes, width), f32),
        ],
        (attended, embedded, vec, select) + weights,
        2 * total * width * (width + 2 * units),
        scratch=mlp_weights(width, units, len(weights)),
        events=events,
    )


def mlp_back_kernel(
    count, pull_ref, select_ref, second_ref, first_ref, slope_ref, vec_ref, *refs
):
    (
        branch_ref, hidden_ref, attn_ref, first_grad_ref, attended_ref, sums_ref,
        out_s, both_s, out_sems, sems,
    ) = refs[count:]
    units = both_s.shape[1] // 2
    out_copies = transfers(refs[:count], ((2 * units, out_s),), out_sems)
    copies = transfers(refs[:count], ((0, both_s),), sems)
    starting = pl.program_id(0) == 0

    @pl.when(starting)
    def _():
        begin(copies)
        begin(out_copies)
        sums_ref[...] = jnp.zeros_like(sums_ref)

    pull = lax.dot_general(
        select_ref[0],
        pull_ref[0],
        (((0,), (0,)), ((), ())),
        precision=PRECISE,
        preferred_element_type=f32,
    )
    unit, scale = standard(second_ref[...])
    sums_ref[2:3] += jnp.sum(pull * unit, axis=0, keepdims=True)
    sums_ref[3:4] += jnp.sum(pull, axis=0, keepdims=True)
    second_grad = standard_back(pull * vec_ref[5:6], unit, scale)
    branch = second_grad.astype(bf16)
    branch_ref[...] = branch

    @pl.when(starting)
    def _():
        finish(copies)

    chunk = units // 4
    normed_grad = jnp.zeros(second_grad.shape, f32)

    for s in range(4):
        at = s * chunk
        active_grad = product(branch, both_s[:, 2 * at : 2 * at + chunk])
        hidden_grad = (active_grad * slope_ref[:, at : at + chunk].astype(f32)).astype(bf16)
        hidden_ref[:, at : at + chunk] = hidden_grad
        normed_grad = normed_grad + contract_last(
            hidden_grad, both_s[:, 2 * at + chunk : 2 * at + 2 * chunk]
        )

    @pl.when(starting)
    def _():
        finish(out_copies)

    unit, scale = standard(first_ref[...])
    sums_ref[0:1] += jnp.sum(normed_grad * unit, axis=0, keepdims=True)
    sums_ref[1:2] += jnp.sum(normed_grad, axis=0, keepdims=True)
    first_grad = standard_back(normed_grad * vec_ref[3:4], unit, scale) + second_grad
    first_grad_ref[...] = first_grad
    attn = first_grad.astype(bf16)
    attn_ref[...] = attn
    attended_ref[...] = product(attn, out_s[...]).astype(bf16)


def mlp_back(pull, select, second, first, slope, vec, weights, events=()):
    total, width = second.shape
    rows = total // MICRO
    units = (weights[0].shape[1] - width) // 2
    boxes = select.shape[1]

    def tile(columns):
        return pl.BlockSpec((rows, columns), lambda i: (i, 0))

    return call(
        functools.partial(mlp_back_kernel, len(weights)),
        (MICRO,),
        [
            pl.BlockSpec((1, boxes, width), lambda i: (i, 0, 0)),
            pl.BlockSpec((1, boxes, rows), lambda i: (i, 0, 0)),
            tile(width),
            tile(width),
            tile(units),
            whole(vec),
        ]
        + [pl.BlockSpec(memory_space=pl.ANY)] * len(weights),
        [tile(width), tile(units), tile(width), tile(width), tile(width)]
        + [pl.BlockSpec((8, width), lambda i: (0, 0))],
        [
            jax.ShapeDtypeStruct((total, width), bf16),
            jax.ShapeDtypeStruct((total, units), bf16),
            jax.ShapeDtypeStruct((total, width), bf16),
            jax.ShapeDtypeStruct((total, width), f32),
            jax.ShapeDtypeStruct((total, width), bf16),
            jax.ShapeDtypeStruct((8, width), f32),
        ],
        (pull, select, second, first, slope, vec) + weights,
        2 * total * width * (width + 2 * units),
        scratch=mlp_weights(width, units, len(weights)),
        events=events,
    )


def embed_back_kernel(
    count, dq_ref, key_ref, value_ref, taps_ref, embedded_ref, first_ref, normed_ref, patch_ref,
    vec_ref, head_ref, more_ref, *refs
):
    pools = refs[: 3 * MICRO]
    (
        near_ref, far_ref, taps_out, qk_s, v_s, pool_s, sums_s, normed_s, projected_s, grad_s,
        patch_s, sems,
    ) = refs[3 * MICRO + count :]
    rows, width = embedded_ref.shape
    step = pl.program_id(0)

    @pl.when(step == 0)
    def _():
        sums_s[...] = jnp.zeros_like(sums_s)
        sums_s[3:7] = more_ref[0:4]
        sums_s[8 : 8 + head_ref.shape[0]] = head_ref[...]
        taps_out[...] = jnp.zeros_like(taps_out)
        patch_s[...] = jnp.zeros_like(patch_s)
        for m in range(MICRO):
            kept, got, far = pools[3 * m : 3 * m + 3]
            for ch in range(2):
                pool_s[m, ch] = (
                    kept[0, ch].astype(f32) + got[0, ch].astype(f32) + far[ch].astype(f32)
                )
        fetch(refs[3 * MICRO : 3 * MICRO + count], ((0, qk_s), (2 * width, v_s)), sems)

    at = pl.multiple_of(step * rows, 128)
    here = pl.ds(at, rows)
    projected_s[here, :width] = dq_ref[...]
    pooled = rows // 4
    for ch, raw_ref in ((0, key_ref), (1, value_ref)):
        pool = pool_s[step, ch]
        for t in range(4):
            projected_s[
                pl.ds(at + t * pooled, pooled), (1 + ch) * width : (2 + ch) * width
            ] = (pool * taps_ref[ch, t : t + 1]).astype(bf16)
            raw = raw_ref[t * pooled : (t + 1) * pooled].astype(f32)
            taps_out[4 * ch + t : 4 * ch + t + 1] += jnp.sum(pool * raw, axis=0, keepdims=True)
    normed_grad = contract_last(projected_s[here, : 2 * width], qk_s[...])
    normed_grad = normed_grad + contract_last(projected_s[here, 2 * width :], v_s[...])
    unit, scale = standard(embedded_ref[...])
    sums_s[1:2] += jnp.sum(normed_grad * unit, axis=0, keepdims=True)
    sums_s[2:3] += jnp.sum(normed_grad, axis=0, keepdims=True)
    grad = standard_back(normed_grad * vec_ref[1:2], unit, scale) + first_ref[...]
    grad = grad.astype(bf16)
    sums_s[0:1] += jnp.sum(grad.astype(f32), axis=0, keepdims=True)
    normed_s[:, here] = normed_ref[...].T
    grad_s[:, here] = grad.T
    patch_s[here, : patch_ref.shape[1]] = patch_ref[...]

    @pl.when(step == MICRO - 1)
    def _():
        half = width // 2
        edge = 3 * width + patch_s.shape[1]
        for out_ref, top in ((far_ref, half), (near_ref, 0)):
            part = slice(top, top + half)
            for c in range(3):
                out_ref[:, c * width : (c + 1) * width] = product(
                    normed_s[part], projected_s[:, c * width : (c + 1) * width]
                ).astype(bf16)
            out_ref[:, 3 * width : edge] = product(grad_s[part], patch_s[...]).astype(bf16)
            out_ref[:, edge:] = sums_s[:, part].T.astype(bf16)


def embed_back(
    dq, keys, values, taps, embedded, first_grad, normed, patches, vec, head, more, pools, weights,
    events=(),
):
    total, width = embedded.shape
    rows = total // MICRO
    patch = patches.shape[1]
    edge = patch + (-patch % 128)
    columns = 3 * width + edge + 128

    def tile(columns):
        return pl.BlockSpec((rows, columns), lambda i: (i, 0))

    operands = (dq, keys, values, taps, embedded, first_grad, normed, patches, vec, head, more)
    half = pl.BlockSpec((width // 2, columns), lambda i: (0, 0))
    return call(
        functools.partial(embed_back_kernel, len(weights)),
        (MICRO,),
        [tile(width)] * 3
        + [whole(taps)]
        + [tile(width)] * 3
        + [tile(patch)]
        + [whole(a) for a in (vec, head, more) + pools]
        + [pl.BlockSpec(memory_space=pl.ANY)] * len(weights),
        [half, half, pl.BlockSpec((8, width), lambda i: (0, 0))],
        [
            jax.ShapeDtypeStruct((width // 2, columns), bf16),
            jax.ShapeDtypeStruct((width // 2, columns), bf16),
            jax.ShapeDtypeStruct((8, width), f32),
        ],
        operands + pools + weights,
        2 * total * width * 3 * width,
        scratch=[
            pltpu.VMEM((width, 2 * width), bf16),
            pltpu.VMEM((width, width), bf16),
            pltpu.VMEM((MICRO, 2, rows // 4, width), f32),
            pltpu.VMEM((128, width), f32),
            pltpu.VMEM((width, total), bf16),
            pltpu.VMEM((total, 3 * width), bf16),
            pltpu.VMEM((width, total), bf16),
            pltpu.VMEM((total, edge), bf16),
            pltpu.SemaphoreType.DMA((2 * len(weights),)),
        ],
        events=events,
    )


def squares_kernel(*refs):
    grads, flat_ref, outs = refs[:6], refs[6], refs[7:]
    total = 0.0
    for i in range(3):
        found = grads[2 * i][...].astype(f32) + grads[2 * i + 1][...].astype(f32)
        outs[i][...] = found
        total = total + jnp.sum(found * found)
    rows = flat_ref.shape[0]
    outs[3][...] = jnp.zeros_like(outs[3]) + total
    outs[3][:rows] = flat_ref[...]


def squares_of(attn, small, rest, flat, events=()):
    operands = tuple(attn) + tuple(small) + tuple(rest) + (flat,)
    rows = flat.shape[0] + (-flat.shape[0] % 8)
    rows += 8 * (rows == flat.shape[0])
    shapes = [jax.ShapeDtypeStruct(g[0].shape, f32) for g in (attn, small, rest)]
    shapes.append(jax.ShapeDtypeStruct((rows, flat.shape[1]), f32))
    return call(
        squares_kernel,
        (1,),
        [whole(o) for o in operands],
        [whole(o) for o in shapes],
        shapes,
        operands,
        0,
        events=events,
    )


def update_kernel(rates, patch, odd_ref, one_ref, two_ref, *refs):
    count = len(rates)
    attn_ref, small_ref, rest_ref = refs[:3]
    weights, moments, averages = (refs[3 + i * count : 3 + (i + 1) * count] for i in range(3))
    outs = refs[3 + 3 * count :]
    heads = weights[6].shape[0] * 3
    blocks = []
    square = one_ref[52:53, 0:1] + two_ref[52:53, 0:1]
    spot = lax.broadcasted_iota(jnp.int32, (13, one_ref.shape[1]), 1)
    row = lax.broadcasted_iota(jnp.int32, (13, one_ref.shape[1]), 0)
    counted = (row < 12) | (spot < heads)
    for c in range(4):
        far = 13 * (c ^ 2)
        block = one_ref[13 * c : 13 * c + 13] + two_ref[far : far + 13]
        kept = jnp.where(counted, block, 0.0)
        square = square + jnp.sum(kept * kept)
        blocks.append(block)
    mine = jnp.where(odd_ref[0] == 1, blocks[1], blocks[0])
    boxes = blocks[0][12:13, heads + 1 : heads + 2]
    norm = jnp.sqrt(square) / boxes
    outs[-3][...] = blocks[0][12:13, heads : heads + 1]
    outs[-2][...] = boxes
    outs[-1][...] = norm
    scaling = jnp.minimum(1.0, THRESHOLD / norm) / boxes
    hidden = weights[0].shape[1] - attn_ref.shape[1]
    edge = small_ref.shape[1] - 128
    classes = weights[3].shape[1]
    tail = small_ref[:, edge:]

    def step(i, at, grad):
        grad = grad * scaling
        moment = MOMENTUM * moments[i][at] + grad
        updated = weights[i][at] - rates[i] * (grad + MOMENTUM * moment)
        outs[i][at] = updated
        outs[count + i][at] = moment
        outs[2 * count + i][at] = AVERAGING * averages[i][at] + (1.0 - AVERAGING) * updated
        if i < 2:
            outs[3 * count + i][at] = updated.astype(bf16)

    step(0, ..., jnp.concatenate([attn_ref[...], rest_ref[:, :hidden]], axis=1))
    step(1, ..., rest_ref[:, hidden:])
    step(2, ..., small_ref[:, :patch])
    step(3, ..., tail[:, 8 : 8 + classes])
    step(4, ..., tail.T[:7])
    for t in range(6):
        step(5, t, mine[2 * t : 2 * t + 2])
    for h in range(heads // 3):
        step(6, slice(h, h + 1), mine[12:13, 3 * h : 3 * h + 3])


def update(odd, one, two, grads, patch, weights, moments, averages, rates):
    operands = (odd, one, two) + grads + weights + moments + averages
    kept = [jax.ShapeDtypeStruct(w.shape, f32) for w in weights]
    shapes = kept * 3 + [jax.ShapeDtypeStruct(w.shape, bf16) for w in weights[:2]]
    shapes = shapes + [jax.ShapeDtypeStruct((1, 1), f32)] * 3
    return call(
        functools.partial(update_kernel, rates, patch),
        (1,),
        [pl.BlockSpec(memory_space=pltpu.SMEM)] + [whole(o) for o in operands[1:]],
        [pl.BlockSpec(o.shape, lambda i, n=len(o.shape): (0,) * n) for o in shapes],
        shapes,
        operands,
        0,
    )


def one_hot_rows(index, count):
    return (index[:, None] == jnp.arange(count)[None, :]).astype(bf16)


def shards(
    patches,
    clip_len,
    box_count,
    box_bounds,
    box_labels,
    memory,
    up_weight,
    down_weight,
    embed_weight,
    head_weight,
    vector_weight,
    conv_weight,
    position_bias,
    up_moment,
    down_moment,
    embed_moment,
    head_moment,
    vector_moment,
    conv_moment,
    position_moment,
    up_average,
    down_average,
    embed_average,
    head_average,
    vector_average,
    conv_average,
    position_average,
):
    dp_index = lax.axis_index("dp")
    mp_index = lax.axis_index("mp")
    dp_count = lax.axis_size("dp")
    across, core = mp_index % 2, dp_index % 2
    upper = mp_index - across
    quarter = 2 * core + across
    rows = patches.shape[1]
    eighth = rows // 8
    pooled = rows // 4
    half_pool = pooled // 2
    head_cols = conv_weight.shape[2]
    width = 4 * head_cols
    sub = embed_weight.shape[1]
    patch = embed_weight.shape[0]
    classes = head_weight.shape[0]
    boxes = box_bounds.shape[2]
    own_heads = position_bias.shape[0]
    heads = own_heads * 4
    hidden_cols = up_weight.shape[1] - 3 * head_cols

    ints = jnp.concatenate(
        [clip_len.reshape(-1), box_count.reshape(-1), box_bounds.reshape(-1), box_labels.reshape(-1)]
    )
    total_ints = ints.shape[0]
    ints = jnp.pad(ints, (0, -total_ints % 1024)).reshape(-1, 128)
    ints = regroup(ints).reshape(-1)
    lengths_all = ints[:5]
    counts = ints[5:8]
    bounds = ints[8 : 8 + MICRO * boxes * 2].reshape(MICRO, boxes, 2)
    labels = ints[8 + MICRO * boxes * 2 : total_ints].reshape(MICRO * boxes, classes)

    def in_three(array):
        high = lax.reduce_precision(array, 8, 7)
        middle = lax.reduce_precision(array - high, 8, 7)
        return [high, middle, array - high - middle]

    edge = patch + (-patch % 128)
    columns_in = [jnp.pad(embed_weight, ((0, edge - patch), (0, 0)))]
    columns_in += [jnp.pad(v, ((0, 1), (0, 0))) for v in in_three(vector_weight)]
    columns_in += [jnp.pad(head_weight, ((0, 128 - 24 - classes), (0, 0)))]
    taps_pos = jnp.concatenate(
        [
            conv_weight.reshape(12, head_cols),
            jnp.pad(position_bias.reshape(1, -1), ((0, 0), (0, head_cols - position_bias.size))),
        ]
    )
    taps_pos = jnp.concatenate(in_three(taps_pos)).reshape(sub, -1)
    small = jnp.concatenate([jnp.concatenate(columns_in).T, taps_pos], axis=1).astype(bf16)
    strip = -(-small.shape[1] // 512) * 128
    small = jnp.pad(small, ((0, 0), (0, 4 * strip - small.shape[1])))
    small = jnp.concatenate([small[:, i * strip : (i + 1) * strip] for i in range(4)])
    up_low = up_weight.astype(bf16)
    down_low = down_weight.astype(bf16)
    pieces = gather_mp(jnp.concatenate([up_low[:, : 3 * head_cols], small], axis=1))
    place = jnp.arange(16 * sub)
    source = (
        (((place // sub) % 4) ^ mp_index) * 4 * sub + place // (4 * sub) * sub + place % sub
    )
    small = product(
        one_hot_rows(source, 16 * sub), jnp.concatenate([p[:, 3 * head_cols :] for p in pieces])
    ).astype(bf16)
    small = jnp.concatenate(
        [small[i * 4 * sub : (i + 1) * 4 * sub] for i in range(4)], axis=1
    )
    small_mine = small[:, : edge + 128]
    taps_pos = small[:, edge + 128 : edge + 128 + 39 * head_cols // sub]
    taps_pos = jnp.sum(taps_pos.reshape(4, 3, 13, head_cols).astype(f32), axis=1)
    taps_pos = jnp.where(upper == 2, jnp.roll(taps_pos, 2, axis=0), taps_pos)
    conv_all = taps_pos[:, :12].transpose(1, 0, 2).reshape(2, 6, width)
    rel_bias = taps_pos[:, 12, : position_bias.size].reshape(heads, 3)
    weights = jnp.concatenate(
        [p[:, j * head_cols : (j + 1) * head_cols] for j in range(3) for p in pick(pieces)]
        + [small_mine],
        axis=1,
    )
    weights = spread_core(spread_dp(weights))
    patches_t = regroup(after(patches.transpose(0, 2, 1), *pieces))
    pieces = gather_mp(
        after(
            jnp.concatenate(
                [down_low[:, head_cols:], up_low[:, 3 * head_cols :], down_low[:, :head_cols]],
                axis=1,
            ),
            patches_t,
        )
    )

    place = jnp.arange(rows)
    token = 8 * (place % eighth) + 4 * ((place // eighth) % 2) + place // (2 * eighth)
    token_order = one_hot_rows(token, rows)
    mem_rows = memory.shape[2]
    half_mem = mem_rows // 2
    mem_place = jnp.arange(mem_rows)
    mem_order = one_hot_rows(2 * (mem_place % half_mem) + mem_place // half_mem, mem_rows)
    part_quarter = [2 * (core ^ (s % 2)) + (across ^ (s // 2)) for s in range(4)]
    pool_place = jnp.arange(pooled)
    pool_token = 2 * (pool_place % half_pool) + pool_place // half_pool
    now_index = jnp.concatenate([pq * pooled + pool_token for pq in part_quarter])
    pool_index = jnp.concatenate([pq * half_pool + jnp.arange(half_pool) for pq in part_quarter])
    mem_index = jnp.arange(half_mem)

    def key_bias(m):
        sides = [
            (now_index, lengths_all[2 + m] // 4),
            (mem_index if m == 0 else pool_index, lengths_all[1 + m] // 8),
            (mem_index if m < 2 else pool_index, lengths_all[m] // 8),
        ]
        return jnp.concatenate(
            [
                jnp.where((index < limit)[None, :], rel_bias[:, g : g + 1], -3e38)
                for g, (index, limit) in enumerate(sides)
            ],
            axis=1,
        ).reshape(heads // QUAD, QUAD, -1)

    biases = [key_bias(m) for m in range(MICRO)]

    (
        patches_in,
        embedded,
        normed,
        query,
        raw_keys,
        raw_values,
        pools,
        vectors,
        head_low,
    ) = embed(patches_t, token_order, conv_all, weights, classes)
    two = swap_mp(pools, 1)
    rest = join(2 * hidden_cols, across[None], [after(p, pools) for p in pieces])
    rest = [rest, swap_dp(rest, 2), swap_dp(rest, 4)]
    rest_late = after(rest[0], *rest[1:])
    rest_late = [swap_dp(rest_late, b) for b in range(6, dp_count, 2)]
    gathered = (pools, swap_dp(pools, 1), two, swap_dp(after(two, *biases), 1))
    stored = [[(a, m) for a in gathered] for m in range(MICRO)]
    memory_t = regroup(after(memory.transpose(0, 1, 3, 2), rest[0]))
    mem_two = swap_mp(after(memory_t, two), 1)
    stored = [None, None] + stored

    attended, saved = None, {}
    for m in (2, 1, 0):
        arrived = {2: rest[1:], 1: [], 0: rest_late}[m]
        attended, probs, keys, values = attend(
            m,
            after(query, *arrived) if arrived else query,
            conv_all,
            biases[m],
            stored[m + 2],
            stored[m + 1],
            stored[m],
            attended,
        )
        saved[m] = (keys, values, probs)
        if m == 2:
            rest_core = [swap_dp(after(p, attended), 1) for p in rest]
        if m == 1:
            late_core = [swap_dp(after(p, attended), 1) for p in rest_late]
        if m > 1:
            mem_two = after(mem_two, attended)
            mem_parts = (
                memory_t,
                swap_dp(after(memory_t, attended), 1),
                mem_two,
                swap_dp(mem_two, 1),
            )
            mem_full = memory_in(
                jnp.stack(
                    [
                        (((c ^ upper) // 2) ^ core) + 2 * (((c ^ upper) % 2) ^ across)
                        for c in range(4)
                    ]
                ),
                mem_order,
                mem_parts,
            )
            stored[:2] = [[(mem_full, 0)], [(mem_full, 1)]]
    rest = one_or_all(rest + rest_late + rest_core + late_core)

    position = quarter * rows + token
    within = position % FRAME
    live = position[None, :] < lengths_all[2:, None]
    inside = (
        (within[None, None, :] >= bounds[:, :, 0:1])
        & (within[None, None, :] < bounds[:, :, 1:2])
        & live[:, None, :]
    )
    denominator = ((bounds[:, :, 1] - bounds[:, :, 0]) * (lengths_all[2:, None] // FRAME)).astype(
        f32
    )
    select = inside.astype(f32) / denominator[:, :, None]
    first_res, normed_mlp, active, slope, second_res, feature = mlp(
        attended, embedded, vectors, select, rest
    )
    target_row = jnp.arange(4 * pooled)
    target_quarter, target_rest = target_row // pooled, target_row % pooled
    source_row = (
        (((target_quarter // 2) ^ core) + 2 * ((target_quarter % 2) ^ across)) * pooled
        + (target_rest % 2) * half_pool
        + target_rest // 2
    )
    new_memory = memory_out(
        (quarter ^ upper)[None],
        one_hot_rows(source_row, 4 * pooled).T,
        stored[3] + stored[4],
        events=(feature,),
    )
    feature = feature.reshape(MICRO * boxes, width)
    feature = group_sum_features(feature).astype(bf16)
    logits = contract_last(feature, head_low)
    target = labels.astype(f32)
    keep = (jnp.arange(boxes)[None, :] < counts[:, None]).astype(f32).reshape(-1, 1)
    lead = (quarter == 0).astype(f32)
    loss_part = jnp.sum((jax.nn.softplus(logits) - target * logits) * keep) * lead
    grad_logits = ((jax.nn.sigmoid(logits) - target) * keep).astype(bf16)

    grad_head = contract_rows(grad_logits, feature) * lead
    grad_feature = product(grad_logits, head_low).reshape(MICRO, boxes, width)
    grad_branch, grad_hidden, grad_attn, grad_first, grad_attended, sums = mlp_back(
        grad_feature, select, second_res, first_res, slope, vectors, rest, (new_memory,)
    )
    new_memory = regroup(new_memory)
    grad_branch = after(grad_branch, new_memory)

    half = width // 2

    def weight_grad(left, right, at):
        return contract_rows(left[:, at : at + half], right).astype(bf16)

    sides = ((grad_branch, active), (normed_mlp, grad_hidden), (grad_attn, attended))
    rest_far = [weight_grad(*side, half) for side in sides]
    rest_near = [weight_grad(*side, 0) for side in sides]
    rest_pieces = halve_dp(rest_near, rest_far)

    dq, pool_grads, bias_grad, mem_taps = None, [], 0.0, 0.0
    events = tuple(rest_pieces)
    rest_found = trade_dp(rest_pieces, 1, 3)
    for m in range(MICRO):
        keys, values, probs = saved[m]
        dq, kept, sent, taps_part, bias_part = attend_back(
            m,
            query,
            keys,
            values,
            probs,
            after(grad_attended, *events),
            stored[m + 1],
            stored[m],
            dq,
        )
        got = swap_dp(sent, 1)
        away = (kept[1].astype(f32) + got[1].astype(f32)).astype(bf16)
        pool_grads.extend([kept, got, swap_mp(away, 1)])
        bias_grad = bias_grad + bias_part
        mem_taps = mem_taps + taps_part
        events = (away,)
        if m == 1:
            events = (away, pool_grads[2]) + tuple(rest_found)
            rest_pieces[3:] = [after(p, *rest_found) for p in rest_pieces[3:]]
            rest_found += trade_dp(rest_pieces, 3, None)
    rest_total = sum((f.astype(f32) for f in rest_found), rest_pieces[0].astype(f32))
    units = 4 * hidden_cols
    rest_pieces = []
    out_blocks = pick(
        [
            rest_total[:, 2 * units + c * head_cols : 2 * units + (c + 1) * head_cols]
            for c in range(4)
        ]
    )
    for s in range(4):
        piece = jnp.concatenate(
            [
                rest_total[:, units + s * hidden_cols : units + (s + 1) * hidden_cols],
                out_blocks[s],
                rest_total[:, s * hidden_cols : (s + 1) * hidden_cols],
            ],
            axis=1,
        )
        rest_pieces.append(piece)
    rest_near, rest_far, rest_got = halve_mp(rest_pieces)
    attn_near, attn_far, taps_grad = embed_back(
        after(dq, rest_near, *rest_far),
        raw_keys,
        raw_values,
        conv_all,
        embedded,
        grad_first,
        normed,
        patches_in,
        vectors,
        grad_head,
        sums,
        tuple(pool_grads),
        weights,
        events=(),
    )
    attn_pieces = halve_dp([attn_near], [attn_far])
    attn_found = trade_dp(attn_pieces, 1, None)
    rest_got = after(rest_got, *attn_pieces)
    columns = rest_near.shape[1]
    far = (rest_far[0].astype(f32) + rest_got[:, columns:].astype(f32)).astype(bf16)
    rest_mine = (rest_near + rest_got[:, :columns].astype(f32), swap_mp(far, 2))
    attn_found[-1] = after(attn_found[-1], far)
    attn_total = sum((f.astype(f32) for f in attn_found), attn_pieces[0].astype(f32))
    small_total = attn_total[:, 3 * width :]
    small_parts = halve_more(*halve_mp(
        [
            lax.dynamic_slice_in_dim(small_total, (mp_index ^ s) * sub, sub, axis=0)
            for s in range(4)
        ]
    ))
    attn_parts = halve_more(*halve_mp(
        pick(
            [
                jnp.concatenate(
                    [
                        attn_total[:, (4 * j + c) * head_cols : (4 * j + c + 1) * head_cols]
                        for j in range(3)
                    ],
                    axis=1,
                )
                for c in range(4)
            ]
        )
    ))

    count_local = jnp.sum(box_count).astype(f32) * (mp_index == 0).astype(f32)
    taps_rows = jnp.stack(
        [
            jnp.concatenate([taps_grad[4 * ch : 4 * ch + 4], mem_taps[ch]], axis=0)
            for ch in range(2)
        ],
        axis=1,
    ).reshape(12, 4, head_cols)
    scalars = jnp.stack([loss_part, count_local])
    last = jnp.concatenate(
        [
            bias_grad.reshape(heads, 128)[:, :3].reshape(4, -1),
            jnp.broadcast_to(scalars[None], (4, 2)),
        ],
        axis=1,
    )
    last = jnp.pad(last, ((0, 0), (0, head_cols - last.shape[1])))
    flat = jnp.concatenate([taps_rows, last[None]]).transpose(1, 0, 2)
    attn_mine, small_mine, rest_mine, both = squares_of(
        attn_parts, small_parts, rest_mine, flat.reshape(52, head_cols), (new_memory,)
    )
    both = both + swap_dp(both, 1)
    both = both + sum(swap_dp(both, b) for b in range(2, dp_count, 2))
    both = both + swap_mp(both, 1)
    both_two = swap_mp(both, 2)

    def turned(arrays):
        up, down, embed_part, head, vector, conv, position = arrays
        return (up, down, embed_part.T, head.T, vector, conv.transpose(1, 0, 2), position)

    masters = (
        up_weight,
        down_weight,
        embed_weight,
        head_weight,
        vector_weight,
        conv_weight,
        position_bias,
    )
    moments = (
        up_moment,
        down_moment,
        embed_moment,
        head_moment,
        vector_moment,
        conv_moment,
        position_moment,
    )
    averages = (
        up_average,
        down_average,
        embed_average,
        head_average,
        vector_average,
        conv_average,
        position_average,
    )
    rates = (LEARNING,) * 4 + (VECTOR_LEARNING,) * 3
    made = update(
        across[None],
        both,
        both_two,
        (attn_mine, small_mine, rest_mine),
        patch,
        turned(masters),
        turned(moments),
        turned(averages),
        rates,
    )
    loss_global, box_total, grad_norm = (made[23 + i].reshape(()) for i in range(3))
    results = []
    for i in range(3):
        results.extend(turned(made[7 * i : 7 * i + 7]))

    return (
        (loss_global, box_total, grad_norm, new_memory.transpose(0, 1, 3, 2)) + tuple(results) + tuple(made[21:23])
    )


def solution(mesh):
    both = ("dp", "mp")
    weight_specs = (
        P("dp", "mp"),
        P("dp", "mp"),
        P(None, both),
        P(None, both),
        P(None, both),
        P(None, None, "mp"),
        P("mp", None),
    )
    memory_spec = P(None, None, "dp", "mp")
    return jax.shard_map(
        shards,
        mesh=mesh,
        in_specs=(
            P(None, both, None),
            P("dp", None),
            P("dp", None),
            P("dp", None, None, None),
            P("dp", None, None, None),
            memory_spec,
        )
        + weight_specs * 3,
        out_specs=(P(), P(), P(), memory_spec)
        + weight_specs * 3
        + (P("dp", "mp"), P("dp", "mp")),
        check_vma=False,
    )
```

```python
import functools

import jax
import jax.numpy as jnp
from jax import lax
from jax.experimental import pallas as pl
from jax.experimental.pallas import tpu as pltpu
from jax.sharding import PartitionSpec as P

MICRO = 3
FRAME = 64
EPSILON = 1e-06
LEARNING = 300.0
VECTOR_LEARNING = 6000.0
MOMENTUM = 0.5
AVERAGING = 0.5
THRESHOLD = 0.05
PRECISE = lax.Precision.HIGHEST
QUAD = 4
bf16 = jnp.bfloat16
f32 = jnp.float32


NEAR = 60 * 1024 * 1024


def product(first_operand, second_operand):
    return jnp.dot(first_operand, second_operand, preferred_element_type=f32)


def contract_last(first_operand, second_operand):
    return lax.dot_general(
        first_operand, second_operand, (((1,), (1,)), ((), ())), preferred_element_type=f32
    )


def contract_rows(first_operand, second_operand):
    return lax.dot_general(
        first_operand, second_operand, (((0,), (0,)), ((), ())), preferred_element_type=f32
    )


def swap_dp(inputs, mask):
    size = lax.axis_size("dp")
    return lax.ppermute(inputs, "dp", [(i, i ^ mask) for i in range(size)])


def swap_mp(inputs, mask):
    size = lax.axis_size("mp")
    return lax.ppermute(inputs, "mp", [(i, i ^ mask) for i in range(size)])


def dp_bits():
    return lax.axis_size("dp").bit_length() - 1


def regroup(inputs):
    count = lax.axis_size("dp")
    pairs = []
    for d in range(count):
        for z in range(4):
            moved = (d % 2) ^ (z // 2)
            pairs.append((d * 4 + z, (d ^ moved) * 4 + (z ^ (2 * moved))))
    return lax.ppermute(inputs, ("dp", "mp"), pairs)


def pick(pieces):
    odd = lax.axis_index("mp") % 2 == 1
    return [jnp.where(odd, pieces[c ^ 1], pieces[c]) for c in range(4)]


def gather_mp(inputs):
    return [inputs] + [swap_mp(inputs, s) for s in (1, 2, 3)]


def halve_mp(pieces):
    sent = jnp.concatenate([pieces[1], pieces[3]], axis=1).astype(bf16)
    return pieces[0], (pieces[2], sent), swap_mp(sent, 1)


def halve_more(near, far, got):
    columns = near.shape[1]
    far = far[0].astype(f32) + got[:, columns:].astype(f32)
    return near.astype(f32) + got[:, :columns].astype(f32), swap_mp(far.astype(bf16), 2)


def spread_dp(inputs):
    return [inputs] + [swap_dp(inputs, b) for b in range(2, lax.axis_size("dp"), 2)]


def spread_core(pieces):
    return one_or_all(pieces + [swap_dp(p, 1) for p in pieces])


def one_or_all(pieces):
    if pieces[0].shape[0] % 16:
        pieces = [jnp.concatenate(pieces)]
    return tuple(pieces)


def halve_dp(near, far):
    got = [swap_dp(f, 1) for f in far]
    count = lax.axis_size("dp") // 2
    rows = near[0].shape[0] // count
    return [
        jnp.concatenate(
            [
                n[i * rows : (i + 1) * rows].astype(f32) + g[i * rows : (i + 1) * rows].astype(f32)
                for n, g in zip(near, got)
            ],
            axis=1,
        ).astype(bf16)
        for i in range(count)
    ]


def trade_dp(pieces, first, last):
    return [swap_dp(piece, 2 * first + 2 * i) for i, piece in enumerate(pieces[first:last])]


def after(value, *events):
    return lax.optimization_barrier((value,) + events)[0]


def group_sum_features(inputs):
    count = lax.axis_size("dp")
    width = inputs.shape[1] // count
    order = [b for b in range(count) if b % 2 == 0] + [b for b in range(count) if b % 2]
    at = [order.index(b ^ 1) for b in order]
    pairs = [(d * 4 + z, (d ^ 1) * 4 + (z ^ 1)) for d in range(count) for z in range(4)]
    got = swap_dp(inputs, 1) + lax.ppermute(inputs, ("dp", "mp"), pairs)
    inputs = inputs + swap_mp(inputs, 1)
    return inputs + jnp.concatenate([got[:, p * width : (p + 1) * width] for p in at], axis=1)


def call(
    body, grid, in_specs, out_specs, out_shape, operands, flops, scratch=(), alias=None, events=()
):
    known, late = len(operands), len(operands) + len(events)

    def run(*refs):
        body(*refs[:known], *refs[late:])

    return pl.pallas_call(
        run,
        grid=grid,
        in_specs=list(in_specs) + [pl.BlockSpec(memory_space=pl.ANY)] * len(events),
        out_specs=out_specs,
        out_shape=out_shape,
        scratch_shapes=list(scratch),
        input_output_aliases=alias or {},
        compiler_params=pltpu.CompilerParams(vmem_limit_bytes=NEAR),
        cost_estimate=pl.CostEstimate(flops=1000, bytes_accessed=1000, transcendentals=0),
    )(*operands, *events)


def whole(array):
    return pl.BlockSpec(array.shape, lambda *i, n=len(array.shape): (0,) * n)


def transfers(pieces, targets, sems):
    copies, at = [], 0
    for piece in pieces:
        rows = piece.shape[0]
        for column, target in targets:
            copies.append(
                pltpu.make_async_copy(
                    piece.at[:, column : column + target.shape[1]],
                    target.at[at : at + rows],
                    sems.at[len(copies)],
                )
            )
        at += rows
    return copies


def begin(copies):
    for copy in copies:
        copy.start()


def finish(copies):
    for copy in copies:
        copy.wait()


def fetch(pieces, targets, sems):
    copies = transfers(pieces, targets, sems)
    begin(copies)
    finish(copies)


def standard(inputs):
    centered = inputs - jnp.mean(inputs, axis=-1, keepdims=True)
    scale = lax.rsqrt(jnp.mean(centered * centered, axis=-1, keepdims=True) + EPSILON)
    return centered * scale, scale


def standard_back(grad, unit, scale):
    return scale * (
        grad
        - jnp.mean(grad, axis=-1, keepdims=True)
        - unit * jnp.mean(grad * unit, axis=-1, keepdims=True)
    )


def memory_in_kernel(index_ref, order_ref, *refs):
    parts, (out_ref, held, sems) = refs[:4], refs[4:]
    columns = parts[0].shape[2]

    def copy(p, c):
        target = held.at[:, :, c * columns : (c + 1) * columns]
        return pltpu.make_async_copy(parts[p], target, sems.at[c])

    for c in range(4):
        for p in range(4):

            @pl.when(index_ref[c] == p)
            def _(p=p, c=c):
                copy(p, c).start()

    for c in range(4):
        copy(0, c).wait()
    order = order_ref[...]
    for m in range(2):
        for ch in range(2):
            out_ref[m, ch] = contract_last(order, held[m, ch]).astype(bf16)


def memory_in(index, order, parts, events=()):
    _, _, columns, rows = parts[0].shape
    return call(
        memory_in_kernel,
        (1,),
        [pl.BlockSpec(memory_space=pltpu.SMEM), whole(order)]
        + [pl.BlockSpec(memory_space=pl.ANY)] * 4,
        pl.BlockSpec((2, 2, rows, 4 * columns), lambda i: (0, 0, 0, 0)),
        jax.ShapeDtypeStruct((2, 2, rows, 4 * columns), bf16),
        (index, order) + tuple(parts),
        0,
        scratch=[
            pltpu.VMEM((2, 2, 4 * columns, rows), bf16),
            pltpu.SemaphoreType.DMA((4,)),
        ],
        events=events,
    )


def memory_out_kernel(index_ref, order_ref, *refs):
    out_ref, turned = refs[-2:]
    columns = turned.shape[0] // 4
    at = pl.multiple_of(index_ref[0] * columns, 64)
    for m in range(2):
        rows = jnp.concatenate([r[0, 0] for r in refs[4 * m : 4 * m + 4]])
        turned[...] = contract_rows(rows, order_ref[...])
        out_ref[m, 0] = turned[pl.ds(at, columns)].astype(bf16)


def memory_out(index, order, parts, events=()):
    _, _, rows, width = parts[0][0].shape
    return call(
        memory_out_kernel,
        (2,),
        [
            pl.BlockSpec(memory_space=pltpu.SMEM),
            pl.BlockSpec((4 * rows, 4 * rows), lambda i: (0, 0)),
        ]
        + [pl.BlockSpec((1, 1, rows, width), lambda i, m=m: (m, i, 0, 0)) for _, m in parts],
        pl.BlockSpec((2, 1, width // 4, 4 * rows), lambda i: (0, i, 0, 0)),
        jax.ShapeDtypeStruct((2, 2, width // 4, 4 * rows), bf16),
        (index, order) + tuple(a for a, _ in parts),
        8 * (4 * rows) ** 2 * width,
        scratch=[pltpu.VMEM((width, 4 * rows), f32)],
        events=events,
    )


def join_kernel(main, odd_ref, *refs):
    pieces, out_ref = refs[:-1], refs[-1]
    odd = odd_ref[0] == 1
    for c in range(4):
        out_ref[:, c * main : (c + 1) * main] = pieces[c][:, :main]
    tails = [p[:, main:].astype(f32) for p in pieces]
    heads = [jnp.where(odd, tails[c ^ 1], tails[c]) for c in range(4)]
    out_ref[:, 4 * main :] = jnp.concatenate(heads, axis=1).astype(bf16)


def join(main, odd, pieces):
    rows, columns = pieces[0].shape
    return call(
        functools.partial(join_kernel, main),
        (1,),
        [pl.BlockSpec(memory_space=pltpu.SMEM)] + [whole(p) for p in pieces],
        pl.BlockSpec((rows, 4 * columns), lambda i: (0, 0)),
        jax.ShapeDtypeStruct((rows, 4 * columns), bf16),
        (odd,) + tuple(pieces),
        0,
    )


def embed_kernel(count, patch_ref, order_ref, taps_ref, *refs):
    pieces = refs[:count]
    (
        sorted_ref, embedded_ref, normed_ref, query_ref, key_ref, value_ref, pool_ref,
        vec_ref, head_ref, qk_s, v_s, small_s, sems,
    ) = refs[count:]
    width = embedded_ref.shape[1]
    edge = small_s.shape[1] - 128

    @pl.when(pl.program_id(0) == 0)
    def _():
        fetch(pieces, ((0, qk_s), (2 * width, v_s), (3 * width, small_s)), sems)
        turned = small_s[:, edge:].astype(f32).T
        vec_ref[...] = turned[0:8] + turned[8:16] + turned[16:24]
        head_ref[...] = turned[24 : 24 + head_ref.shape[0]].astype(bf16)

    patch = contract_last(order_ref[...], patch_ref[0]).astype(bf16)
    sorted_ref[...] = patch
    embedded = contract_last(patch, small_s[:, : patch.shape[1]]) + vec_ref[0:1]
    embedded_ref[...] = embedded
    unit, _ = standard(embedded)
    normed = (unit * vec_ref[1:2] + vec_ref[2:3]).astype(bf16)
    normed_ref[...] = normed
    query_ref[...] = product(normed, qk_s[:, :width]).astype(bf16)
    for ch, weight, raw_ref in ((0, qk_s[:, width:], key_ref), (1, v_s[...], value_ref)):
        raw = product(normed, weight)
        raw_ref[...] = raw.astype(bf16)
        rows = raw.shape[0] // 4
        pooled = raw[:rows] * taps_ref[ch, 0:1]
        for t in range(1, 4):
            pooled = pooled + raw[t * rows : (t + 1) * rows] * taps_ref[ch, t : t + 1]
        pool_ref[0, ch] = pooled.astype(bf16)


def embed(patches_t, order, taps, weights, classes, events=()):
    _, patch, rows = patches_t.shape
    width = taps.shape[2]
    total = MICRO * rows
    edge = weights[0].shape[1] - 3 * width

    def tile(columns):
        return pl.BlockSpec((rows, columns), lambda i: (i, 0))

    return call(
        functools.partial(embed_kernel, len(weights)),
        (MICRO,),
        [pl.BlockSpec((1, patch, rows), lambda i: (i, 0, 0)), whole(order), whole(taps)]
        + [pl.BlockSpec(memory_space=pl.ANY)] * len(weights),
        [tile(patch), tile(width), tile(width), tile(width), tile(width), tile(width)]
        + [
            pl.BlockSpec((1, 2, rows // 4, width), lambda i: (i, 0, 0, 0)),
            pl.BlockSpec((8, width), lambda i: (0, 0)),
            pl.BlockSpec((classes, width), lambda i: (0, 0)),
        ],
        [
            jax.ShapeDtypeStruct((total, patch), bf16),
            jax.ShapeDtypeStruct((total, width), f32),
        ]
        + [jax.ShapeDtypeStruct((total, width), bf16)] * 4
        + [
            jax.ShapeDtypeStruct((MICRO, 2, rows // 4, width), bf16),
            jax.ShapeDtypeStruct((8, width), f32),
            jax.ShapeDtypeStruct((classes, width), bf16),
        ],
        (patches_t, order, taps) + weights,
        2 * total * width * (patch + 3 * width),
        scratch=[
            pltpu.VMEM((width, 2 * width), bf16),
            pltpu.VMEM((width, width), bf16),
            pltpu.VMEM((width, edge), bf16),
            pltpu.SemaphoreType.DMA((3 * len(weights),)),
        ],
        events=events,
    )


def attend_kernel(sources, q_ref, taps_ref, bias_ref, *refs):
    count = sum(sources)
    now, newer = refs[: sources[0]], refs[sources[0] : sources[0] + sources[1]]
    older = refs[sources[0] + sources[1] : count]
    out_ref, prob_ref, key_ref, value_ref = refs[-4:]
    query = q_ref[...]
    rows, width = query.shape
    size = width // QUAD
    for ch, target in ((0, key_ref), (1, value_ref)):
        at = 0
        for r in now:
            n = r.shape[2]
            target[at : at + n] = r[0, ch]
            at += n
        first, second = taps_ref[ch, 4:5], taps_ref[ch, 5:6]
        for r in newer + older:
            n = r.shape[2] // 2
            target[at : at + n] = (
                r[0, ch, :n].astype(f32) * first + r[0, ch, n:].astype(f32) * second
            ).astype(bf16)
            at += n
    keys_t = key_ref[...].T
    values = value_ref[...]
    lane = lax.broadcasted_iota(jnp.int32, (rows, width), 1) // size
    scaled = query * (size**-0.5)
    total = query.astype(f32)
    def score(h):
        own = jnp.where(lane == h, scaled, jnp.zeros_like(scaled))
        return product(own, keys_t) + bias_ref[0, h : h + 1, :]

    following = score(0)
    for h in range(QUAD):
        scores = following
        if h + 1 < QUAD:
            following = score(h + 1)
        top = jnp.max(scores, axis=-1, keepdims=True)
        exponent = jnp.exp(scores - top)
        denominator = jnp.sum(exponent, axis=-1, keepdims=True)
        probs = (exponent * (1.0 / denominator)).astype(bf16)
        prob_ref[h] = probs
        total = total + jnp.where(lane == h, product(probs, values), 0.0)
    out_ref[...] = total.astype(bf16)


def source_specs(entries, block):
    return [
        pl.BlockSpec((1, 2, a.shape[2], block), lambda i, m=m: (m, 0, 0, i)) for a, m in entries
    ]


def attend(micro, query, taps, bias, now, newer, older, before, events=()):
    rows = query.shape[0] // MICRO
    width = query.shape[1]
    count = bias.shape[2]
    quads = bias.shape[0]
    block = width // quads
    entries = now + newer + older
    operands = (query, taps, bias) + tuple(a for a, _ in entries)
    specs = [
        pl.BlockSpec((rows, block), lambda i: (micro, i)),
        pl.BlockSpec((2, 6, block), lambda i: (0, 0, i)),
        pl.BlockSpec((1, QUAD, count), lambda i: (i, 0, 0)),
    ] + source_specs(entries, block)
    alias = {}
    if before is not None:
        alias = {len(operands): 0}
        operands = operands + (before,)
        specs.append(pl.BlockSpec(memory_space=pl.ANY))
    return call(
        functools.partial(attend_kernel, (len(now), len(newer), len(older))),
        (quads,),
        specs,
        [
            pl.BlockSpec((rows, block), lambda i: (micro, i)),
            pl.BlockSpec((QUAD, rows, count), lambda i: (i, 0, 0)),
            pl.BlockSpec((count, block), lambda i: (0, i)),
            pl.BlockSpec((count, block), lambda i: (0, i)),
        ],
        [
            jax.ShapeDtypeStruct(query.shape, bf16),
            jax.ShapeDtypeStruct((quads * QUAD, rows, count), bf16),
            jax.ShapeDtypeStruct((count, width), bf16),
            jax.ShapeDtypeStruct((count, width), bf16),
        ],
        operands,
        4 * rows * count * width * 4,
        alias=alias,
        events=events,
    )


def attend_back_kernel(sources, q_ref, k_ref, v_ref, prob_ref, grad_ref, *refs):
    entries = refs[: sum(sources)]
    dq_ref, keep_ref, send_ref, taps_ref, bias_ref = refs[-5:]
    query = q_ref[...]
    grad = grad_ref[...]
    rows, width = query.shape
    size = width // QUAD
    keys = k_ref[...]
    count = keys.shape[0]
    values_t = v_ref[...].T
    query_t = query.T
    grad_t = grad.T
    scaling = size**-0.5
    lane = lax.broadcasted_iota(jnp.int32, (rows, width), 1) // size
    total = jnp.zeros((rows, width), f32)
    ones = jnp.ones((16, rows), bf16)
    half = count // 2
    spot = lax.broadcasted_iota(jnp.int32, (1, 128), 1)
    key_parts, value_parts = [], []
    def pull(h):
        own = jnp.where(lane == h, grad, jnp.zeros_like(grad))
        return product(own, values_t)

    following = pull(0)
    for h in range(QUAD):
        current = following
        if h + 1 < QUAD:
            following = pull(h + 1)
        probs_low = prob_ref[h]
        probs = probs_low.astype(f32)
        pulled = probs * current
        shift = jnp.sum(pulled, axis=-1, keepdims=True)
        score_grad = (pulled - probs * shift).astype(bf16)
        total = total + jnp.where(lane == h, product(score_grad, keys), 0.0)
        left = jnp.concatenate([query_t[h * size : (h + 1) * size], ones])
        found = product(left, score_grad)
        key_parts.append(found[:size])
        sums = found[size : size + 1]
        row = jnp.zeros((1, 128), f32)
        for g, (a, b) in enumerate(((0, half), (half, half + half // 2), (half + half // 2, count))):
            row = row + jnp.where(spot == g, jnp.sum(sums[:, a:b], axis=1, keepdims=True), 0.0)
        bias_ref[0, h : h + 1, :] = row
        value_parts.append(product(grad_t[h * size : (h + 1) * size], probs_low))
    dq_ref[...] = (total * scaling + grad.astype(f32)).astype(bf16)
    part = keep_ref.shape[2]
    for ch, parts, factor in ((0, key_parts, scaling), (1, value_parts, 1.0)):
        found = jnp.concatenate(parts).T * factor
        for s in range(4):
            target = send_ref if s % 2 else keep_ref
            target[s // 2, ch] = found[s * part : (s + 1) * part].astype(bf16)
        at = half
        first = jnp.zeros((1, width), f32)
        second = jnp.zeros((1, width), f32)
        for r in entries:
            n = r.shape[2] // 2
            piece = found[at : at + n]
            first = first + jnp.sum(piece * r[0, ch, :n].astype(f32), axis=0, keepdims=True)
            second = second + jnp.sum(piece * r[0, ch, n:].astype(f32), axis=0, keepdims=True)
            at += n
        taps_ref[ch, 0:1] = first
        taps_ref[ch, 1:2] = second


def attend_back(micro, query, keys, values, probs, grad, newer, older, before, events=()):
    heads, rows, count = probs.shape
    width = query.shape[1]
    quads = heads // QUAD
    block = width // quads
    entries = newer + older
    operands = (query, keys, values, probs, grad) + tuple(a for a, _ in entries)
    specs = [
        pl.BlockSpec((rows, block), lambda i: (micro, i)),
        pl.BlockSpec((count, block), lambda i: (0, i)),
        pl.BlockSpec((count, block), lambda i: (0, i)),
        pl.BlockSpec((QUAD, rows, count), lambda i: (i, 0, 0)),
        pl.BlockSpec((rows, block), lambda i: (micro, i)),
    ] + source_specs(entries, block)
    alias = {}
    if before is not None:
        alias = {len(operands): 0}
        operands = operands + (before,)
        specs.append(pl.BlockSpec(memory_space=pl.ANY))
    part = count // 8
    return call(
        functools.partial(attend_back_kernel, (len(newer), len(older))),
        (quads,),
        specs,
        [
            pl.BlockSpec((rows, block), lambda i: (micro, i)),
            pl.BlockSpec((2, 2, part, block), lambda i: (0, 0, 0, i)),
            pl.BlockSpec((2, 2, part, block), lambda i: (0, 0, 0, i)),
            pl.BlockSpec((2, 2, block), lambda i: (0, 0, i)),
            pl.BlockSpec((1, QUAD, 128), lambda i: (i, 0, 0)),
        ],
        [
            jax.ShapeDtypeStruct(query.shape, bf16),
            jax.ShapeDtypeStruct((2, 2, part, width), bf16),
            jax.ShapeDtypeStruct((2, 2, part, width), bf16),
            jax.ShapeDtypeStruct((2, 2, width), f32),
            jax.ShapeDtypeStruct((quads, QUAD, 128), f32),
        ],
        operands,
        8 * rows * count * width * 4,
        alias=alias,
        events=events,
    )


def gelu_pair(inputs):
    size = jnp.abs(inputs)
    t = 1.0 / (1.0 + (0.3275911 * 0.5**0.5) * size)
    bell = jnp.exp(-0.5 * inputs * inputs)
    tail = (
        t
        * (
            0.5 * 0.254829592
            + t
            * (
                0.5 * -0.284496736
                + t * (0.5 * 1.421413741 + t * (0.5 * -1.453152027 + t * (0.5 * 1.061405429)))
            )
        )
        * bell
    )
    share = jnp.where(inputs > 0.0, 1.0 - tail, tail)
    return inputs * share, share + inputs * bell * 0.3989422804014327


def mlp_weights(width, units, count):
    return [
        pltpu.VMEM((width, width), bf16),
        pltpu.VMEM((width, 2 * units), bf16),
        pltpu.SemaphoreType.DMA((count,)),
        pltpu.SemaphoreType.DMA((count,)),
    ]


def mlp_kernel(count, attended_ref, embedded_ref, vec_ref, select_ref, *refs):
    (
        first_ref, normed_ref, active_ref, slope_ref, second_ref, feature_ref,
        out_s, both_s, out_sems, sems,
    ) = refs[count:]
    units = both_s.shape[1] // 2
    out_copies = transfers(refs[:count], ((2 * units, out_s),), out_sems)
    copies = transfers(refs[:count], ((0, both_s),), sems)
    starting = pl.program_id(0) == 0

    @pl.when(starting)
    def _():
        begin(out_copies)
        begin(copies)
        finish(out_copies)

    first = embedded_ref[...] + contract_last(attended_ref[...], out_s[...])
    first_ref[...] = first
    unit, _ = standard(first)
    normed = (unit * vec_ref[3:4] + vec_ref[4:5]).astype(bf16)
    normed_ref[...] = normed
    total = first

    @pl.when(starting)
    def _():
        finish(copies)

    chunk = units // 4

    def entry(s):
        return product(normed, both_s[:, (2 * s + 1) * chunk : (2 * s + 2) * chunk])

    following = entry(0)
    for s in range(4):
        at = s * chunk
        hidden = following
        if s < 3:
            following = entry(s + 1)
        value, slope = gelu_pair(hidden)
        value = value.astype(bf16)
        active_ref[:, at : at + chunk] = value
        slope_ref[:, at : at + chunk] = slope.astype(bf16)
        total = total + contract_last(value, both_s[:, 2 * at : 2 * at + chunk])
    second_ref[...] = total
    unit, _ = standard(total)
    final = unit * vec_ref[5:6] + vec_ref[6:7]
    feature_ref[0] = jnp.dot(
        select_ref[0], final, precision=PRECISE, preferred_element_type=f32
    )


def mlp(attended, embedded, vec, select, weights, events=()):
    total, width = embedded.shape
    rows = total // MICRO
    units = (weights[0].shape[1] - width) // 2
    boxes = select.shape[1]

    def tile(columns):
        return pl.BlockSpec((rows, columns), lambda i: (i, 0))

    return call(
        functools.partial(mlp_kernel, len(weights)),
        (MICRO,),
        [
            tile(width),
            tile(width),
            whole(vec),
            pl.BlockSpec((1, boxes, rows), lambda i: (i, 0, 0)),
        ]
        + [pl.BlockSpec(memory_space=pl.ANY)] * len(weights),
        [tile(width), tile(width), tile(units), tile(units), tile(width)]
        + [pl.BlockSpec((1, boxes, width), lambda i: (i, 0, 0))],
        [
            jax.ShapeDtypeStruct((total, width), f32),
            jax.ShapeDtypeStruct((total, width), bf16),
            jax.ShapeDtypeStruct((total, units), bf16),
            jax.ShapeDtypeStruct((total, units), bf16),
            jax.ShapeDtypeStruct((total, width), f32),
            jax.ShapeDtypeStruct((MICRO, boxes, width), f32),
        ],
        (attended, embedded, vec, select) + weights,
        2 * total * width * (width + 2 * units),
        scratch=mlp_weights(width, units, len(weights)),
        events=events,
    )


def mlp_back_kernel(
    count, pull_ref, select_ref, second_ref, first_ref, slope_ref, vec_ref, *refs
):
    (
        branch_ref, hidden_ref, attn_ref, first_grad_ref, attended_ref, sums_ref,
        out_s, both_s, out_sems, sems,
    ) = refs[count:]
    units = both_s.shape[1] // 2
    out_copies = transfers(refs[:count], ((2 * units, out_s),), out_sems)
    copies = transfers(refs[:count], ((0, both_s),), sems)
    starting = pl.program_id(0) == 0

    @pl.when(starting)
    def _():
        begin(copies)
        begin(out_copies)
        sums_ref[...] = jnp.zeros_like(sums_ref)

    pull = lax.dot_general(
        select_ref[0],
        pull_ref[0],
        (((0,), (0,)), ((), ())),
        precision=PRECISE,
        preferred_element_type=f32,
    )
    unit, scale = standard(second_ref[...])
    sums_ref[2:3] += jnp.sum(pull * unit, axis=0, keepdims=True)
    sums_ref[3:4] += jnp.sum(pull, axis=0, keepdims=True)
    second_grad = standard_back(pull * vec_ref[5:6], unit, scale)
    branch = second_grad.astype(bf16)
    branch_ref[...] = branch

    @pl.when(starting)
    def _():
        finish(copies)

    chunk = units // 4
    normed_grad = jnp.zeros(second_grad.shape, f32)

    for s in range(4):
        at = s * chunk
        active_grad = product(branch, both_s[:, 2 * at : 2 * at + chunk])
        hidden_grad = (active_grad * slope_ref[:, at : at + chunk].astype(f32)).astype(bf16)
        hidden_ref[:, at : at + chunk] = hidden_grad
        normed_grad = normed_grad + contract_last(
            hidden_grad, both_s[:, 2 * at + chunk : 2 * at + 2 * chunk]
        )

    @pl.when(starting)
    def _():
        finish(out_copies)

    unit, scale = standard(first_ref[...])
    sums_ref[0:1] += jnp.sum(normed_grad * unit, axis=0, keepdims=True)
    sums_ref[1:2] += jnp.sum(normed_grad, axis=0, keepdims=True)
    first_grad = standard_back(normed_grad * vec_ref[3:4], unit, scale) + second_grad
    first_grad_ref[...] = first_grad
    attn = first_grad.astype(bf16)
    attn_ref[...] = attn
    attended_ref[...] = product(attn, out_s[...]).astype(bf16)


def mlp_back(pull, select, second, first, slope, vec, weights, events=()):
    total, width = second.shape
    rows = total // MICRO
    units = (weights[0].shape[1] - width) // 2
    boxes = select.shape[1]

    def tile(columns):
        return pl.BlockSpec((rows, columns), lambda i: (i, 0))

    return call(
        functools.partial(mlp_back_kernel, len(weights)),
        (MICRO,),
        [
            pl.BlockSpec((1, boxes, width), lambda i: (i, 0, 0)),
            pl.BlockSpec((1, boxes, rows), lambda i: (i, 0, 0)),
            tile(width),
            tile(width),
            tile(units),
            whole(vec),
        ]
        + [pl.BlockSpec(memory_space=pl.ANY)] * len(weights),
        [tile(width), tile(units), tile(width), tile(width), tile(width)]
        + [pl.BlockSpec((8, width), lambda i: (0, 0))],
        [
            jax.ShapeDtypeStruct((total, width), bf16),
            jax.ShapeDtypeStruct((total, units), bf16),
            jax.ShapeDtypeStruct((total, width), bf16),
            jax.ShapeDtypeStruct((total, width), f32),
            jax.ShapeDtypeStruct((total, width), bf16),
            jax.ShapeDtypeStruct((8, width), f32),
        ],
        (pull, select, second, first, slope, vec) + weights,
        2 * total * width * (width + 2 * units),
        scratch=mlp_weights(width, units, len(weights)),
        events=events,
    )


def embed_back_kernel(
    count, dq_ref, key_ref, value_ref, taps_ref, embedded_ref, first_ref, normed_ref, patch_ref,
    vec_ref, head_ref, more_ref, *refs
):
    pools = refs[: 3 * MICRO]
    (
        near_ref, far_ref, taps_out, qk_s, v_s, pool_s, sums_s, normed_s, projected_s, grad_s,
        patch_s, sems,
    ) = refs[3 * MICRO + count :]
    rows, width = embedded_ref.shape
    step = pl.program_id(0)

    @pl.when(step == 0)
    def _():
        sums_s[...] = jnp.zeros_like(sums_s)
        sums_s[3:7] = more_ref[0:4]
        sums_s[8 : 8 + head_ref.shape[0]] = head_ref[...]
        taps_out[...] = jnp.zeros_like(taps_out)
        patch_s[...] = jnp.zeros_like(patch_s)
        for m in range(MICRO):
            kept, got, far = pools[3 * m : 3 * m + 3]
            for ch in range(2):
                pool_s[m, ch] = (
                    kept[0, ch].astype(f32) + got[0, ch].astype(f32) + far[ch].astype(f32)
                )
        fetch(refs[3 * MICRO : 3 * MICRO + count], ((0, qk_s), (2 * width, v_s)), sems)

    at = pl.multiple_of(step * rows, 128)
    here = pl.ds(at, rows)
    projected_s[here, :width] = dq_ref[...]
    pooled = rows // 4
    for ch, raw_ref in ((0, key_ref), (1, value_ref)):
        pool = pool_s[step, ch]
        for t in range(4):
            projected_s[
                pl.ds(at + t * pooled, pooled), (1 + ch) * width : (2 + ch) * width
            ] = (pool * taps_ref[ch, t : t + 1]).astype(bf16)
            raw = raw_ref[t * pooled : (t + 1) * pooled].astype(f32)
            taps_out[4 * ch + t : 4 * ch + t + 1] += jnp.sum(pool * raw, axis=0, keepdims=True)
    normed_grad = contract_last(projected_s[here, : 2 * width], qk_s[...])
    normed_grad = normed_grad + contract_last(projected_s[here, 2 * width :], v_s[...])
    unit, scale = standard(embedded_ref[...])
    sums_s[1:2] += jnp.sum(normed_grad * unit, axis=0, keepdims=True)
    sums_s[2:3] += jnp.sum(normed_grad, axis=0, keepdims=True)
    grad = standard_back(normed_grad * vec_ref[1:2], unit, scale) + first_ref[...]
    grad = grad.astype(bf16)
    sums_s[0:1] += jnp.sum(grad.astype(f32), axis=0, keepdims=True)
    normed_s[:, here] = normed_ref[...].T
    grad_s[:, here] = grad.T
    patch_s[here, : patch_ref.shape[1]] = patch_ref[...]

    @pl.when(step == MICRO - 1)
    def _():
        half = width // 2
        edge = 3 * width + patch_s.shape[1]
        for out_ref, top in ((far_ref, half), (near_ref, 0)):
            part = slice(top, top + half)
            for c in range(3):
                out_ref[:, c * width : (c + 1) * width] = product(
                    normed_s[part], projected_s[:, c * width : (c + 1) * width]
                ).astype(bf16)
            out_ref[:, 3 * width : edge] = product(grad_s[part], patch_s[...]).astype(bf16)
            out_ref[:, edge:] = sums_s[:, part].T.astype(bf16)


def embed_back(
    dq, keys, values, taps, embedded, first_grad, normed, patches, vec, head, more, pools, weights,
    events=(),
):
    total, width = embedded.shape
    rows = total // MICRO
    patch = patches.shape[1]
    edge = patch + (-patch % 128)
    columns = 3 * width + edge + 128

    def tile(columns):
        return pl.BlockSpec((rows, columns), lambda i: (i, 0))

    operands = (dq, keys, values, taps, embedded, first_grad, normed, patches, vec, head, more)
    half = pl.BlockSpec((width // 2, columns), lambda i: (0, 0))
    return call(
        functools.partial(embed_back_kernel, len(weights)),
        (MICRO,),
        [tile(width)] * 3
        + [whole(taps)]
        + [tile(width)] * 3
        + [tile(patch)]
        + [whole(a) for a in (vec, head, more) + pools]
        + [pl.BlockSpec(memory_space=pl.ANY)] * len(weights),
        [half, half, pl.BlockSpec((8, width), lambda i: (0, 0))],
        [
            jax.ShapeDtypeStruct((width // 2, columns), bf16),
            jax.ShapeDtypeStruct((width // 2, columns), bf16),
            jax.ShapeDtypeStruct((8, width), f32),
        ],
        operands + pools + weights,
        2 * total * width * 3 * width,
        scratch=[
            pltpu.VMEM((width, 2 * width), bf16),
            pltpu.VMEM((width, width), bf16),
            pltpu.VMEM((MICRO, 2, rows // 4, width), f32),
            pltpu.VMEM((128, width), f32),
            pltpu.VMEM((width, total), bf16),
            pltpu.VMEM((total, 3 * width), bf16),
            pltpu.VMEM((width, total), bf16),
            pltpu.VMEM((total, edge), bf16),
            pltpu.SemaphoreType.DMA((2 * len(weights),)),
        ],
        events=events,
    )


def squares_kernel(*refs):
    grads, flat_ref, outs = refs[:6], refs[6], refs[7:]
    total = 0.0
    for i in range(3):
        found = grads[2 * i][...].astype(f32) + grads[2 * i + 1][...].astype(f32)
        outs[i][...] = found
        total = total + jnp.sum(found * found)
    rows = flat_ref.shape[0]
    outs[3][...] = jnp.zeros_like(outs[3]) + total
    outs[3][:rows] = flat_ref[...]


def squares_of(attn, small, rest, flat, events=()):
    operands = tuple(attn) + tuple(small) + tuple(rest) + (flat,)
    rows = flat.shape[0] + (-flat.shape[0] % 8)
    rows += 8 * (rows == flat.shape[0])
    shapes = [jax.ShapeDtypeStruct(g[0].shape, f32) for g in (attn, small, rest)]
    shapes.append(jax.ShapeDtypeStruct((rows, flat.shape[1]), f32))
    return call(
        squares_kernel,
        (1,),
        [whole(o) for o in operands],
        [whole(o) for o in shapes],
        shapes,
        operands,
        0,
        events=events,
    )


def update_kernel(rates, patch, odd_ref, own_ref, one_ref, two_ref, three_ref, *refs):
    count = len(rates)
    near = own_ref[...] + one_ref[...]
    away = two_ref[...] + three_ref[...]
    attn_ref, small_ref, rest_ref = refs[:3]
    weights, moments, averages = (refs[3 + i * count : 3 + (i + 1) * count] for i in range(3))
    outs = refs[3 + 3 * count :]
    heads = weights[6].shape[0] * 3
    blocks = []
    square = near[52:53, 0:1] + away[52:53, 0:1]
    spot = lax.broadcasted_iota(jnp.int32, (13, near.shape[1]), 1)
    row = lax.broadcasted_iota(jnp.int32, (13, near.shape[1]), 0)
    counted = (row < 12) | (spot < heads)
    for c in range(4):
        far = 13 * (c ^ 2)
        block = near[13 * c : 13 * c + 13] + away[far : far + 13]
        kept = jnp.where(counted, block, 0.0)
        square = square + jnp.sum(kept * kept)
        blocks.append(block)
    mine = jnp.where(odd_ref[0] == 1, blocks[1], blocks[0])
    boxes = blocks[0][12:13, heads + 1 : heads + 2]
    norm = jnp.sqrt(square) / boxes
    outs[-3][...] = blocks[0][12:13, heads : heads + 1]
    outs[-2][...] = boxes
    outs[-1][...] = norm
    scaling = jnp.minimum(1.0, THRESHOLD / norm) / boxes
    hidden = weights[0].shape[1] - attn_ref.shape[1]
    edge = small_ref.shape[1] - 128
    classes = weights[3].shape[1]
    tail = small_ref[:, edge:]

    def step(i, at, grad):
        grad = grad * scaling
        moment = MOMENTUM * moments[i][at] + grad
        updated = weights[i][at] - rates[i] * (grad + MOMENTUM * moment)
        outs[i][at] = updated
        outs[count + i][at] = moment
        outs[2 * count + i][at] = AVERAGING * averages[i][at] + (1.0 - AVERAGING) * updated
        if i < 2:
            outs[3 * count + i][at] = updated.astype(bf16)

    step(0, ..., jnp.concatenate([attn_ref[...], rest_ref[:, :hidden]], axis=1))
    step(1, ..., rest_ref[:, hidden:])
    step(2, ..., small_ref[:, :patch])
    step(3, ..., tail[:, 8 : 8 + classes])
    step(4, ..., tail.T[:7])
    for t in range(6):
        step(5, t, mine[2 * t : 2 * t + 2])
    for h in range(heads // 3):
        step(6, slice(h, h + 1), mine[12:13, 3 * h : 3 * h + 3])


def update(odd, parts, grads, patch, weights, moments, averages, rates):
    operands = (odd,) + parts + grads + weights + moments + averages
    kept = [jax.ShapeDtypeStruct(w.shape, f32) for w in weights]
    shapes = kept * 3 + [jax.ShapeDtypeStruct(w.shape, bf16) for w in weights[:2]]
    shapes = shapes + [jax.ShapeDtypeStruct((1, 1), f32)] * 3
    return call(
        functools.partial(update_kernel, rates, patch),
        (1,),
        [pl.BlockSpec(memory_space=pltpu.SMEM)] + [whole(o) for o in operands[1:]],
        [pl.BlockSpec(o.shape, lambda i, n=len(o.shape): (0,) * n) for o in shapes],
        shapes,
        operands,
        0,
    )


def one_hot_rows(index, count):
    return (index[:, None] == jnp.arange(count)[None, :]).astype(bf16)


def shards(
    patches,
    clip_len,
    box_count,
    box_bounds,
    box_labels,
    memory,
    up_weight,
    down_weight,
    embed_weight,
    head_weight,
    vector_weight,
    conv_weight,
    position_bias,
    up_moment,
    down_moment,
    embed_moment,
    head_moment,
    vector_moment,
    conv_moment,
    position_moment,
    up_average,
    down_average,
    embed_average,
    head_average,
    vector_average,
    conv_average,
    position_average,
):
    dp_index = lax.axis_index("dp")
    mp_index = lax.axis_index("mp")
    dp_count = lax.axis_size("dp")
    across, core = mp_index % 2, dp_index % 2
    upper = mp_index - across
    quarter = 2 * core + across
    rows = patches.shape[1]
    eighth = rows // 8
    pooled = rows // 4
    half_pool = pooled // 2
    head_cols = conv_weight.shape[2]
    width = 4 * head_cols
    sub = embed_weight.shape[1]
    patch = embed_weight.shape[0]
    classes = head_weight.shape[0]
    boxes = box_bounds.shape[2]
    own_heads = position_bias.shape[0]
    heads = own_heads * 4
    hidden_cols = up_weight.shape[1] - 3 * head_cols

    ints = jnp.concatenate(
        [clip_len.reshape(-1), box_count.reshape(-1), box_bounds.reshape(-1), box_labels.reshape(-1)]
    )
    total_ints = ints.shape[0]
    ints = jnp.pad(ints, (0, -total_ints % 1024)).reshape(-1, 128)
    ints = regroup(ints).reshape(-1)
    lengths_all = ints[:5]
    counts = ints[5:8]
    bounds = ints[8 : 8 + MICRO * boxes * 2].reshape(MICRO, boxes, 2)
    labels = ints[8 + MICRO * boxes * 2 : total_ints].reshape(MICRO * boxes, classes)

    def in_three(array):
        high = lax.reduce_precision(array, 8, 7)
        middle = lax.reduce_precision(array - high, 8, 7)
        return [high, middle, array - high - middle]

    edge = patch + (-patch % 128)
    columns_in = [jnp.pad(embed_weight, ((0, edge - patch), (0, 0)))]
    columns_in += [jnp.pad(v, ((0, 1), (0, 0))) for v in in_three(vector_weight)]
    columns_in += [jnp.pad(head_weight, ((0, 128 - 24 - classes), (0, 0)))]
    taps_pos = jnp.concatenate(
        [
            conv_weight.reshape(12, head_cols),
            jnp.pad(position_bias.reshape(1, -1), ((0, 0), (0, head_cols - position_bias.size))),
        ]
    )
    taps_pos = jnp.concatenate(in_three(taps_pos)).reshape(sub, -1)
    small = jnp.concatenate([jnp.concatenate(columns_in).T, taps_pos], axis=1).astype(bf16)
    strip = -(-small.shape[1] // 512) * 128
    small = jnp.pad(small, ((0, 0), (0, 4 * strip - small.shape[1])))
    small = jnp.concatenate([small[:, i * strip : (i + 1) * strip] for i in range(4)])
    up_low = up_weight.astype(bf16)
    down_low = down_weight.astype(bf16)
    pieces = gather_mp(jnp.concatenate([up_low[:, : 3 * head_cols], small], axis=1))
    place = jnp.arange(16 * sub)
    source = (
        (((place // sub) % 4) ^ mp_index) * 4 * sub + place // (4 * sub) * sub + place % sub
    )
    small = product(
        one_hot_rows(source, 16 * sub), jnp.concatenate([p[:, 3 * head_cols :] for p in pieces])
    ).astype(bf16)
    small = jnp.concatenate(
        [small[i * 4 * sub : (i + 1) * 4 * sub] for i in range(4)], axis=1
    )
    small_mine = small[:, : edge + 128]
    taps_pos = small[:, edge + 128 : edge + 128 + 39 * head_cols // sub]
    taps_pos = jnp.sum(taps_pos.reshape(4, 3, 13, head_cols).astype(f32), axis=1)
    taps_pos = jnp.where(upper == 2, jnp.roll(taps_pos, 2, axis=0), taps_pos)
    conv_all = taps_pos[:, :12].transpose(1, 0, 2).reshape(2, 6, width)
    rel_bias = taps_pos[:, 12, : position_bias.size].reshape(heads, 3)
    weights = jnp.concatenate(
        [p[:, j * head_cols : (j + 1) * head_cols] for j in range(3) for p in pick(pieces)]
        + [small_mine],
        axis=1,
    )
    weights = spread_core(spread_dp(weights))
    patches_t = regroup(after(patches.transpose(0, 2, 1), *pieces))
    pieces = gather_mp(
        after(
            jnp.concatenate(
                [down_low[:, head_cols:], up_low[:, 3 * head_cols :], down_low[:, :head_cols]],
                axis=1,
            ),
            patches_t,
        )
    )

    place = jnp.arange(rows)
    token = 8 * (place % eighth) + 4 * ((place // eighth) % 2) + place // (2 * eighth)
    token_order = one_hot_rows(token, rows)
    mem_rows = memory.shape[2]
    half_mem = mem_rows // 2
    mem_place = jnp.arange(mem_rows)
    mem_order = one_hot_rows(2 * (mem_place % half_mem) + mem_place // half_mem, mem_rows)
    part_quarter = [2 * (core ^ (s % 2)) + (across ^ (s // 2)) for s in range(4)]
    pool_place = jnp.arange(pooled)
    pool_token = 2 * (pool_place % half_pool) + pool_place // half_pool
    now_index = jnp.concatenate([pq * pooled + pool_token for pq in part_quarter])
    pool_index = jnp.concatenate([pq * half_pool + jnp.arange(half_pool) for pq in part_quarter])
    mem_index = jnp.arange(half_mem)

    def key_bias(m):
        sides = [
            (now_index, lengths_all[2 + m] // 4),
            (mem_index if m == 0 else pool_index, lengths_all[1 + m] // 8),
            (mem_index if m < 2 else pool_index, lengths_all[m] // 8),
        ]
        return jnp.concatenate(
            [
                jnp.where((index < limit)[None, :], rel_bias[:, g : g + 1], -3e38)
                for g, (index, limit) in enumerate(sides)
            ],
            axis=1,
        ).reshape(heads // QUAD, QUAD, -1)

    biases = [key_bias(m) for m in range(MICRO)]

    (
        patches_in,
        embedded,
        normed,
        query,
        raw_keys,
        raw_values,
        pools,
        vectors,
        head_low,
    ) = embed(patches_t, token_order, conv_all, weights, classes)
    two = swap_mp(pools, 1)
    rest = join(2 * hidden_cols, across[None], [after(p, pools) for p in pieces])
    rest = [rest, swap_dp(rest, 2), swap_dp(rest, 4)]
    rest_late = after(rest[0], *rest[1:])
    rest_late = [swap_dp(rest_late, b) for b in range(6, dp_count, 2)]
    gathered = (pools, swap_dp(pools, 1), two, swap_dp(after(two, *biases), 1))
    stored = [[(a, m) for a in gathered] for m in range(MICRO)]
    memory_t = regroup(after(memory.transpose(0, 1, 3, 2), rest[0]))
    mem_two = swap_mp(after(memory_t, two), 1)
    stored = [None, None] + stored

    attended, saved = None, {}
    for m in (2, 1, 0):
        arrived = {2: rest[1:], 1: [], 0: rest_late}[m]
        attended, probs, keys, values = attend(
            m,
            after(query, *arrived) if arrived else query,
            conv_all,
            biases[m],
            stored[m + 2],
            stored[m + 1],
            stored[m],
            attended,
        )
        saved[m] = (keys, values, probs)
        if m == 2:
            rest_core = [swap_dp(after(p, attended), 1) for p in rest]
        if m == 1:
            late_core = [swap_dp(after(p, attended), 1) for p in rest_late]
        if m > 1:
            mem_two = after(mem_two, attended)
            mem_parts = (
                memory_t,
                swap_dp(after(memory_t, attended), 1),
                mem_two,
                swap_dp(mem_two, 1),
            )
            mem_full = memory_in(
                jnp.stack(
                    [
                        (((c ^ upper) // 2) ^ core) + 2 * (((c ^ upper) % 2) ^ across)
                        for c in range(4)
                    ]
                ),
                mem_order,
                mem_parts,
            )
            stored[:2] = [[(mem_full, 0)], [(mem_full, 1)]]
    rest = one_or_all(rest + rest_late + rest_core + late_core)

    position = quarter * rows + token
    within = position % FRAME
    live = position[None, :] < lengths_all[2:, None]
    inside = (
        (within[None, None, :] >= bounds[:, :, 0:1])
        & (within[None, None, :] < bounds[:, :, 1:2])
        & live[:, None, :]
    )
    denominator = ((bounds[:, :, 1] - bounds[:, :, 0]) * (lengths_all[2:, None] // FRAME)).astype(
        f32
    )
    select = inside.astype(f32) / denominator[:, :, None]
    first_res, normed_mlp, active, slope, second_res, feature = mlp(
        attended, embedded, vectors, select, rest
    )
    target_row = jnp.arange(4 * pooled)
    target_quarter, target_rest = target_row // pooled, target_row % pooled
    source_row = (
        (((target_quarter // 2) ^ core) + 2 * ((target_quarter % 2) ^ across)) * pooled
        + (target_rest % 2) * half_pool
        + target_rest // 2
    )
    new_memory = memory_out(
        (quarter ^ upper)[None],
        one_hot_rows(source_row, 4 * pooled).T,
        stored[3] + stored[4],
        events=(feature,),
    )
    feature = feature.reshape(MICRO * boxes, width)
    feature = group_sum_features(feature).astype(bf16)
    logits = contract_last(feature, head_low)
    target = labels.astype(f32)
    keep = (jnp.arange(boxes)[None, :] < counts[:, None]).astype(f32).reshape(-1, 1)
    lead = (quarter == 0).astype(f32)
    loss_part = jnp.sum((jax.nn.softplus(logits) - target * logits) * keep) * lead
    grad_logits = ((jax.nn.sigmoid(logits) - target) * keep).astype(bf16)

    grad_head = contract_rows(grad_logits, feature) * lead
    grad_feature = product(grad_logits, head_low).reshape(MICRO, boxes, width)
    grad_branch, grad_hidden, grad_attn, grad_first, grad_attended, sums = mlp_back(
        grad_feature, select, second_res, first_res, slope, vectors, rest, (new_memory,)
    )
    new_memory = regroup(new_memory)
    grad_branch = after(grad_branch, new_memory)

    half = width // 2

    def weight_grad(left, right, at):
        return contract_rows(left[:, at : at + half], right).astype(bf16)

    sides = ((grad_branch, active), (normed_mlp, grad_hidden), (grad_attn, attended))
    rest_far = [weight_grad(*side, half) for side in sides]
    rest_near = [weight_grad(*side, 0) for side in sides]
    rest_pieces = halve_dp(rest_near, rest_far)

    dq, pool_grads, bias_grad, mem_taps = None, [], 0.0, 0.0
    events = tuple(rest_pieces)
    rest_found = trade_dp(rest_pieces, 1, 3)
    for m in range(MICRO):
        keys, values, probs = saved[m]
        dq, kept, sent, taps_part, bias_part = attend_back(
            m,
            query,
            keys,
            values,
            probs,
            after(grad_attended, *events),
            stored[m + 1],
            stored[m],
            dq,
        )
        got = swap_dp(sent, 1)
        away = (kept[1].astype(f32) + got[1].astype(f32)).astype(bf16)
        pool_grads.extend([kept, got, swap_mp(away, 1)])
        bias_grad = bias_grad + bias_part
        mem_taps = mem_taps + taps_part
        events = (away,)
        if m == 1:
            events = (away, pool_grads[2]) + tuple(rest_found)
            rest_pieces[3:] = [after(p, *rest_found) for p in rest_pieces[3:]]
            rest_found += trade_dp(rest_pieces, 3, None)
    rest_total = sum((f.astype(f32) for f in rest_found), rest_pieces[0].astype(f32))
    units = 4 * hidden_cols
    rest_pieces = []
    out_blocks = pick(
        [
            rest_total[:, 2 * units + c * head_cols : 2 * units + (c + 1) * head_cols]
            for c in range(4)
        ]
    )
    for s in range(4):
        piece = jnp.concatenate(
            [
                rest_total[:, units + s * hidden_cols : units + (s + 1) * hidden_cols],
                out_blocks[s],
                rest_total[:, s * hidden_cols : (s + 1) * hidden_cols],
            ],
            axis=1,
        )
        rest_pieces.append(piece)
    rest_near, rest_far, rest_got = halve_mp(rest_pieces)
    attn_near, attn_far, taps_grad = embed_back(
        after(dq, rest_near, *rest_far),
        raw_keys,
        raw_values,
        conv_all,
        embedded,
        grad_first,
        normed,
        patches_in,
        vectors,
        grad_head,
        sums,
        tuple(pool_grads),
        weights,
        events=(),
    )
    attn_pieces = halve_dp([attn_near], [attn_far])
    attn_found = trade_dp(attn_pieces, 1, None)
    rest_got = after(rest_got, *attn_pieces)
    columns = rest_near.shape[1]
    far = (rest_far[0].astype(f32) + rest_got[:, columns:].astype(f32)).astype(bf16)
    rest_mine = (rest_near + rest_got[:, :columns].astype(f32), swap_mp(far, 2))
    attn_found[-1] = after(attn_found[-1], far)
    attn_total = sum((f.astype(f32) for f in attn_found), attn_pieces[0].astype(f32))
    small_total = attn_total[:, 3 * width :]
    small_parts = halve_more(*halve_mp(
        [
            lax.dynamic_slice_in_dim(small_total, (mp_index ^ s) * sub, sub, axis=0)
            for s in range(4)
        ]
    ))
    attn_parts = halve_more(*halve_mp(
        pick(
            [
                jnp.concatenate(
                    [
                        attn_total[:, (4 * j + c) * head_cols : (4 * j + c + 1) * head_cols]
                        for j in range(3)
                    ],
                    axis=1,
                )
                for c in range(4)
            ]
        )
    ))

    count_local = jnp.sum(box_count).astype(f32) * (mp_index == 0).astype(f32)
    taps_rows = jnp.stack(
        [
            jnp.concatenate([taps_grad[4 * ch : 4 * ch + 4], mem_taps[ch]], axis=0)
            for ch in range(2)
        ],
        axis=1,
    ).reshape(12, 4, head_cols)
    scalars = jnp.stack([loss_part, count_local])
    last = jnp.concatenate(
        [
            bias_grad.reshape(heads, 128)[:, :3].reshape(4, -1),
            jnp.broadcast_to(scalars[None], (4, 2)),
        ],
        axis=1,
    )
    last = jnp.pad(last, ((0, 0), (0, head_cols - last.shape[1])))
    flat = jnp.concatenate([taps_rows, last[None]]).transpose(1, 0, 2)
    attn_mine, small_mine, rest_mine, both = squares_of(
        attn_parts, small_parts, rest_mine, flat.reshape(52, head_cols), (new_memory,)
    )
    both = both + swap_dp(both, 1)
    both = both + sum(swap_dp(both, b) for b in range(2, dp_count, 2))
    parts = (both,) + tuple(swap_mp(both, mask) for mask in (1, 2, 3))

    def turned(arrays):
        up, down, embed_part, head, vector, conv, position = arrays
        return (up, down, embed_part.T, head.T, vector, conv.transpose(1, 0, 2), position)

    masters = (
        up_weight,
        down_weight,
        embed_weight,
        head_weight,
        vector_weight,
        conv_weight,
        position_bias,
    )
    moments = (
        up_moment,
        down_moment,
        embed_moment,
        head_moment,
        vector_moment,
        conv_moment,
        position_moment,
    )
    averages = (
        up_average,
        down_average,
        embed_average,
        head_average,
        vector_average,
        conv_average,
        position_average,
    )
    rates = (LEARNING,) * 4 + (VECTOR_LEARNING,) * 3
    made = update(
        across[None],
        parts,
        (attn_mine, small_mine, rest_mine),
        patch,
        turned(masters),
        turned(moments),
        turned(averages),
        rates,
    )
    loss_global, box_total, grad_norm = (made[23 + i].reshape(()) for i in range(3))
    results = []
    for i in range(3):
        results.extend(turned(made[7 * i : 7 * i + 7]))

    return (
        (loss_global, box_total, grad_norm, new_memory.transpose(0, 1, 3, 2)) + tuple(results) + tuple(made[21:23])
    )


def solution(mesh):
    both = ("dp", "mp")
    weight_specs = (
        P("dp", "mp"),
        P("dp", "mp"),
        P(None, both),
        P(None, both),
        P(None, both),
        P(None, None, "mp"),
        P("mp", None),
    )
    memory_spec = P(None, None, "dp", "mp")
    return jax.shard_map(
        shards,
        mesh=mesh,
        in_specs=(
            P(None, both, None),
            P("dp", None),
            P("dp", None),
            P("dp", None, None, None),
            P("dp", None, None, None),
            memory_spec,
        )
        + weight_specs * 3,
        out_specs=(P(), P(), P(), memory_spec)
        + weight_specs * 3
        + (P("dp", "mp"), P("dp", "mp")),
        check_vma=False,
    )
```
